32 devices in a mesh: dp: 8 (over y, x, core), mp: 4 (over z).
Axes of the slice: x: 2, y: 2, z: 4, core: 2. Of those that a mesh axis runs over, the one named last changes fastest.
Arguments:
- patches: bfloat16 [2048, 6144], P('dp', 'mp'), may hold values from -6 to 6
- dest_group: int32 [2048], P('dp'), may hold values from 0 to 7, as said below
- dest_row: int32 [2048], P('dp'), may hold values from 0 to 255, as said below
- segment: int32 [2048], P('dp'), may hold values from 0 to 15, as said below
- ln_gain: float32 [6144], replicated, may hold values from 0.1 to 1.9
- w_qkv: bfloat16 [6144, 3, 3072], P(None, None, 'mp'), may hold values from -0.078125 to 0.078125
- qk_gain: float32 [2, 128], replicated, may hold values from 0.1 to 1.9
- w_out: bfloat16 [6144, 3072], P(None, 'mp'), may hold values from -0.4375 to 0.4375
- cotangent: bfloat16 [2048, 6144], P('dp', 'mp'), may hold values from -6 to 6
Outputs:
- output: bfloat16 [2048, 6144], P('dp', 'mp')
- input_grad: bfloat16 [2048, 6144], P('dp', 'mp')
- qkv_grad: bfloat16 [6144, 3, 3072], P('dp', None, 'mp')
- out_grad: bfloat16 [6144, 3072], P('dp', 'mp')
The draws below stay inside these ranges and needn't reach their ends.
Inputs may be any that keep to these rules, and one draw needn't show every extreme that they name: The pairs (dest_group, dest_row) of all rows name every row of every group exactly once. The rows of one group send at most 64 rows to any one group, and in every draw some group sends exactly 64 rows to some group. `dest_row`: see dest_group. `segment`: rows of one group with equal numbers are one image and stand in consecutive rows; numbers lie between 0 and 15.
All inputs are finite; a program needn't handle non-finite values.
Results may differ from the reference program's by a relative error of at most 0.024.
Values may be sent and summed in bfloat16 or wider, within the bound.
No kernel may reach another device: no remote copies, remote signals or barrier semaphores. Data moves between devices by JAX's collectives and lax.ppermute only.
A program may use at most 192 MiB of HBM per device.

```python
import math
import jax
import jax.numpy as jnp
from jax import lax

D = 6144
DH = 128
ROWS = 256
HD = 3072
SLOT = 64
TOKENS = 2048
N_DP = 8
N_MP = 4


def route_plan(key):
    half_slot = SLOT // 2
    pair_count = (N_DP - 2) // 2
    key_delta = jax.random.fold_in(key, 11)
    key_order = jax.random.fold_in(key, 12)
    key_split = jax.random.fold_in(key, 13)
    delta = jax.random.randint(key_delta, (pair_count,), 0, half_slot + 1).astype(jnp.int32)
    base_counts = jnp.concatenate([jnp.array([SLOT, 0], jnp.int32), half_slot + delta, half_slot - delta]).astype(jnp.int32)
    order = jax.random.permutation(key_order, N_DP)
    counts = base_counts[order]
    source_ids = jnp.arange(N_DP, dtype=jnp.int32)[:, None]
    target_ids = jnp.arange(N_DP, dtype=jnp.int32)[None, :]
    load = counts[(target_ids - source_ids) % N_DP]
    src_start = jnp.cumsum(load, 1) - load
    dst_start = jnp.cumsum(load, 0) - load
    src_end = src_start + load
    dst_end = dst_start + load
    position = jnp.arange(ROWS, dtype=jnp.int32)
    target = jnp.sum((src_end[:, None, :] <= position[None, :, None]).astype(jnp.int32), 2)
    offset = position[None, :] - jnp.take_along_axis(src_start, target, 1)
    row_there = jnp.take_along_axis(dst_start, target, 1) + offset
    source = jnp.sum((dst_end.T[:, None, :] <= position[None, :, None]).astype(jnp.int32), 2)
    cut = jax.random.randint(key_split, (N_DP, N_DP), 0, load + 1).astype(jnp.int32)
    inside = position[None, :] - jnp.take_along_axis(dst_start.T, source, 1)
    cut_here = jnp.take_along_axis(cut.T, source, 1)
    image_ids = 2 * source + (inside >= cut_here).astype(jnp.int32)
    return (target.reshape(-1).astype(jnp.int32), row_there.reshape(-1).astype(jnp.int32), image_ids.reshape(-1).astype(jnp.int32))


def draw_dest_group(key, part):
    return route_plan(key)[0]


def draw_dest_row(key, part):
    return route_plan(key)[1]


def draw_segment(key, part):
    return route_plan(key)[2]


def strengthened(entries, rng, source, target, parts, factor):
    owner, partner = [(jnp.arange(entries.shape[dim]) // (entries.shape[dim] // parts)).reshape([-1 if axis == dim else 1 for axis in range(entries.ndim)]) for dim in (source, target)]
    chosen = jax.random.permutation(rng, parts)[partner]
    strong = (owner == chosen) | (owner == (partner + parts // 2) % parts)
    return jnp.where(strong, factor * entries, entries)


def block_scale(own_key, extent, cuts, low, largest):
    loudness = 1.0
    for axis_at, blocks in cuts:
        steps = jax.random.uniform(jax.random.fold_in(jax.random.fold_in(own_key, 6), axis_at), (blocks,), jnp.float32, low / len(cuts), largest / len(cuts))
        loudness = loudness * jnp.repeat(jnp.exp(steps), extent[axis_at] // blocks).reshape((-1,) + (1,) * (len(extent) - 1 - axis_at))
    return loudness


def noise(key, shape, scale, reach, shards=(), kind=jnp.bfloat16):
    result = jax.random.normal(key, shape, jnp.float32) * scale
    if len(shards) > 0:
        result = block_scale(key, shape, shards, -0.22, 0.18) * result
    return jnp.clip(result, min=-reach, max=reach).astype(kind)


def noise_with(stream_key, extent, scale, reach, split, heavy, held_as=jnp.bfloat16):
    result = scale * jax.random.normal(stream_key, extent, jnp.float32)
    if split:
        result = result * block_scale(stream_key, extent, split, -0.22, 0.18)
    return jnp.clip(strengthened(result, jax.random.fold_in(stream_key, 3), *heavy), -reach, reach).astype(held_as)


def setup_inputs(seed: int = 0) -> dict:
    key_list = jax.random.split(jax.random.key(seed), 10)
    patches = noise(key_list[0], (TOKENS, D), 1.0, 6.0, ((0, 8), (1, 4)))
    dest_group = draw_dest_group(jax.random.fold_in(key_list[9], 71), 0)
    dest_row = draw_dest_row(jax.random.fold_in(key_list[9], 71), 0)
    segment = draw_segment(jax.random.fold_in(key_list[9], 71), 0)
    ln_gain = jnp.clip(1.0 + 0.18 * jax.random.normal(key_list[4], (D,), jnp.float32), 0.1, 1.9)
    w_qkv = noise(key_list[5], (D, 3, HD), D ** -0.5, 0.078125, ((2, 4),))
    qk_gain = jnp.clip(1.0 + 0.18 * jax.random.normal(key_list[6], (2, DH), jnp.float32), 0.1, 1.9)
    w_out = noise(key_list[7], (D, HD), (HD // 16) ** -0.5, 0.4375, ((1, 4),))
    cotangent = noise_with(key_list[8], (TOKENS, D), 1.0, 6.0, ((0, 8), (1, 4)), (0, 1, 8, 2.0))
    return dict(patches=patches, dest_group=dest_group, dest_row=dest_row, segment=segment, ln_gain=ln_gain, w_qkv=w_qkv, qk_gain=qk_gain, w_out=w_out, cotangent=cotangent)


def norm_heads(values, gain):
    center = values - lax.optimization_barrier(jnp.mean(values, -1, keepdims=True))
    variance = lax.optimization_barrier(jnp.mean(center * center, -1, keepdims=True))
    return center * lax.rsqrt(variance + 1e-06) * gain

def attend(projected, image_ids, qk_gain):
    row_count = projected.shape[0]
    head_count = projected.shape[2] // DH
    split_heads = projected.reshape(row_count, 3, head_count, DH)
    queries = norm_heads(split_heads[:, 0], qk_gain[0]).astype(jnp.bfloat16)
    keys_normed = norm_heads(split_heads[:, 1], qk_gain[1]).astype(jnp.bfloat16)
    values_bf = split_heads[:, 2].astype(jnp.bfloat16)
    scores = jnp.einsum('qhd,khd->hqk', queries, keys_normed, preferred_element_type=jnp.float32) * DH ** (-0.5)
    same_image = image_ids[:, None] == image_ids[None, :]
    raised = jnp.where(same_image[None], jnp.exp(scores), 0.0)
    weights = (raised / lax.optimization_barrier(jnp.sum(raised, -1, keepdims=True))).astype(jnp.bfloat16)
    mixed = jnp.einsum('hqk,khd->qhd', weights, values_bf, preferred_element_type=jnp.float32)
    return mixed.reshape(row_count, head_count * DH).astype(jnp.bfloat16)

def reference(patches, dest_group, dest_row, segment, ln_gain, w_qkv, qk_gain, w_out, cotangent):
    token_total = patches.shape[0]
    group_rows = token_total // N_DP
    local_width = HD // N_MP
    target = (dest_group * group_rows + dest_row).astype(jnp.int32)
    packed = jnp.zeros_like(patches).at[target].set(patches)
    qkv_flat = w_qkv.reshape(D, 3 * HD)
    qkv_wide = w_qkv.reshape(D, 3, N_MP, local_width).astype(jnp.float32)
    out_wide = w_out.reshape(D, N_MP, local_width).astype(jnp.float32)
    scale_grad = 1.0 / math.sqrt(token_total)

    def one_group(carry, group_inputs):
        sum_qkv, sum_out = carry
        block, image_ids, cot_block = group_inputs
        wide = block.astype(jnp.float32)
        center = wide - lax.optimization_barrier(jnp.mean(wide, -1, keepdims=True))
        rstd = lax.rsqrt(lax.optimization_barrier(jnp.mean(center * center, -1, keepdims=True)) + 1e-06)
        unit_rows = center * rstd
        normed = (unit_rows * ln_gain).astype(jnp.bfloat16)
        projected = jnp.dot(normed, qkv_flat, preferred_element_type=jnp.float32).reshape(group_rows, 3, HD)
        heads_out, backward = jax.vjp(lambda values: attend(values, image_ids, qk_gain), projected)
        pieces = jnp.einsum('rmk,dmk->mrd', heads_out.reshape(group_rows, N_MP, local_width).astype(jnp.float32), out_wide)
        attn = lax.optimization_barrier(jnp.sum(lax.optimization_barrier(pieces.astype(jnp.bfloat16)).astype(jnp.float32), 0))
        output = (wide + attn).astype(jnp.bfloat16)
        d_heads = jnp.dot(cot_block, w_out, preferred_element_type=jnp.float32).astype(jnp.bfloat16)
        d_projected, = backward(d_heads)
        d_proj_bf = d_projected.astype(jnp.bfloat16)
        d_pieces = jnp.einsum('rtmk,dtmk->mrd', d_proj_bf.reshape(group_rows, 3, N_MP, local_width).astype(jnp.float32), qkv_wide)
        d_normed = lax.optimization_barrier(jnp.sum(lax.optimization_barrier(d_pieces.astype(jnp.bfloat16)).astype(jnp.float32), 0))
        d_unit = d_normed * ln_gain
        d_input = rstd * (d_unit - lax.optimization_barrier(jnp.mean(d_unit, -1, keepdims=True)) - unit_rows * lax.optimization_barrier(jnp.mean(d_unit * unit_rows, -1, keepdims=True)))
        input_grad = (cot_block.astype(jnp.float32) + d_input).astype(jnp.bfloat16)
        term_qkv = lax.dot_general(normed, d_proj_bf.reshape(group_rows, 3 * HD), (((0,), (0,)), ((), ())), preferred_element_type=jnp.float32)
        term_out = lax.dot_general(cot_block, heads_out, (((0,), (0,)), ((), ())), preferred_element_type=jnp.float32)
        sum_qkv = sum_qkv + lax.optimization_barrier(term_qkv.astype(jnp.bfloat16)).astype(jnp.float32)
        sum_out = sum_out + lax.optimization_barrier(term_out.astype(jnp.bfloat16)).astype(jnp.float32)
        return ((sum_qkv, sum_out), (output, input_grad))
    start_sums = (jnp.zeros((D, 3 * HD), jnp.float32), jnp.zeros((D, HD), jnp.float32))
    stacked = (packed.reshape(N_DP, group_rows, D), segment.reshape(N_DP, group_rows), cotangent.reshape(N_DP, group_rows, D))
    (sum_qkv, sum_out), (outputs, grads) = lax.scan(one_group, start_sums, stacked)
    qkv_grad = (sum_qkv * scale_grad).reshape(D, 3, HD).astype(jnp.bfloat16)
    out_grad = (sum_out * scale_grad).astype(jnp.bfloat16)
    return (outputs.reshape(token_total, D), grads.reshape(token_total, D), qkv_grad, out_grad)
```

```python
import math

import jax
import jax.numpy as jnp
from jax import lax
from jax.sharding import PartitionSpec as P

DH = 128


def norm_heads(values, gain):
    center = values - jnp.mean(values, -1, keepdims=True)
    variance = jnp.mean(center * center, -1, keepdims=True)
    return center * lax.rsqrt(variance + 1e-06) * gain


def attend(projected, image_ids, qk_gain):
    row_count = projected[0].shape[0]
    head_count = projected[0].shape[1] // DH
    q_raw, k_raw, v_raw = [part.reshape(row_count, head_count, DH) for part in projected]
    queries = norm_heads(q_raw, qk_gain[0]).astype(jnp.bfloat16)
    keys_normed = norm_heads(k_raw, qk_gain[1]).astype(jnp.bfloat16)
    values_bf = v_raw.astype(jnp.bfloat16)
    scores = jnp.einsum(
        "qhd,khd->hqk", queries, keys_normed, preferred_element_type=jnp.float32
    ) * DH ** (-0.5)
    same_image = image_ids[:, None] == image_ids[None, :]
    raised = jnp.where(same_image[None], jnp.exp(scores), 0.0)
    weights = (raised / jnp.sum(raised, -1, keepdims=True)).astype(jnp.bfloat16)
    mixed = jnp.einsum("hqk,khd->qhd", weights, values_bf, preferred_element_type=jnp.float32)
    return mixed.reshape(row_count, head_count * DH).astype(jnp.bfloat16)


def dot_f32(left, right, left_dims, right_dims):
    return lax.dot_general(
        left, right, ((left_dims, right_dims), ((), ())), preferred_element_type=jnp.float32
    )


def exchange_small(values, axis):
    count = lax.axis_size(axis)
    return lax.all_to_all(
        jnp.broadcast_to(values[None], (count,) + values.shape), axis, 0, 0, tiled=True
    )


def flip(values, axis, bit):
    count = lax.axis_size(axis)
    return lax.ppermute(values, axis, [(at, at ^ bit) for at in range(count)])


def gather_xor(values, axis):
    count = lax.axis_size(axis)
    half = values.shape[0] // 2
    high, low = count // 2, count // 4
    one, two = values[:half], values[half:]
    one_h, two_l = flip(one, axis, high), flip(two, axis, low)
    pair_one, pair_two = jnp.stack([one, one_h]), jnp.stack([two, two_l])
    far_one, far_two = flip(pair_one, axis, low), flip(pair_two, axis, high)
    blocks = [
        jnp.concatenate([one, two]),
        jnp.concatenate([far_one[0], two_l]),
        jnp.concatenate([one_h, far_two[0]]),
        jnp.concatenate([far_one[1], far_two[1]]),
    ]
    held = {at * low: block for at, block in enumerate(blocks)}
    bit = low // 2
    while bit >= 1:
        keys = sorted(held)
        other = flip(jnp.stack([held[key] for key in keys]), axis, bit)
        for at, key in enumerate(keys):
            held[key | bit] = other[at]
        bit //= 2
    return jnp.stack([held[key] for key in range(count)])


def columns_xor(values, axis):
    count = lax.axis_size(axis)
    rows, width = values.shape
    cut = values.reshape(rows, count, width // count).transpose(1, 0, 2)
    got = lax.all_to_all(cut, axis, 0, 0, tiled=True)
    return got[lax.axis_index(axis) ^ jnp.arange(count, dtype=jnp.int32)]


def shards(patches, dest_group, dest_row, segment, ln_gain, w_qkv, qk_gain, w_out, cotangent):
    group_rows, part_width = patches.shape
    groups = lax.axis_size("dp")
    parts = lax.axis_size("mp")
    slot_size = 2 * group_rows // groups
    full_width, local_width = w_out.shape
    my_index = lax.axis_index("mp")
    w_t = jnp.transpose(w_qkv, (1, 0, 2))

    whole_cot = lax.all_gather(cotangent, "mp", axis=1, tiled=True)

    position = jnp.arange(group_rows, dtype=jnp.int32)
    earlier = (dest_group[:, None] == dest_group[None, :]) & (position[None, :] < position[:, None])
    rank_within = jnp.sum(earlier.astype(jnp.int32), 1)
    place = dest_group * slot_size + rank_within
    slots = groups * slot_size
    to_slot = jnp.arange(slots, dtype=jnp.int32)[:, None] == place[None, :]
    outbox = dot_f32(to_slot.astype(jnp.bfloat16), patches, (1,), (0,)).astype(jnp.bfloat16)
    inbox = lax.all_to_all(
        outbox.reshape(groups, slot_size, part_width), "dp", split_axis=0, concat_axis=0, tiled=True
    ).reshape(slots, part_width)

    wide = patches.astype(jnp.float32)
    part_mean = jnp.mean(wide, -1)
    part_dev = jnp.sum(jnp.square(wide - part_mean[:, None]), -1)
    seen = exchange_small(jnp.stack([part_mean, part_dev]), "mp")
    row_mean = jnp.mean(seen[:, 0], 0)
    row_dev = jnp.sum(seen[:, 1], 0) + part_width * jnp.sum(
        jnp.square(seen[:, 0] - row_mean[None]), 0
    )
    row_rstd = lax.rsqrt(row_dev / full_width + 1e-06)
    notes = jnp.stack([dest_row.astype(jnp.float32) + 1.0, row_mean, row_rstd])
    outnotes = jnp.sum(jnp.where(to_slot[None], notes[:, None, :], 0.0), -1)
    innotes = lax.all_to_all(
        outnotes.reshape(3, groups, slot_size).transpose(1, 0, 2), "dp", 0, 0, tiled=True
    )
    arrived_at = innotes[:, 0].reshape(slots).astype(jnp.int32) - 1
    from_slot = position[:, None] == arrived_at[None, :]
    packed = dot_f32(from_slot.astype(jnp.bfloat16), inbox, (1,), (0,)).astype(jnp.bfloat16)
    mean = jnp.sum(jnp.where(from_slot, innotes[:, 1].reshape(1, slots), 0.0), -1, keepdims=True)
    rstd = jnp.sum(jnp.where(from_slot, innotes[:, 2].reshape(1, slots), 0.0), -1, keepdims=True)

    my_gain = lax.dynamic_slice_in_dim(ln_gain, my_index * part_width, part_width, 0)
    unit_rows = (packed.astype(jnp.float32) - mean) * rstd
    normed_part = (unit_rows * my_gain).astype(jnp.bfloat16)
    normed = lax.all_gather(normed_part, "mp", axis=1, tiled=True)

    projected = tuple(jnp.dot(normed, w_t[t], preferred_element_type=jnp.float32) for t in range(3))
    heads_out, backward = jax.vjp(lambda values: attend(values, segment, qk_gain), projected)
    attn = lax.psum_scatter(
        dot_f32(heads_out, w_out, (1,), (1,)).astype(jnp.bfloat16),
        "mp",
        scatter_dimension=1,
        tiled=True,
    ).astype(jnp.float32)
    output = (packed.astype(jnp.float32) + attn).astype(jnp.bfloat16)

    d_heads = jnp.dot(whole_cot, w_out, preferred_element_type=jnp.float32).astype(jnp.bfloat16)
    (d_projected,) = backward(d_heads)
    d_proj_bf = jnp.concatenate([part.astype(jnp.bfloat16) for part in d_projected], 1)
    d_part = sum(
        dot_f32(d_proj_bf[:, t * local_width : (t + 1) * local_width], w_t[t], (1,), (1,))
        for t in range(3)
    )
    d_normed = lax.psum_scatter(
        d_part.astype(jnp.bfloat16), "mp", scatter_dimension=1, tiled=True
    ).astype(jnp.float32)
    d_unit = d_normed * my_gain
    sums = jnp.stack([jnp.sum(d_unit, -1), jnp.sum(d_unit * unit_rows, -1)])
    sums = jnp.sum(exchange_small(sums, "mp"), 0) / full_width
    d_input = rstd * (d_unit - sums[0][:, None] - unit_rows * sums[1][:, None])
    input_grad = (cotangent.astype(jnp.float32) + d_input).astype(jnp.bfloat16)

    scale_grad = 1.0 / math.sqrt(group_rows * groups)
    normed_cols = columns_xor(normed, "dp").reshape(groups * group_rows, -1)
    cot_cols = columns_xor(whole_cot, "dp").reshape(groups * group_rows, -1)
    heads_all = gather_xor(heads_out, "dp").reshape(groups * group_rows, -1)
    d_proj_all = gather_xor(d_proj_bf, "dp").reshape(groups * group_rows, -1)
    out_grad = (dot_f32(cot_cols, heads_all, (0,), (0,)) * scale_grad).astype(jnp.bfloat16)
    qkv_grad = jnp.stack(
        [
            (
                dot_f32(
                    normed_cols,
                    d_proj_all[:, t * local_width : (t + 1) * local_width],
                    (0,),
                    (0,),
                )
                * scale_grad
            ).astype(jnp.bfloat16)
            for t in range(3)
        ]
    ).transpose(1, 0, 2)
    return (output, input_grad, qkv_grad, out_grad)


def solution(mesh):
    placed = (
        P("dp", "mp"),
        P("dp"),
        P("dp"),
        P("dp"),
        P(),
        P(None, None, "mp"),
        P(),
        P(None, "mp"),
        P("dp", "mp"),
    )
    return jax.shard_map(
        shards,
        mesh=mesh,
        in_specs=placed,
        out_specs=(P("dp", "mp"), P("dp", "mp"), P("dp", None, "mp"), P("dp", "mp")),
        check_vma=False,
    )
```

```python
import functools
import math

import jax
import jax.numpy as jnp
from jax import lax
from jax.experimental import pallas as pl
from jax.experimental.pallas import tpu as pltpu
from jax.sharding import PartitionSpec as P

DH = 128
VMEM_BYTES = 48 * 1024 * 1024


def dot_f32(left, right, left_dims, right_dims):
    return lax.dot_general(
        left, right, ((left_dims, right_dims), ((), ())), preferred_element_type=jnp.float32
    )


def params():
    return pltpu.CompilerParams(vmem_limit_bytes=VMEM_BYTES)


def project_kernel(steps, width, x_ref, w_ref, out_ref, total):
    at, t = pl.program_id(0), pl.program_id(1)
    columns = pl.ds(pl.multiple_of(t * width, width), width)
    term = jnp.dot(x_ref[0], w_ref[0], preferred_element_type=jnp.float32)

    @pl.when(at == 0)
    def _():
        total[:, columns] = term

    @pl.when(at > 0)
    def _():
        total[:, columns] += term

    @pl.when(at == steps - 1)
    def _():
        out_ref[:, columns] = total[:, columns].astype(out_ref.dtype)


def project(x, w, steps, dtype):
    _, rows, part = x.shape
    kinds, depth, width = w.shape
    return pl.pallas_call(
        functools.partial(project_kernel, steps, width),
        grid=(steps, kinds),
        in_specs=[
            pl.BlockSpec((1, rows, part), lambda at, t: (at, 0, 0)),
            pl.BlockSpec((1, part, width), lambda at, t: (t, at, 0)),
        ],
        out_specs=pl.BlockSpec((rows, kinds * width), lambda at, t: (0, 0)),
        out_shape=jax.ShapeDtypeStruct((rows, kinds * width), dtype),
        scratch_shapes=[pltpu.VMEM((rows, kinds * width), jnp.float32)],
        compiler_params=params(),
        cost_estimate=pl.CostEstimate(
            flops=2 * rows * depth * kinds * width,
            bytes_accessed=2 * kinds * depth * width + 2 * rows * depth,
            transcendentals=0,
        ),
    )(x, w)


def expand_kernel(kinds, width, x_ref, w_ref, out_ref):
    total = None
    for t in range(kinds):
        term = dot_f32(x_ref[:, t * width : (t + 1) * width], w_ref[t], (1,), (1,))
        total = term if total is None else total + term
    out_ref[0] = total.astype(jnp.bfloat16)


def expand(x, w, parts, cuts):
    rows = x.shape[0]
    kinds, depth, width = w.shape
    part = depth // parts
    piece = part // cuts
    return pl.pallas_call(
        functools.partial(expand_kernel, kinds, width),
        grid=(parts, cuts),
        in_specs=[
            pl.BlockSpec((rows, kinds * width), lambda at, cut: (0, 0)),
            pl.BlockSpec((kinds, piece, width), lambda at, cut: (0, at * cuts + cut, 0)),
        ],
        out_specs=pl.BlockSpec((1, rows, piece), lambda at, cut: (at, 0, cut)),
        out_shape=jax.ShapeDtypeStruct((parts, rows, part), jnp.bfloat16),
        compiler_params=params(),
        cost_estimate=pl.CostEstimate(
            flops=2 * rows * depth * kinds * width,
            bytes_accessed=2 * kinds * depth * width + 2 * rows * depth,
            transcendentals=0,
        ),
    )(x, w)


def unit_heads(raw):
    center = raw - jnp.mean(raw, -1, keepdims=True)
    rstd = lax.rsqrt(jnp.mean(center * center, -1, keepdims=True) + 1e-06)
    return center * rstd, rstd


def head_forward(proj_ref, same, gain_ref, heads, head):
    width = heads * DH
    q_unit, q_rstd = unit_heads(proj_ref[:, head * DH : (head + 1) * DH])
    k_unit, k_rstd = unit_heads(proj_ref[:, width + head * DH : width + (head + 1) * DH])
    values = proj_ref[:, 2 * width + head * DH : 2 * width + (head + 1) * DH].astype(jnp.bfloat16)
    queries = (q_unit * gain_ref[0:1, :]).astype(jnp.bfloat16)
    keys = (k_unit * gain_ref[1:2, :]).astype(jnp.bfloat16)
    scores = dot_f32(queries, keys, (1,), (1,)) * DH ** (-0.5)
    raised = jnp.where(same, jnp.exp(scores), 0.0)
    weights = raised / jnp.sum(raised, -1, keepdims=True)
    return q_unit, q_rstd, k_unit, k_rstd, values, queries, keys, weights


def forward_kernel(heads, proj_ref, row_ref, col_ref, gain_ref, out_ref):
    same = row_ref[...] == col_ref[...]
    for head in range(heads):
        values, _, _, weights = head_forward(proj_ref, same, gain_ref, heads, head)[4:]
        mixed = dot_f32(weights.astype(jnp.bfloat16), values, (1,), (0,))
        out_ref[:, head * DH : (head + 1) * DH] = mixed.astype(jnp.bfloat16)


def unit_backward(grad, unit, rstd, gain):
    scaled = grad.astype(jnp.bfloat16).astype(jnp.float32) * gain
    return rstd * (
        scaled
        - jnp.mean(scaled, -1, keepdims=True)
        - unit * jnp.mean(scaled * unit, -1, keepdims=True)
    )


def backward_kernel(heads, proj_ref, row_ref, col_ref, gain_ref, d_ref, out_ref):
    same = row_ref[...] == col_ref[...]
    width = heads * DH
    for head in range(heads):
        q_unit, q_rstd, k_unit, k_rstd, values, queries, keys, weights = head_forward(
            proj_ref, same, gain_ref, heads, head
        )
        at = head * DH
        weights_bf = weights.astype(jnp.bfloat16)
        d_out = d_ref[:, at : at + DH]
        mixed = dot_f32(weights_bf, values, (1,), (0,))
        out_ref[:, 3 * width + at : 3 * width + at + DH] = mixed.astype(jnp.bfloat16)
        d_values = dot_f32(weights_bf, d_out, (0,), (0,))
        out_ref[:, 2 * width + at : 2 * width + at + DH] = d_values.astype(jnp.bfloat16)
        d_weights = dot_f32(d_out, values, (1,), (1,)).astype(jnp.bfloat16).astype(jnp.float32)
        inner = jnp.sum(d_weights * weights, -1, keepdims=True)
        d_scores = (weights * (d_weights - inner) * DH ** (-0.5)).astype(jnp.bfloat16)
        d_queries = unit_backward(
            dot_f32(d_scores, keys, (1,), (0,)), q_unit, q_rstd, gain_ref[0:1, :]
        )
        d_keys = unit_backward(
            dot_f32(d_scores, queries, (0,), (0,)), k_unit, k_rstd, gain_ref[1:2, :]
        )
        out_ref[:, at : at + DH] = d_queries.astype(jnp.bfloat16)
        out_ref[:, width + at : width + at + DH] = d_keys.astype(jnp.bfloat16)


def attention(kernel, projected, segment, qk_gain, extra, kinds):
    rows, wide = projected.shape
    heads = wide // (3 * DH)
    return pl.pallas_call(
        functools.partial(kernel, heads),
        out_shape=jax.ShapeDtypeStruct((rows, kinds * heads * DH), jnp.bfloat16),
        compiler_params=params(),
        cost_estimate=pl.CostEstimate(
            flops=heads * rows * rows * DH * 16,
            bytes_accessed=rows * wide * 8,
            transcendentals=heads * rows * rows,
        ),
    )(projected, segment.reshape(rows, 1), segment.reshape(1, rows), qk_gain, *extra)


def weight_kernel(count, scale, normed_ref, cot_ref, *refs):
    b_refs, (qkv_ref, out_ref, total) = refs[:count], refs[count:]
    me, t = lax.axis_index("dp"), pl.program_id(0)

    def product(a_ref):
        for k in range(count):
            term = jnp.dot(a_ref[me ^ k], b_refs[k][...], preferred_element_type=jnp.float32)
            total[...] = term if k == 0 else total[...] + term
        return (total[...] * scale).astype(jnp.bfloat16)

    @pl.when(t < 3)
    def _():
        qkv_ref[0] = product(normed_ref)

    @pl.when(t == 3)
    def _():
        out_ref[...] = product(cot_ref)


def weight_grads(normed_cols, cot_cols, gathered, scale):
    count, depth, rows = normed_cols.shape
    width = gathered[0].shape[1] // 4
    whole = pl.BlockSpec((count, depth, rows), lambda t: (0, 0, 0))
    return pl.pallas_call(
        functools.partial(weight_kernel, count, scale),
        grid=(4,),
        in_specs=[whole, whole] + [pl.BlockSpec((rows, width), lambda t: (0, t))] * count,
        out_specs=[
            pl.BlockSpec((1, depth, width), lambda t: (jnp.minimum(t, 2), 0, 0)),
            pl.BlockSpec((depth, width), lambda t: (0, 0)),
        ],
        out_shape=[
            jax.ShapeDtypeStruct((3, depth, width), jnp.bfloat16),
            jax.ShapeDtypeStruct((depth, width), jnp.bfloat16),
        ],
        scratch_shapes=[pltpu.VMEM((depth, width), jnp.float32)],
        compiler_params=params(),
        cost_estimate=pl.CostEstimate(
            flops=8 * count * depth * rows * width,
            bytes_accessed=4 * count * depth * rows + 8 * count * rows * width,
            transcendentals=0,
        ),
    )(normed_cols, cot_cols, *gathered)


def flip(values, axis, bit):
    count = lax.axis_size(axis)
    return lax.ppermute(values, axis, [(at, at ^ bit) for at in range(count)])


def exchange_small(values, axis):
    return [values] + [flip(values, axis, bit) for bit in range(1, lax.axis_size(axis))]


def gather_xor(values, axis):
    count = lax.axis_size(axis)
    high, low = count // 2, count // 4
    over_high, over_low = flip(values, axis, high), flip(values, axis, low)
    even = lax.axis_index(axis) % 2 == 0
    onward = jnp.where(even, over_low, over_high)
    pairs = [(at, at ^ (high if at % 2 == 0 else low)) for at in range(count)]
    held = {0: values, low: over_low, high: over_high, high | low: lax.ppermute(onward, axis, pairs)}
    bit = low // 2
    while bit >= 1:
        for key in sorted(held):
            held[key | bit] = flip(held[key], axis, bit)
        bit //= 2
    return [held[key] for key in range(count)]


def line_gather(values, axis):
    count, me = lax.axis_size(axis), lax.axis_index(axis)
    zeros = (0,) * values.ndim
    held = jnp.zeros((count + 1,) + values.shape, values.dtype)
    held = lax.dynamic_update_slice(held, values[None], (me,) + zeros)
    right = left = values
    for step in range(1, count):
        right = lax.ppermute(right, axis, [(at, at + 1) for at in range(step - 1, count - 1)])
        left = lax.ppermute(left, axis, [(at, at - 1) for at in range(1, count - step + 1)])
        from_left = jnp.where(me >= step, me - step, count)
        from_right = jnp.where(me + step < count, me + step, count)
        held = lax.dynamic_update_slice(held, right[None], (from_left,) + zeros)
        held = lax.dynamic_update_slice(held, left[None], (from_right,) + zeros)
    return held


def add_bf(one, two):
    return (one.astype(jnp.float32) + two.astype(jnp.float32)).astype(jnp.bfloat16)


def line_reduce(parts, axis):
    count, me = lax.axis_size(axis), lax.axis_index(axis)

    def block(at):
        return lax.dynamic_index_in_dim(parts, jnp.clip(at, 0, count - 1), 0, keepdims=False)

    right = left = None
    for step in range(1, count):
        to_right, to_left = block(me + count - step), block(me - count + step)
        if step > 1:
            to_right, to_left = add_bf(to_right, right), add_bf(to_left, left)
        right = lax.ppermute(to_right, axis, [(at, at + 1) for at in range(step)])
        left = lax.ppermute(to_left, axis, [(at, at - 1) for at in range(count - step, count)])
    return block(me).astype(jnp.float32) + right.astype(jnp.float32) + left.astype(jnp.float32)


def columns_to_owner(whole, axis):
    count = lax.axis_size(axis)
    parts, rows, part = whole.shape
    cut = jnp.swapaxes(whole, 1, 2).reshape(count, parts * part // count, rows)
    return lax.all_to_all(cut, axis, 0, 0, tiled=True)


def shards(patches, dest_group, dest_row, segment, ln_gain, w_qkv, qk_gain, w_out, cotangent):
    group_rows, part_width = patches.shape
    groups = lax.axis_size("dp")
    parts = lax.axis_size("mp")
    slot_size = 2 * group_rows // groups
    slots = groups * slot_size
    full_width, local_width = w_out.shape
    my_group, my_index = lax.axis_index("dp"), lax.axis_index("mp")
    w_t = jnp.transpose(w_qkv, (1, 0, 2))
    w_out_t = w_out[None]

    whole_cot = lax.all_gather(cotangent, "mp", axis=0, tiled=False)

    position = jnp.arange(group_rows, dtype=jnp.int32)
    earlier = (dest_group[:, None] == dest_group[None, :]) & (position[None, :] < position[:, None])
    rank_within = jnp.sum(earlier.astype(jnp.int32), 1)
    place = dest_group * slot_size + rank_within
    to_slot = jnp.arange(slots, dtype=jnp.int32)[:, None] == place[None, :]
    outbox = dot_f32(to_slot.astype(jnp.bfloat16), patches, (1,), (0,)).astype(jnp.bfloat16)
    inbox = lax.all_to_all(
        outbox.reshape(groups, slot_size, part_width), "dp", split_axis=0, concat_axis=0, tiled=True
    ).reshape(slots, part_width)

    wide = patches.astype(jnp.float32)
    part_mean = jnp.mean(wide, -1)
    part_dev = jnp.sum(jnp.square(wide - part_mean[:, None]), -1)
    seen = exchange_small(jnp.stack([part_mean, part_dev]), "mp")
    row_mean = sum(entry[0] for entry in seen) / parts
    row_dev = sum(entry[1] + part_width * jnp.square(entry[0] - row_mean) for entry in seen)
    row_rstd = lax.rsqrt(row_dev / full_width + 1e-06)
    notes = jnp.stack([dest_row.astype(jnp.float32) + 1.0, row_mean, row_rstd])
    outnotes = jnp.sum(jnp.where(to_slot[None], notes[:, None, :], 0.0), -1)
    outnotes = outnotes.reshape(3, groups, slot_size)
    came = []
    for bit in range(groups):
        mine = lax.dynamic_index_in_dim(outnotes, my_group ^ bit, 1, keepdims=False)
        came.append(mine if bit == 0 else flip(mine, "dp", bit))
    sender = jnp.arange(groups, dtype=jnp.int32)[None, :, None]
    innotes = sum(
        jnp.where(sender == (my_group ^ bit), entry[:, None, :], 0.0)
        for bit, entry in enumerate(came)
    ).reshape(3, slots)
    arrived_at = innotes[0].astype(jnp.int32) - 1
    from_slot = position[:, None] == arrived_at[None, :]
    mean = jnp.sum(jnp.where(from_slot, innotes[1][None, :], 0.0), -1, keepdims=True)
    rstd = jnp.sum(jnp.where(from_slot, innotes[2][None, :], 0.0), -1, keepdims=True)
    packed = dot_f32(from_slot.astype(jnp.bfloat16), inbox, (1,), (0,)).astype(jnp.bfloat16)

    my_gain = lax.dynamic_slice_in_dim(ln_gain, my_index * part_width, part_width, 0)
    unit_rows = (packed.astype(jnp.float32) - mean) * rstd
    normed = line_gather((unit_rows * my_gain).astype(jnp.bfloat16), "mp")

    d_heads = project(whole_cot, w_out_t, parts, jnp.bfloat16)
    projected = project(normed, w_t, parts, jnp.float32)
    heads_out = attention(forward_kernel, projected, segment, qk_gain, (), 1)
    attn = line_reduce(expand(heads_out, w_out_t, parts, 1), "mp")
    output = (packed.astype(jnp.float32) + attn).astype(jnp.bfloat16)

    d_all = attention(backward_kernel, projected, segment, qk_gain, (d_heads,), 4)
    d_part = expand(d_all, w_t, parts, 2)
    d_normed = lax.psum_scatter(d_part, "mp", scatter_dimension=0, tiled=False)
    d_unit = d_normed.astype(jnp.float32) * my_gain
    sums = jnp.stack([jnp.sum(d_unit, -1), jnp.sum(d_unit * unit_rows, -1)])
    sums = sum(exchange_small(sums, "mp")) / full_width
    d_input = rstd * (d_unit - sums[0][:, None] - unit_rows * sums[1][:, None])
    input_grad = (cotangent.astype(jnp.float32) + d_input).astype(jnp.bfloat16)

    scale_grad = 1.0 / math.sqrt(group_rows * groups)
    cot_cols = columns_to_owner(whole_cot, "dp")
    normed_cols = columns_to_owner(normed[:parts], "dp")
    qkv_grad, out_grad = weight_grads(
        normed_cols, cot_cols, gather_xor(d_all, "dp"), scale_grad
    )
    return (output, input_grad, qkv_grad.transpose(1, 0, 2), out_grad)


def solution(mesh):
    placed = (
        P("dp", "mp"),
        P("dp"),
        P("dp"),
        P("dp"),
        P(),
        P(None, None, "mp"),
        P(),
        P(None, "mp"),
        P("dp", "mp"),
    )
    return jax.shard_map(
        shards,
        mesh=mesh,
        in_specs=placed,
        out_specs=(P("dp", "mp"), P("dp", "mp"), P("dp", None, "mp"), P("dp", "mp")),
        check_vma=False,
    )
```

```python
import functools
import math

import jax
import jax.numpy as jnp
from jax import lax
from jax.experimental import pallas as pl
from jax.experimental.pallas import tpu as pltpu
from jax.sharding import PartitionSpec as P

DH = 128
VMEM_BYTES = 48 * 1024 * 1024


def dot_f32(left, right, left_dims, right_dims):
    return lax.dot_general(
        left, right, ((left_dims, right_dims), ((), ())), preferred_element_type=jnp.float32
    )


def params():
    return pltpu.CompilerParams(vmem_limit_bytes=VMEM_BYTES)


def project_kernel(steps, width, x_ref, w_ref, out_ref, total):
    at, t = pl.program_id(0), pl.program_id(1)
    columns = pl.ds(pl.multiple_of(t * width, width), width)
    term = jnp.dot(x_ref[0], w_ref[0], preferred_element_type=jnp.float32)

    @pl.when(at == 0)
    def _():
        total[:, columns] = term

    @pl.when(at > 0)
    def _():
        total[:, columns] += term

    @pl.when(at == steps - 1)
    def _():
        out_ref[:, columns] = total[:, columns].astype(out_ref.dtype)


def project(x, w, steps, dtype):
    _, rows, part = x.shape
    kinds, depth, width = w.shape
    return pl.pallas_call(
        functools.partial(project_kernel, steps, width),
        grid=(steps, kinds),
        in_specs=[
            pl.BlockSpec((1, rows, part), lambda at, t: (at, 0, 0)),
            pl.BlockSpec((1, part, width), lambda at, t: (t, at, 0)),
        ],
        out_specs=pl.BlockSpec((rows, kinds * width), lambda at, t: (0, 0)),
        out_shape=jax.ShapeDtypeStruct((rows, kinds * width), dtype),
        scratch_shapes=[pltpu.VMEM((rows, kinds * width), jnp.float32)],
        compiler_params=params(),
        cost_estimate=pl.CostEstimate(
            flops=2 * rows * depth * kinds * width,
            bytes_accessed=2 * kinds * depth * width + 2 * rows * depth,
            transcendentals=0,
        ),
    )(x, w)


def add_block_kernel(first, width, at_ref, x_ref, w_ref, *refs):
    out_ref = refs[-1]
    term = jnp.dot(x_ref[...], w_ref[0], preferred_element_type=jnp.float32)
    out_ref[...] = term if first else refs[0][...] + term


def add_block(total, x, w, at):
    rows, part = x.shape
    kinds, _, width = w.shape
    sums = pl.BlockSpec((rows, width), lambda t, at_ref: (0, t))
    before = [] if total is None else [total]
    return pl.pallas_call(
        functools.partial(add_block_kernel, total is None, width),
        grid_spec=pltpu.PrefetchScalarGridSpec(
            num_scalar_prefetch=1,
            grid=(kinds,),
            in_specs=[
                pl.BlockSpec((rows, part), lambda t, at_ref: (0, 0)),
                pl.BlockSpec((1, part, width), lambda t, at_ref: (t, at_ref[0], 0)),
            ]
            + [sums] * len(before),
            out_specs=sums,
        ),
        out_shape=jax.ShapeDtypeStruct((rows, kinds * width), jnp.float32),
        input_output_aliases={} if total is None else {3: 0},
        compiler_params=params(),
        cost_estimate=pl.CostEstimate(
            flops=2 * rows * part * kinds * width,
            bytes_accessed=2 * kinds * part * width + 8 * rows * kinds * width,
            transcendentals=0,
        ),
    )(at.reshape(1).astype(jnp.int32), x, w, *before)


def expand_kernel(kinds, width, x_ref, w_ref, out_ref):
    total = None
    for t in range(kinds):
        term = dot_f32(x_ref[:, t * width : (t + 1) * width], w_ref[t], (1,), (1,))
        total = term if total is None else total + term
    out_ref[0] = total.astype(jnp.bfloat16)


def expand(x, w, parts, cuts):
    rows = x.shape[0]
    kinds, depth, width = w.shape
    part = depth // parts
    piece = part // cuts
    return pl.pallas_call(
        functools.partial(expand_kernel, kinds, width),
        grid=(parts, cuts),
        in_specs=[
            pl.BlockSpec((rows, kinds * width), lambda at, cut: (0, 0)),
            pl.BlockSpec((kinds, piece, width), lambda at, cut: (0, at * cuts + cut, 0)),
        ],
        out_specs=pl.BlockSpec((1, rows, piece), lambda at, cut: (at, 0, cut)),
        out_shape=jax.ShapeDtypeStruct((parts, rows, part), jnp.bfloat16),
        compiler_params=params(),
        cost_estimate=pl.CostEstimate(
            flops=2 * rows * depth * kinds * width,
            bytes_accessed=2 * kinds * depth * width + 2 * rows * depth,
            transcendentals=0,
        ),
    )(x, w)


def unit_heads(raw):
    center = raw - jnp.mean(raw, -1, keepdims=True)
    rstd = lax.rsqrt(jnp.mean(center * center, -1, keepdims=True) + 1e-06)
    return center * rstd, rstd


def head_forward(proj_ref, same, gain_ref, heads, head):
    width = heads * DH
    q_unit, q_rstd = unit_heads(proj_ref[:, head * DH : (head + 1) * DH])
    k_unit, k_rstd = unit_heads(proj_ref[:, width + head * DH : width + (head + 1) * DH])
    values = proj_ref[:, 2 * width + head * DH : 2 * width + (head + 1) * DH].astype(jnp.bfloat16)
    queries = (q_unit * gain_ref[0:1, :]).astype(jnp.bfloat16)
    keys = (k_unit * gain_ref[1:2, :]).astype(jnp.bfloat16)
    scores = dot_f32(queries, keys, (1,), (1,)) * DH ** (-0.5)
    raised = jnp.where(same, jnp.exp(scores), 0.0)
    weights = raised / jnp.sum(raised, -1, keepdims=True)
    return q_unit, q_rstd, k_unit, k_rstd, values, queries, keys, weights


def forward_kernel(heads, proj_ref, row_ref, col_ref, gain_ref, out_ref):
    same = row_ref[...] == col_ref[...]
    for head in range(heads):
        values, _, _, weights = head_forward(proj_ref, same, gain_ref, heads, head)[4:]
        mixed = dot_f32(weights.astype(jnp.bfloat16), values, (1,), (0,))
        out_ref[:, head * DH : (head + 1) * DH] = mixed.astype(jnp.bfloat16)


def unit_backward(grad, unit, rstd, gain):
    scaled = grad.astype(jnp.bfloat16).astype(jnp.float32) * gain
    return rstd * (
        scaled
        - jnp.mean(scaled, -1, keepdims=True)
        - unit * jnp.mean(scaled * unit, -1, keepdims=True)
    )


def backward_kernel(heads, proj_ref, row_ref, col_ref, gain_ref, d_one_ref, d_two_ref, out_ref):
    same = row_ref[...] == col_ref[...]
    width = heads * DH
    for head in range(heads):
        q_unit, q_rstd, k_unit, k_rstd, values, queries, keys, weights = head_forward(
            proj_ref, same, gain_ref, heads, head
        )
        at = head * DH
        weights_bf = weights.astype(jnp.bfloat16)
        d_out = jnp.concatenate([d_one_ref[:, at : at + DH], d_two_ref[:, at : at + DH]], 0)
        mixed = dot_f32(weights_bf, values, (1,), (0,))
        out_ref[:, 3 * width + at : 3 * width + at + DH] = mixed.astype(jnp.bfloat16)
        d_values = dot_f32(weights_bf, d_out, (0,), (0,))
        out_ref[:, 2 * width + at : 2 * width + at + DH] = d_values.astype(jnp.bfloat16)
        d_weights = dot_f32(d_out, values, (1,), (1,)).astype(jnp.bfloat16).astype(jnp.float32)
        inner = jnp.sum(d_weights * weights, -1, keepdims=True)
        d_scores = (weights * (d_weights - inner) * DH ** (-0.5)).astype(jnp.bfloat16)
        d_queries = unit_backward(
            dot_f32(d_scores, keys, (1,), (0,)), q_unit, q_rstd, gain_ref[0:1, :]
        )
        d_keys = unit_backward(
            dot_f32(d_scores, queries, (0,), (0,)), k_unit, k_rstd, gain_ref[1:2, :]
        )
        out_ref[:, at : at + DH] = d_queries.astype(jnp.bfloat16)
        out_ref[:, width + at : width + at + DH] = d_keys.astype(jnp.bfloat16)


def attention(kernel, projected, segment, qk_gain, extra, kinds):
    rows, wide = projected.shape
    heads = wide // (3 * DH)
    return pl.pallas_call(
        functools.partial(kernel, heads),
        out_shape=jax.ShapeDtypeStruct((rows, kinds * heads * DH), jnp.bfloat16),
        compiler_params=params(),
        cost_estimate=pl.CostEstimate(
            flops=heads * rows * rows * DH * 16,
            bytes_accessed=rows * wide * 8,
            transcendentals=heads * rows * rows,
        ),
    )(projected, segment.reshape(rows, 1), segment.reshape(1, rows), qk_gain, *extra)


def weight_kernel(keys, scale, normed_ref, one_ref, two_ref, *refs):
    b_refs, refs = refs[: len(keys)], refs[len(keys) :]
    me, t = lax.axis_index("dp"), pl.program_id(0)

    def product(load, total):
        for order, key in enumerate(keys):
            term = jnp.dot(load(me ^ key), b_refs[order][...], preferred_element_type=jnp.float32)
            if scale is None and order == 0:
                total[...] = term
            else:
                total[...] += term

    def normed(at):
        return normed_ref[at]

    def cot(at):
        return jnp.concatenate([one_ref[at], two_ref[at]], 1)

    if scale is None:
        total = refs[0].at[0]
    else:
        before_ref, qkv_ref, out_ref, total = refs
        total[...] = before_ref[0]

    @pl.when(t < 3)
    def _():
        product(normed, total)
        if scale is not None:
            qkv_ref[0] = (total[...] * scale).astype(jnp.bfloat16)

    @pl.when(t == 3)
    def _():
        product(cot, total)
        if scale is not None:
            out_ref[...] = (total[...] * scale).astype(jnp.bfloat16)


def weight_grads(normed_cols, cot_one, cot_two, gathered, keys, before, scale):
    count, depth, rows = normed_cols.shape
    width = gathered[0].shape[1] // 4
    whole = pl.BlockSpec((count, depth, rows), lambda t: (0, 0, 0))
    half = pl.BlockSpec((count, depth, rows // 2), lambda t: (0, 0, 0))
    sums = pl.BlockSpec((1, depth, width), lambda t: (t, 0, 0))
    sums_shape = jax.ShapeDtypeStruct((4, depth, width), jnp.float32)
    return pl.pallas_call(
        functools.partial(weight_kernel, keys, scale),
        grid=(4,),
        in_specs=[whole, half, half]
        + [pl.BlockSpec((rows, width), lambda t: (0, t))] * len(keys)
        + ([] if before is None else [sums]),
        out_specs=sums
        if before is None
        else [
            pl.BlockSpec((1, depth, width), lambda t: (jnp.minimum(t, 2), 0, 0)),
            pl.BlockSpec((depth, width), lambda t: (0, 0)),
        ],
        out_shape=sums_shape
        if before is None
        else [
            jax.ShapeDtypeStruct((3, depth, width), jnp.bfloat16),
            jax.ShapeDtypeStruct((depth, width), jnp.bfloat16),
        ],
        scratch_shapes=[] if before is None else [pltpu.VMEM((depth, width), jnp.float32)],
        compiler_params=params(),
        cost_estimate=pl.CostEstimate(
            flops=8 * len(keys) * depth * rows * width,
            bytes_accessed=4 * count * depth * rows + 8 * len(keys) * rows * width,
            transcendentals=0,
        ),
    )(normed_cols, cot_one, cot_two, *gathered, *([] if before is None else [before]))


def flip(values, axis, bit):
    count = lax.axis_size(axis)
    return lax.ppermute(values, axis, [(at, at ^ bit) for at in range(count)])


def exchange_small(values, axis):
    return [values] + [flip(values, axis, bit) for bit in range(1, lax.axis_size(axis))]


def gather_xor(values, axis):
    count = lax.axis_size(axis)
    high, low = count // 2, count // 4

    def spread(held):
        bit = low // 2
        while bit >= 1:
            for key in sorted(held):
                held[key | bit] = flip(held[key], axis, bit)
            bit //= 2
        return held

    over_high, over_low = flip(values, axis, high), flip(values, axis, low)
    own = spread({0: values})
    keys = sorted(own)
    spread_own, over_high, over_low = lax.optimization_barrier(
        ([own[key] for key in keys], over_high, over_low)
    )
    even = lax.axis_index(axis) % 2 == 0
    onward = jnp.where(even, over_low, over_high)
    pairs = [(at, at ^ (high if at % 2 == 0 else low)) for at in range(count)]
    far = lax.ppermute(onward, axis, pairs)
    near = dict(zip(keys, spread_own))
    near.update(spread({high: over_high}))
    near.update(spread({low: over_low}))
    return near, spread({high | low: far})


def line_blocks(values, axis, between):
    count, me = lax.axis_size(axis), lax.axis_index(axis)
    blocks = [(me, None, values)]
    right = left = values
    for step in range(1, count):
        right = lax.ppermute(right, axis, [(at, at + 1) for at in range(step - 1, count - 1)])
        left = lax.ppermute(left, axis, [(at, at - 1) for at in range(1, count - step + 1)])
        if step == count // 2:
            right, left = between(right, left)
        over, under = me >= step, me + step < count
        if 2 * step >= count:
            at = jnp.where(over, me - step, jnp.minimum(me + step, count - 1))
            blocks.append((at, over | under, right + left))
        else:
            blocks.append((jnp.maximum(me - step, 0), over, right))
            blocks.append((jnp.minimum(me + step, count - 1), under, left))
    return blocks


def add_bf(one, two):
    return (one.astype(jnp.float32) + two.astype(jnp.float32)).astype(jnp.bfloat16)


def line_reduce(parts, axis):
    count, me = lax.axis_size(axis), lax.axis_index(axis)

    def block(at):
        return lax.dynamic_index_in_dim(parts, jnp.clip(at, 0, count - 1), 0, keepdims=False)

    def send(step, to_right, to_left):
        return (
            lax.ppermute(to_right, axis, [(at, at + 1) for at in range(step)]),
            lax.ppermute(to_left, axis, [(at, at - 1) for at in range(count - step, count)]),
        )

    def go_on(right, left):
        for step in range(2, count):
            right, left = send(
                step,
                add_bf(block(me + count - step), right),
                add_bf(block(me - count + step), left),
            )
        return block(me).astype(jnp.float32) + right.astype(jnp.float32) + left.astype(jnp.float32)

    return send(1, block(me + count - 1), block(me - count + 1)), go_on


def columns_to_owner(turned, axis):
    count = lax.axis_size(axis)
    parts, part, rows = turned.shape
    cut = turned.reshape(count, parts * part // count, rows)
    return lax.all_to_all(cut, axis, 0, 0, tiled=True)


def shards(patches, dest_group, dest_row, segment, ln_gain, w_qkv, qk_gain, w_out, cotangent):
    group_rows, part_width = patches.shape
    groups = lax.axis_size("dp")
    parts = lax.axis_size("mp")
    slot_size = 2 * group_rows // groups
    slots = groups * slot_size
    full_width, local_width = w_out.shape
    my_group, my_index = lax.axis_index("dp"), lax.axis_index("mp")
    w_t = jnp.transpose(w_qkv, (1, 0, 2))
    w_out_t = w_out[None]

    half = group_rows // 2
    first_rows, dest_group = lax.optimization_barrier((cotangent[:half], dest_group))
    cot_one = lax.all_gather(first_rows, "mp", axis=0, tiled=False)

    position = jnp.arange(group_rows, dtype=jnp.int32)
    earlier = (dest_group[:, None] == dest_group[None, :]) & (position[None, :] < position[:, None])
    rank_within = jnp.sum(earlier.astype(jnp.int32), 1)
    place = dest_group * slot_size + rank_within
    to_slot = jnp.arange(slots, dtype=jnp.int32)[:, None] == place[None, :]
    outbox = dot_f32(to_slot.astype(jnp.bfloat16), patches, (1,), (0,)).astype(jnp.bfloat16)
    inbox = lax.all_to_all(
        outbox.reshape(groups, slot_size, part_width), "dp", split_axis=0, concat_axis=0, tiled=True
    ).reshape(slots, part_width)

    outbox, late_patches = lax.optimization_barrier((outbox, patches))
    wide = late_patches.astype(jnp.float32)
    part_mean = jnp.mean(wide, -1)
    part_dev = jnp.sum(jnp.square(wide - part_mean[:, None]), -1)
    seen = exchange_small(jnp.stack([part_mean, part_dev]), "mp")
    row_mean = sum(entry[0] for entry in seen) / parts
    row_dev = sum(entry[1] + part_width * jnp.square(entry[0] - row_mean) for entry in seen)
    row_rstd = lax.rsqrt(row_dev / full_width + 1e-06)
    notes = jnp.stack([dest_row.astype(jnp.float32) + 1.0, row_mean, row_rstd])
    outnotes = jnp.sum(jnp.where(to_slot[None], notes[:, None, :], 0.0), -1)
    outnotes = outnotes.reshape(3, groups, slot_size)
    came = []
    for bit in range(groups):
        mine = lax.dynamic_index_in_dim(outnotes, my_group ^ bit, 1, keepdims=False)
        came.append(mine if bit == 0 else flip(mine, "dp", bit))
    sender = jnp.arange(groups, dtype=jnp.int32)[None, :, None]
    innotes = sum(
        jnp.where(sender == (my_group ^ bit), entry[:, None, :], 0.0)
        for bit, entry in enumerate(came)
    ).reshape(3, slots)
    arrived_at = innotes[0].astype(jnp.int32) - 1
    from_slot = position[:, None] == arrived_at[None, :]
    mean = jnp.sum(jnp.where(from_slot, innotes[1][None, :], 0.0), -1, keepdims=True)
    rstd = jnp.sum(jnp.where(from_slot, innotes[2][None, :], 0.0), -1, keepdims=True)
    packed = dot_f32(from_slot.astype(jnp.bfloat16), inbox, (1,), (0,)).astype(jnp.bfloat16)

    my_gain = lax.dynamic_slice_in_dim(ln_gain, my_index * part_width, part_width, 0)
    unit_rows = (packed.astype(jnp.float32) - mean) * rstd
    normed_part = (unit_rows * my_gain).astype(jnp.bfloat16)
    normed_part, cot_one = lax.optimization_barrier((normed_part, cot_one))

    late = [None]

    def between(right, left):
        right, left, late[0] = lax.optimization_barrier((right, left, cotangent[half:]))
        return right, left

    blocks = line_blocks(normed_part, "mp", between)
    cot_two = lax.all_gather(late[0], "mp", axis=0, tiled=False)
    cot_cols_one = columns_to_owner(jnp.swapaxes(cot_one, 1, 2), "dp")
    d_heads_one = project(cot_one, w_out_t, parts, jnp.bfloat16)
    projected = None
    turned = jnp.zeros((parts, part_width, group_rows), jnp.bfloat16)
    for order, (at, there, block) in enumerate(blocks):
        if order == len(blocks) - 1:
            block, cot_cols_one, d_heads_one, projected = lax.optimization_barrier(
                (block, cot_cols_one, d_heads_one, projected)
            )
        projected = add_block(projected, block, w_t, at)
        block_t = block.T
        if there is not None:
            held = lax.dynamic_index_in_dim(turned, at, 0, keepdims=False)
            block_t = jnp.where(there, block_t, held)
        turned = lax.dynamic_update_index_in_dim(turned, block_t, at, 0)
    normed_cols = columns_to_owner(turned, "dp")

    heads_out = attention(forward_kernel, projected, segment, qk_gain, (), 1)
    first_step, go_on = line_reduce(expand(heads_out, w_out_t, parts, 1), "mp")
    d_heads_two = project(cot_two, w_out_t, parts, jnp.bfloat16)
    first_step, normed_cols, d_heads_one, d_heads_two = lax.optimization_barrier(
        (first_step, normed_cols, d_heads_one, d_heads_two)
    )
    attn = go_on(*first_step)
    output = (packed.astype(jnp.float32) + attn).astype(jnp.bfloat16)

    d_all = attention(backward_kernel, projected, segment, qk_gain, (d_heads_one, d_heads_two), 4)
    d_part = expand(d_all, w_t, parts, 2)
    d_normed = lax.psum_scatter(d_part, "mp", scatter_dimension=0, tiled=False)
    d_unit = d_normed.astype(jnp.float32) * my_gain
    sums = jnp.stack([jnp.sum(d_unit, -1), jnp.sum(d_unit * unit_rows, -1)])
    sums = sum(exchange_small(sums, "mp")) / full_width
    d_input = rstd * (d_unit - sums[0][:, None] - unit_rows * sums[1][:, None])
    input_grad = (cotangent.astype(jnp.float32) + d_input).astype(jnp.bfloat16)

    scale_grad = 1.0 / math.sqrt(group_rows * groups)
    cot_cols_two = columns_to_owner(jnp.swapaxes(cot_two, 1, 2), "dp")
    columns = (normed_cols, cot_cols_one, cot_cols_two)
    sums_near = None
    near, far = gather_xor(d_all, "dp")
    for held, scale in ((near, None), (far, scale_grad)):
        keys = sorted(held)
        sums_near = weight_grads(*columns, [held[key] for key in keys], keys, sums_near, scale)
    qkv_grad, out_grad = sums_near
    return (output, input_grad, qkv_grad.transpose(1, 0, 2), out_grad)


def solution(mesh):
    placed = (
        P("dp", "mp"),
        P("dp"),
        P("dp"),
        P("dp"),
        P(),
        P(None, None, "mp"),
        P(),
        P(None, "mp"),
        P("dp", "mp"),
    )
    return jax.shard_map(
        shards,
        mesh=mesh,
        in_specs=placed,
        out_specs=(P("dp", "mp"), P("dp", "mp"), P("dp", None, "mp"), P("dp", "mp")),
        check_vma=False,
    )
```

```python
import functools
import math

import jax
import jax.numpy as jnp
from jax import lax
from jax.experimental import pallas as pl
from jax.experimental.pallas import tpu as pltpu
from jax.sharding import PartitionSpec as P

DH = 128
VMEM_BYTES = 48 * 1024 * 1024


def dot_f32(left, right, left_dims, right_dims):
    return lax.dot_general(
        left, right, ((left_dims, right_dims), ((), ())), preferred_element_type=jnp.float32
    )


def params():
    return pltpu.CompilerParams(vmem_limit_bytes=VMEM_BYTES)


def project_kernel(steps, width, x_ref, w_ref, out_ref, total):
    at, t = pl.program_id(0), pl.program_id(1)
    columns = pl.ds(pl.multiple_of(t * width, width), width)
    term = jnp.dot(x_ref[0], w_ref[0], preferred_element_type=jnp.float32)

    @pl.when(at == 0)
    def _():
        total[:, columns] = term

    @pl.when(at > 0)
    def _():
        total[:, columns] += term

    @pl.when(at == steps - 1)
    def _():
        out_ref[:, columns] = total[:, columns].astype(out_ref.dtype)


def project(x, w, steps, dtype):
    _, rows, part = x.shape
    kinds, depth, width = w.shape
    return pl.pallas_call(
        functools.partial(project_kernel, steps, width),
        grid=(steps, kinds),
        in_specs=[
            pl.BlockSpec((1, rows, part), lambda at, t: (at, 0, 0)),
            pl.BlockSpec((1, part, width), lambda at, t: (t, at, 0)),
        ],
        out_specs=pl.BlockSpec((rows, kinds * width), lambda at, t: (0, 0)),
        out_shape=jax.ShapeDtypeStruct((rows, kinds * width), dtype),
        scratch_shapes=[pltpu.VMEM((rows, kinds * width), jnp.float32)],
        compiler_params=params(),
        cost_estimate=pl.CostEstimate(
            flops=2 * rows * depth * kinds * width,
            bytes_accessed=2 * kinds * depth * width + 2 * rows * depth,
            transcendentals=0,
        ),
    )(x, w)


def expand_kernel(kinds, width, x_ref, w_ref, out_ref):
    total = None
    for t in range(kinds):
        term = dot_f32(w_ref[t], x_ref[:, t * width : (t + 1) * width], (1,), (1,))
        total = term if total is None else total + term
    out_ref[0] = total.astype(jnp.bfloat16)


def expand(x, w, parts, cuts):
    rows = x.shape[0]
    kinds, depth, width = w.shape
    part = depth // parts
    piece = part // cuts
    return pl.pallas_call(
        functools.partial(expand_kernel, kinds, width),
        grid=(parts, cuts),
        in_specs=[
            pl.BlockSpec((rows, kinds * width), lambda at, cut: (0, 0)),
            pl.BlockSpec((kinds, piece, width), lambda at, cut: (0, at * cuts + cut, 0)),
        ],
        out_specs=pl.BlockSpec((1, piece, rows), lambda at, cut: (at, cut, 0)),
        out_shape=jax.ShapeDtypeStruct((parts, part, rows), jnp.bfloat16),
        compiler_params=params(),
        cost_estimate=pl.CostEstimate(
            flops=2 * rows * depth * kinds * width,
            bytes_accessed=2 * kinds * depth * width + 2 * rows * depth,
            transcendentals=0,
        ),
    )(x, w)


def unit_heads(raw):
    center = raw - jnp.mean(raw, -1, keepdims=True)
    rstd = lax.rsqrt(jnp.mean(center * center, -1, keepdims=True) + 1e-06)
    return center * rstd, rstd


def head_forward(proj_ref, same, gain_ref, heads, head):
    width = heads * DH

    def load(kind):
        start = kind * width + head * DH
        return proj_ref[:, start : start + DH]

    q_unit, q_rstd = unit_heads(load(0))
    k_unit, k_rstd = unit_heads(load(1))
    values = load(2).astype(jnp.bfloat16)
    queries = (q_unit * gain_ref[0:1, :]).astype(jnp.bfloat16)
    keys = (k_unit * gain_ref[1:2, :]).astype(jnp.bfloat16)
    scores = dot_f32(queries, keys, (1,), (1,)) * DH ** (-0.5)
    raised = jnp.where(same, jnp.exp(scores), 0.0)
    weights = raised / jnp.sum(raised, -1, keepdims=True)
    return q_unit, q_rstd, k_unit, k_rstd, values, queries, keys, weights


def forward_kernel(heads, proj_ref, row_ref, col_ref, gain_ref, out_ref):
    same = row_ref[...] == col_ref[...]
    for head in range(heads):
        values, _, _, weights = head_forward(proj_ref, same, gain_ref, heads, head)[4:]
        mixed = dot_f32(weights.astype(jnp.bfloat16), values, (1,), (0,))
        out_ref[:, head * DH : (head + 1) * DH] = mixed.astype(jnp.bfloat16)


def unit_backward(grad, unit, rstd, gain):
    scaled = grad.astype(jnp.bfloat16).astype(jnp.float32) * gain
    return rstd * (
        scaled
        - jnp.mean(scaled, -1, keepdims=True)
        - unit * jnp.mean(scaled * unit, -1, keepdims=True)
    )


def backward_kernel(heads, proj_ref, row_ref, col_ref, gain_ref, d_one_ref, d_two_ref, out_ref):
    same = row_ref[...] == col_ref[...]
    width = heads * DH
    for head in range(heads):
        q_unit, q_rstd, k_unit, k_rstd, values, queries, keys, weights = head_forward(
            proj_ref, same, gain_ref, heads, head
        )
        at = head * DH
        weights_bf = weights.astype(jnp.bfloat16)
        d_out = jnp.concatenate([d_one_ref[:, at : at + DH], d_two_ref[:, at : at + DH]], 0)
        mixed = dot_f32(weights_bf, values, (1,), (0,))
        out_ref[:, 3 * width + at : 3 * width + at + DH] = mixed.astype(jnp.bfloat16)
        d_values = dot_f32(weights_bf, d_out, (0,), (0,))
        out_ref[:, 2 * width + at : 2 * width + at + DH] = d_values.astype(jnp.bfloat16)
        d_weights = dot_f32(d_out, values, (1,), (1,)).astype(jnp.bfloat16).astype(jnp.float32)
        inner = jnp.sum(d_weights * weights, -1, keepdims=True)
        d_scores = (weights * (d_weights - inner) * DH ** (-0.5)).astype(jnp.bfloat16)
        d_queries = unit_backward(
            dot_f32(d_scores, keys, (1,), (0,)), q_unit, q_rstd, gain_ref[0:1, :]
        )
        d_keys = unit_backward(
            dot_f32(d_scores, queries, (0,), (0,)), k_unit, k_rstd, gain_ref[1:2, :]
        )
        out_ref[:, at : at + DH] = d_queries.astype(jnp.bfloat16)
        out_ref[:, width + at : width + at + DH] = d_keys.astype(jnp.bfloat16)


def attention(kernel, projected, segment, qk_gain, extra, kinds):
    rows, wide = projected.shape
    heads = wide // (3 * DH)
    return pl.pallas_call(
        functools.partial(kernel, heads),
        out_shape=jax.ShapeDtypeStruct((rows, kinds * heads * DH), jnp.bfloat16),
        compiler_params=params(),
        cost_estimate=pl.CostEstimate(
            flops=heads * rows * rows * DH * 16,
            bytes_accessed=rows * wide * 8,
            transcendentals=heads * rows * rows,
        ),
    )(projected, segment.reshape(rows, 1), segment.reshape(1, rows), qk_gain, *extra)


def weight_kernel(keys, scale, normed_ref, cot_ref, *refs):
    b_refs, refs = refs[: len(keys)], refs[len(keys) :]
    me, t = lax.axis_index("dp"), pl.program_id(0)

    def product(load, total):
        for order, key in enumerate(keys):
            term = jnp.dot(load(me ^ key), b_refs[order][...], preferred_element_type=jnp.float32)
            if scale is None and order == 0:
                total[...] = term
            else:
                total[...] += term

    def normed(at):
        return normed_ref[at]

    def cot(at):
        return cot_ref[at]

    if scale is None:
        total = refs[0].at[0]
    else:
        before_ref, qkv_ref, out_ref, total = refs
        total[...] = before_ref[0]

    @pl.when(t < 3)
    def _():
        product(normed, total)
        if scale is not None:
            qkv_ref[0] = (total[...] * scale).astype(jnp.bfloat16)

    @pl.when(t == 3)
    def _():
        product(cot, total)
        if scale is not None:
            out_ref[...] = (total[...] * scale).astype(jnp.bfloat16)


def weight_grads(normed_cols, cot_cols, gathered, keys, before, scale):
    count, depth, rows = normed_cols.shape
    width = gathered[0].shape[1] // 4
    whole = pl.BlockSpec((count, depth, rows), lambda t: (0, 0, 0))
    sums = pl.BlockSpec((1, depth, width), lambda t: (t, 0, 0))
    sums_shape = jax.ShapeDtypeStruct((4, depth, width), jnp.float32)
    return pl.pallas_call(
        functools.partial(weight_kernel, keys, scale),
        grid=(4,),
        in_specs=[whole, whole]
        + [pl.BlockSpec((rows, width), lambda t: (0, t))] * len(keys)
        + ([] if before is None else [sums]),
        out_specs=sums
        if before is None
        else [
            pl.BlockSpec((1, depth, width), lambda t: (jnp.minimum(t, 2), 0, 0)),
            pl.BlockSpec((depth, width), lambda t: (0, 0)),
        ],
        out_shape=sums_shape
        if before is None
        else [
            jax.ShapeDtypeStruct((3, depth, width), jnp.bfloat16),
            jax.ShapeDtypeStruct((depth, width), jnp.bfloat16),
        ],
        scratch_shapes=[] if before is None else [pltpu.VMEM((depth, width), jnp.float32)],
        compiler_params=params(),
        cost_estimate=pl.CostEstimate(
            flops=8 * len(keys) * depth * rows * width,
            bytes_accessed=4 * count * depth * rows + 8 * len(keys) * rows * width,
            transcendentals=0,
        ),
    )(normed_cols, cot_cols, *gathered, *([] if before is None else [before]))


def flip(values, axis, bit):
    count = lax.axis_size(axis)
    return lax.ppermute(values, axis, [(at, at ^ bit) for at in range(count)])


def exchange_small(values, axis):
    return [values] + [flip(values, axis, bit) for bit in range(1, lax.axis_size(axis))]


def gather_xor(values, axis):
    count = lax.axis_size(axis)
    high, low = count // 2, count // 4

    def spread(held):
        bit = low // 2
        while bit >= 1:
            for key in sorted(held):
                held[key | bit] = flip(held[key], axis, bit)
            bit //= 2
        return held

    over_high, over_low = flip(values, axis, high), flip(values, axis, low)
    own = spread({0: values})
    keys = sorted(own)
    spread_own, over_high, over_low = lax.optimization_barrier(
        ([own[key] for key in keys], over_high, over_low)
    )
    even = lax.axis_index(axis) % 2 == 0
    onward = jnp.where(even, over_low, over_high)
    pairs = [(at, at ^ (high if at % 2 == 0 else low)) for at in range(count)]
    far = lax.ppermute(onward, axis, pairs)
    near = dict(zip(keys, spread_own))
    near.update(spread({high: over_high}))
    near.update(spread({low: over_low}))
    return near, spread({high | low: far})


def add_bf(one, two):
    return (one.astype(jnp.float32) + two.astype(jnp.float32)).astype(jnp.bfloat16)


def line_reduce(parts, axis):
    count, me = lax.axis_size(axis), lax.axis_index(axis)

    def block(at):
        return lax.dynamic_index_in_dim(parts, jnp.clip(at, 0, count - 1), 0, keepdims=False)

    def send(step, to_right, to_left):
        return (
            lax.ppermute(to_right, axis, [(at, at + 1) for at in range(step)]),
            lax.ppermute(to_left, axis, [(at, at - 1) for at in range(count - step, count)]),
        )

    def go_on(right, left):
        for step in range(2, count):
            right, left = send(
                step,
                add_bf(block(me + count - step), right),
                add_bf(block(me - count + step), left),
            )
        return block(me).astype(jnp.float32) + right.astype(jnp.float32) + left.astype(jnp.float32)

    return send(1, block(me + count - 1), block(me - count + 1)), go_on


def columns_to_owner(turned, axis):
    count = lax.axis_size(axis)
    parts, part, rows = turned.shape
    cut = turned.reshape(count, parts * part // count, rows)
    return lax.all_to_all(cut, axis, 0, 0, tiled=True)


def shards(patches, dest_group, dest_row, segment, ln_gain, w_qkv, qk_gain, w_out, cotangent):
    group_rows, part_width = patches.shape
    groups = lax.axis_size("dp")
    parts = lax.axis_size("mp")
    slot_size = 2 * group_rows // groups
    slots = groups * slot_size
    full_width, local_width = w_out.shape
    my_group, my_index = lax.axis_index("dp"), lax.axis_index("mp")
    w_t = jnp.transpose(w_qkv, (1, 0, 2))
    w_out_t = w_out[None]

    early = group_rows // 4
    first_rows, dest_group = lax.optimization_barrier((cotangent[:early], dest_group))
    cot_one = lax.all_gather(first_rows, "mp", axis=0, tiled=False)

    position = jnp.arange(group_rows, dtype=jnp.int32)
    earlier = (dest_group[:, None] == dest_group[None, :]) & (position[None, :] < position[:, None])
    rank_within = jnp.sum(earlier.astype(jnp.int32), 1)
    place = dest_group * slot_size + rank_within
    to_slot = jnp.arange(slots, dtype=jnp.int32)[:, None] == place[None, :]
    outbox = dot_f32(to_slot.astype(jnp.bfloat16), patches, (1,), (0,)).astype(jnp.bfloat16)
    inbox = lax.all_to_all(
        outbox.reshape(groups, slot_size, part_width), "dp", split_axis=0, concat_axis=0, tiled=True
    ).reshape(slots, part_width)

    outbox, late_patches = lax.optimization_barrier((outbox, patches))
    wide = late_patches.astype(jnp.float32)
    part_mean = jnp.mean(wide, -1)
    part_dev = jnp.sum(jnp.square(wide - part_mean[:, None]), -1)
    seen = exchange_small(jnp.stack([part_mean, part_dev]), "mp")
    row_mean = sum(entry[0] for entry in seen) / parts
    row_dev = sum(entry[1] + part_width * jnp.square(entry[0] - row_mean) for entry in seen)
    row_rstd = lax.rsqrt(row_dev / full_width + 1e-06)
    notes = jnp.stack([dest_row.astype(jnp.float32) + 1.0, row_mean, row_rstd])
    outnotes = jnp.sum(jnp.where(to_slot[None], notes[:, None, :], 0.0), -1)
    outnotes = outnotes.reshape(3, groups, slot_size)
    came = []
    for bit in range(groups):
        mine = lax.dynamic_index_in_dim(outnotes, my_group ^ bit, 1, keepdims=False)
        came.append(mine if bit == 0 else flip(mine, "dp", bit))
    sender = jnp.arange(groups, dtype=jnp.int32)[None, :, None]
    innotes = sum(
        jnp.where(sender == (my_group ^ bit), entry[:, None, :], 0.0)
        for bit, entry in enumerate(came)
    ).reshape(3, slots)
    arrived_at = innotes[0].astype(jnp.int32) - 1
    from_slot = position[:, None] == arrived_at[None, :]
    mean = jnp.sum(jnp.where(from_slot, innotes[1][None, :], 0.0), -1, keepdims=True)
    rstd = jnp.sum(jnp.where(from_slot, innotes[2][None, :], 0.0), -1, keepdims=True)
    packed = dot_f32(from_slot.astype(jnp.bfloat16), inbox, (1,), (0,)).astype(jnp.bfloat16)

    my_gain = lax.dynamic_slice_in_dim(ln_gain, my_index * part_width, part_width, 0)
    unit_rows = (packed.astype(jnp.float32) - mean) * rstd
    normed_part = (unit_rows * my_gain).astype(jnp.bfloat16)

    normed_part, cot_one = lax.optimization_barrier((normed_part, cot_one))
    normed = lax.all_gather(normed_part, "mp", axis=0, tiled=False)
    d_heads_one = project(cot_one, w_out_t, parts, jnp.bfloat16)
    normed, d_heads_one, late_cot = lax.optimization_barrier(
        (normed, d_heads_one, cotangent[early:])
    )
    cot_two = lax.all_gather(late_cot, "mp", axis=0, tiled=False)
    projected = project(normed, w_t, parts, jnp.float32)

    heads_out = attention(forward_kernel, projected, segment, qk_gain, (), 1)
    first_step, go_on = line_reduce(expand(heads_out, w_out_t, parts, 1), "mp")
    normed_cols = columns_to_owner(jnp.swapaxes(normed, 1, 2), "dp")
    d_heads_two = project(cot_two, w_out_t, parts, jnp.bfloat16)
    first_step, normed_cols, d_heads_one, d_heads_two = lax.optimization_barrier(
        (first_step, normed_cols, d_heads_one, d_heads_two)
    )
    attn = go_on(*first_step).T
    output = (packed.astype(jnp.float32) + attn).astype(jnp.bfloat16)

    d_all = attention(backward_kernel, projected, segment, qk_gain, (d_heads_one, d_heads_two), 4)
    d_part = expand(d_all, w_t, parts, 2)
    d_normed = lax.psum_scatter(d_part, "mp", scatter_dimension=0, tiled=False)
    d_unit = d_normed.T.astype(jnp.float32) * my_gain
    sums = jnp.stack([jnp.sum(d_unit, -1), jnp.sum(d_unit * unit_rows, -1)])
    sums = sum(exchange_small(sums, "mp")) / full_width
    d_input = rstd * (d_unit - sums[0][:, None] - unit_rows * sums[1][:, None])
    input_grad = (cotangent.astype(jnp.float32) + d_input).astype(jnp.bfloat16)

    scale_grad = 1.0 / math.sqrt(group_rows * groups)
    cot_turned = jnp.swapaxes(jnp.concatenate([cot_one, cot_two], 1), 1, 2)
    columns = (normed_cols, columns_to_owner(cot_turned, "dp"))
    sums_near = None
    near, far = gather_xor(d_all, "dp")
    for held, scale in ((near, None), (far, scale_grad)):
        keys = sorted(held)
        sums_near = weight_grads(*columns, [held[key] for key in keys], keys, sums_near, scale)
    qkv_grad, out_grad = sums_near
    return (output, input_grad, qkv_grad.transpose(1, 0, 2), out_grad)


def solution(mesh):
    placed = (
        P("dp", "mp"),
        P("dp"),
        P("dp"),
        P("dp"),
        P(),
        P(None, None, "mp"),
        P(),
        P(None, "mp"),
        P("dp", "mp"),
    )
    return jax.shard_map(
        shards,
        mesh=mesh,
        in_specs=placed,
        out_specs=(P("dp", "mp"), P("dp", "mp"), P("dp", None, "mp"), P("dp", "mp")),
        check_vma=False,
    )
```

```python
import functools
import math

import jax
import jax.numpy as jnp
from jax import lax
from jax.experimental import pallas as pl
from jax.experimental.pallas import tpu as pltpu
from jax.sharding import PartitionSpec as P

DH = 128
VMEM_BYTES = 48 * 1024 * 1024


def dot_f32(left, right, left_dims, right_dims):
    return lax.dot_general(
        left, right, ((left_dims, right_dims), ((), ())), preferred_element_type=jnp.float32
    )


def params():
    return pltpu.CompilerParams(vmem_limit_bytes=VMEM_BYTES)


def turn_kernel(x_ref, one_ref, two_ref):
    half = one_ref.shape[1]
    one_ref[...] = x_ref[:half, :].T
    two_ref[...] = x_ref[half:, :].T


def turn_halves(x):
    rows, part = x.shape
    shape = jax.ShapeDtypeStruct((part, rows // 2), x.dtype)
    return pl.pallas_call(
        turn_kernel,
        out_shape=[shape, shape],
        compiler_params=params(),
        cost_estimate=pl.CostEstimate(flops=0, bytes_accessed=4 * rows * part, transcendentals=0),
    )(x)


def project_kernel(steps, width, x_ref, w_ref, out_ref, total, block):
    at, t = pl.program_id(0), pl.program_id(1)
    columns = pl.ds(pl.multiple_of(t * width, width), width)

    @pl.when(t == 0)
    def _():
        block[...] = x_ref[0].T

    term = jnp.dot(block[...], w_ref[0], preferred_element_type=jnp.float32)

    @pl.when(at == 0)
    def _():
        total[:, columns] = term

    @pl.when(at > 0)
    def _():
        total[:, columns] += term

    @pl.when(at == steps - 1)
    def _():
        out_ref[:, columns] = total[:, columns].astype(out_ref.dtype)


def project(x, w, dtype):
    steps, part, rows = x.shape
    kinds, depth, width = w.shape
    return pl.pallas_call(
        functools.partial(project_kernel, steps, width),
        grid=(steps, kinds),
        in_specs=[
            pl.BlockSpec((1, part, rows), lambda at, t: (at, 0, 0)),
            pl.BlockSpec((1, part, width), lambda at, t: (t, at, 0)),
        ],
        out_specs=pl.BlockSpec((rows, kinds * width), lambda at, t: (0, 0)),
        out_shape=jax.ShapeDtypeStruct((rows, kinds * width), dtype),
        scratch_shapes=[
            pltpu.VMEM((rows, kinds * width), jnp.float32),
            pltpu.VMEM((rows, part), jnp.bfloat16),
        ],
        compiler_params=params(),
        cost_estimate=pl.CostEstimate(
            flops=2 * rows * depth * kinds * width,
            bytes_accessed=2 * kinds * depth * width + 2 * rows * depth,
            transcendentals=0,
        ),
    )(x, w)


def expand_kernel(kinds, width, x_ref, w_ref, *refs):
    total = None
    for t in range(kinds):
        term = dot_f32(w_ref[t], x_ref[:, t * width : (t + 1) * width], (1,), (1,))
        total = term if total is None else total + term
    if len(refs) == 1:
        (out_ref,) = refs
    else:
        gain_ref, normed_ref, out_ref, sums_ref = refs

        @pl.when((pl.program_id(0) == 0) & (pl.program_id(1) == 0))
        def _():
            sums_ref[...] = jnp.zeros_like(sums_ref)

        sums_ref[0:1, :] += jnp.sum(total * gain_ref[...], 0, keepdims=True)
        sums_ref[1:2, :] += jnp.sum(total * normed_ref[0].astype(jnp.float32), 0, keepdims=True)
    out_ref[0] = total.astype(jnp.bfloat16)


def expand(x, w, parts, cuts, gain=None, normed=None):
    rows = x.shape[0]
    kinds, depth, width = w.shape
    part = depth // parts
    piece = part // cuts
    turned = pl.BlockSpec((1, piece, rows), lambda at, cut: (at, cut, 0))
    turned_shape = jax.ShapeDtypeStruct((parts, part, rows), jnp.bfloat16)
    more = [] if gain is None else [gain, normed]
    return pl.pallas_call(
        functools.partial(expand_kernel, kinds, width),
        grid=(parts, cuts),
        in_specs=[
            pl.BlockSpec((rows, kinds * width), lambda at, cut: (0, 0)),
            pl.BlockSpec((kinds, piece, width), lambda at, cut: (0, at * cuts + cut, 0)),
        ]
        + ([pl.BlockSpec((piece, 1), lambda at, cut: (at * cuts + cut, 0)), turned] if more else []),
        out_specs=[turned, pl.BlockSpec((2, rows), lambda at, cut: (0, 0))] if more else turned,
        out_shape=[turned_shape, jax.ShapeDtypeStruct((2, rows), jnp.float32)]
        if more
        else turned_shape,
        compiler_params=params(),
        cost_estimate=pl.CostEstimate(
            flops=2 * rows * depth * kinds * width,
            bytes_accessed=2 * kinds * depth * width + 2 * rows * depth,
            transcendentals=0,
        ),
    )(x, w, *more)


def unit_heads(raw):
    center = raw - jnp.mean(raw, -1, keepdims=True)
    rstd = lax.rsqrt(jnp.mean(center * center, -1, keepdims=True) + 1e-06)
    return center * rstd, rstd


def head_forward(proj_ref, same, gain_ref, heads, head):
    width = heads * DH

    def load(kind):
        start = kind * width + head * DH
        return proj_ref[:, start : start + DH]

    q_unit, q_rstd = unit_heads(load(0))
    k_unit, k_rstd = unit_heads(load(1))
    values = load(2).astype(jnp.bfloat16)
    queries = (q_unit * gain_ref[0:1, :]).astype(jnp.bfloat16)
    keys = (k_unit * gain_ref[1:2, :]).astype(jnp.bfloat16)
    scores = dot_f32(queries, keys, (1,), (1,)) * DH ** (-0.5)
    raised = jnp.where(same, jnp.exp(scores), 0.0)
    weights = raised / jnp.sum(raised, -1, keepdims=True)
    return q_unit, q_rstd, k_unit, k_rstd, values, queries, keys, weights


def forward_kernel(heads, proj_ref, row_ref, col_ref, gain_ref, out_ref):
    same = row_ref[...] == col_ref[...]
    for head in range(heads):
        values, _, _, weights = head_forward(proj_ref, same, gain_ref, heads, head)[4:]
        mixed = dot_f32(weights.astype(jnp.bfloat16), values, (1,), (0,))
        out_ref[:, head * DH : (head + 1) * DH] = mixed.astype(jnp.bfloat16)


def unit_backward(grad, unit, rstd, gain):
    scaled = grad.astype(jnp.bfloat16).astype(jnp.float32) * gain
    return rstd * (
        scaled
        - jnp.mean(scaled, -1, keepdims=True)
        - unit * jnp.mean(scaled * unit, -1, keepdims=True)
    )


def backward_kernel(heads, proj_ref, row_ref, col_ref, gain_ref, d_one_ref, d_two_ref, out_ref):
    same = row_ref[...] == col_ref[...]
    width = heads * DH
    for head in range(heads):
        q_unit, q_rstd, k_unit, k_rstd, values, queries, keys, weights = head_forward(
            proj_ref, same, gain_ref, heads, head
        )
        at = head * DH
        weights_bf = weights.astype(jnp.bfloat16)
        d_out = jnp.concatenate([d_one_ref[:, at : at + DH], d_two_ref[:, at : at + DH]], 0)
        mixed = dot_f32(weights_bf, values, (1,), (0,))
        out_ref[:, 3 * width + at : 3 * width + at + DH] = mixed.astype(jnp.bfloat16)
        d_values = dot_f32(weights_bf, d_out, (0,), (0,))
        out_ref[:, 2 * width + at : 2 * width + at + DH] = d_values.astype(jnp.bfloat16)
        d_weights = dot_f32(d_out, values, (1,), (1,)).astype(jnp.bfloat16).astype(jnp.float32)
        inner = jnp.sum(d_weights * weights, -1, keepdims=True)
        d_scores = (weights * (d_weights - inner) * DH ** (-0.5)).astype(jnp.bfloat16)
        d_queries = unit_backward(
            dot_f32(d_scores, keys, (1,), (0,)), q_unit, q_rstd, gain_ref[0:1, :]
        )
        d_keys = unit_backward(
            dot_f32(d_scores, queries, (0,), (0,)), k_unit, k_rstd, gain_ref[1:2, :]
        )
        out_ref[:, at : at + DH] = d_queries.astype(jnp.bfloat16)
        out_ref[:, width + at : width + at + DH] = d_keys.astype(jnp.bfloat16)


def attention(kernel, projected, segment, qk_gain, extra, kinds):
    rows, wide = projected.shape
    heads = wide // (3 * DH)
    return pl.pallas_call(
        functools.partial(kernel, heads),
        out_shape=jax.ShapeDtypeStruct((rows, kinds * heads * DH), jnp.bfloat16),
        compiler_params=params(),
        cost_estimate=pl.CostEstimate(
            flops=heads * rows * rows * DH * 16,
            bytes_accessed=rows * wide * 8,
            transcendentals=heads * rows * rows,
        ),
    )(projected, segment.reshape(rows, 1), segment.reshape(1, rows), qk_gain, *extra)


def weight_kernel(keys, scale, normed_ref, one_ref, two_ref, *refs):
    b_refs, refs = refs[: len(keys)], refs[len(keys) :]
    me, t = lax.axis_index("dp"), pl.program_id(0)

    def product(load, total):
        for order, key in enumerate(keys):
            term = jnp.dot(load(me ^ key), b_refs[order][...], preferred_element_type=jnp.float32)
            if scale is None and order == 0:
                total[...] = term
            else:
                total[...] += term

    def normed(at):
        return normed_ref[at]

    def cot(at):
        return jnp.concatenate([one_ref[at], two_ref[at]], 1)

    if scale is None:
        total = refs[0].at[0]
    else:
        before_ref, qkv_ref, out_ref, total = refs
        total[...] = before_ref[0]

    @pl.when(t < 3)
    def _():
        product(normed, total)
        if scale is not None:
            qkv_ref[0] = (total[...] * scale).astype(jnp.bfloat16)

    @pl.when(t == 3)
    def _():
        product(cot, total)
        if scale is not None:
            out_ref[...] = (total[...] * scale).astype(jnp.bfloat16)


def weight_grads(normed_cols, cot_one, cot_two, gathered, keys, before, scale):
    count, depth, rows = normed_cols.shape
    width = gathered[0].shape[1] // 4
    whole = pl.BlockSpec((count, depth, rows), lambda t: (0, 0, 0))
    half = pl.BlockSpec((count, depth, rows // 2), lambda t: (0, 0, 0))
    sums = pl.BlockSpec((1, depth, width), lambda t: (t, 0, 0))
    sums_shape = jax.ShapeDtypeStruct((4, depth, width), jnp.float32)
    return pl.pallas_call(
        functools.partial(weight_kernel, keys, scale),
        grid=(4,),
        in_specs=[whole, half, half]
        + [pl.BlockSpec((rows, width), lambda t: (0, t))] * len(keys)
        + ([] if before is None else [sums]),
        out_specs=sums
        if before is None
        else [
            pl.BlockSpec((1, depth, width), lambda t: (jnp.minimum(t, 2), 0, 0)),
            pl.BlockSpec((depth, width), lambda t: (0, 0)),
        ],
        out_shape=sums_shape
        if before is None
        else [
            jax.ShapeDtypeStruct((3, depth, width), jnp.bfloat16),
            jax.ShapeDtypeStruct((depth, width), jnp.bfloat16),
        ],
        scratch_shapes=[] if before is None else [pltpu.VMEM((depth, width), jnp.float32)],
        compiler_params=params(),
        cost_estimate=pl.CostEstimate(
            flops=8 * len(keys) * depth * rows * width,
            bytes_accessed=4 * count * depth * rows + 8 * len(keys) * rows * width,
            transcendentals=0,
        ),
    )(normed_cols, cot_one, cot_two, *gathered, *([] if before is None else [before]))


def flip(values, axis, bit):
    count = lax.axis_size(axis)
    return lax.ppermute(values, axis, [(at, at ^ bit) for at in range(count)])


def exchange_small(values, axis):
    return [values] + [flip(values, axis, bit) for bit in range(1, lax.axis_size(axis))]


def gather_xor(values, axis):
    count = lax.axis_size(axis)
    high, low = count // 2, count // 4

    def spread(held):
        bit = low // 2
        while bit >= 1:
            for key in sorted(held):
                held[key | bit] = flip(held[key], axis, bit)
            bit //= 2
        return held

    over_high, over_low = flip(values, axis, high), flip(values, axis, low)
    own = spread({0: values})
    keys = sorted(own)
    spread_own, over_high, over_low = lax.optimization_barrier(
        ([own[key] for key in keys], over_high, over_low)
    )
    even = lax.axis_index(axis) % 2 == 0
    onward = jnp.where(even, over_low, over_high)
    pairs = [(at, at ^ (high if at % 2 == 0 else low)) for at in range(count)]
    far = lax.ppermute(onward, axis, pairs)
    near = dict(zip(keys, spread_own))
    near.update(spread({high: over_high}))
    near.update(spread({low: over_low}))
    return near, spread({high | low: far})


def columns_to_owner(turned, axis):
    count = lax.axis_size(axis)
    parts, part, rows = turned.shape
    cut = turned.reshape(count, parts * part // count, rows)
    return lax.all_to_all(cut, axis, 0, 0, tiled=True)


def shards(patches, dest_group, dest_row, segment, ln_gain, w_qkv, qk_gain, w_out, cotangent):
    group_rows, part_width = patches.shape
    groups = lax.axis_size("dp")
    parts = lax.axis_size("mp")
    slot_size = 2 * group_rows // groups
    slots = groups * slot_size
    full_width, local_width = w_out.shape
    my_group, my_index = lax.axis_index("dp"), lax.axis_index("mp")
    w_t = jnp.transpose(w_qkv, (1, 0, 2))
    w_out_t = w_out[None]

    first_cot, second_cot = turn_halves(cotangent)
    cot_one = lax.all_gather(first_cot, "mp", axis=0, tiled=False)

    position = jnp.arange(group_rows, dtype=jnp.int32)
    earlier = (dest_group[:, None] == dest_group[None, :]) & (position[None, :] < position[:, None])
    rank_within = jnp.sum(earlier.astype(jnp.int32), 1)
    place = dest_group * slot_size + rank_within
    to_slot = jnp.arange(slots, dtype=jnp.int32)[:, None] == place[None, :]
    outbox = dot_f32(to_slot.astype(jnp.bfloat16), patches, (1,), (0,)).astype(jnp.bfloat16)
    inbox = lax.all_to_all(
        outbox.reshape(groups, slot_size, part_width), "dp", split_axis=0, concat_axis=0, tiled=True
    ).reshape(slots, part_width)

    outbox, late_patches = lax.optimization_barrier((outbox, patches))
    wide = late_patches.astype(jnp.float32)
    part_mean = jnp.mean(wide, -1)
    part_dev = jnp.sum(jnp.square(wide - part_mean[:, None]), -1)
    seen = exchange_small(jnp.stack([part_mean, part_dev]), "mp")
    row_mean = sum(entry[0] for entry in seen) / parts
    row_dev = sum(entry[1] + part_width * jnp.square(entry[0] - row_mean) for entry in seen)
    row_rstd = lax.rsqrt(row_dev / full_width + 1e-06)
    notes = jnp.stack([dest_row.astype(jnp.float32) + 1.0, row_mean, row_rstd])
    outnotes = jnp.sum(jnp.where(to_slot[None], notes[:, None, :], 0.0), -1)
    outnotes = outnotes.reshape(3, groups, slot_size)
    came = []
    for bit in range(groups):
        mine = lax.dynamic_index_in_dim(outnotes, my_group ^ bit, 1, keepdims=False)
        came.append(mine if bit == 0 else flip(mine, "dp", bit))
    sender = jnp.arange(groups, dtype=jnp.int32)[None, :, None]
    innotes = sum(
        jnp.where(sender == (my_group ^ bit), entry[:, None, :], 0.0)
        for bit, entry in enumerate(came)
    ).reshape(3, slots)
    arrived_at = innotes[0].astype(jnp.int32) - 1
    at_row = arrived_at[:, None] == position[None, :]
    mean = jnp.sum(jnp.where(at_row, innotes[1][:, None], 0.0), 0, keepdims=True)
    rstd = jnp.sum(jnp.where(at_row, innotes[2][:, None], 0.0), 0, keepdims=True)
    packed = dot_f32(inbox, at_row.astype(jnp.bfloat16), (0,), (0,)).astype(jnp.bfloat16)
    gain_column = ln_gain[:, None]
    my_gain = lax.dynamic_slice_in_dim(gain_column, my_index * part_width, part_width, 0)
    unit_rows = (packed.astype(jnp.float32) - mean) * rstd
    normed_part = (unit_rows * my_gain).astype(jnp.bfloat16)

    normed_part, cot_one = lax.optimization_barrier((normed_part, cot_one))
    normed = lax.all_gather(normed_part, "mp", axis=0, tiled=False)
    d_heads_one = project(cot_one, w_out_t, jnp.bfloat16)
    cot_cols_one = columns_to_owner(cot_one, "dp")
    normed, d_heads_one, cot_cols_one, late_cot = lax.optimization_barrier(
        (normed, d_heads_one, cot_cols_one, second_cot)
    )
    cot_two = lax.all_gather(late_cot, "mp", axis=0, tiled=False)
    projected = project(normed, w_t, jnp.float32)
    normed_cols = columns_to_owner(normed, "dp")

    heads_out = attention(forward_kernel, projected, segment, qk_gain, (), 1)
    attn_part = expand(heads_out, w_out_t, parts, 1)
    attn_part, cot_two = lax.optimization_barrier((attn_part, cot_two))
    attn = lax.psum_scatter(attn_part, "mp", scatter_dimension=0, tiled=False)
    output = (packed.astype(jnp.float32) + attn.astype(jnp.float32)).astype(jnp.bfloat16).T

    d_heads_two = project(cot_two, w_out_t, jnp.bfloat16)
    normed_cols, d_heads_two = lax.optimization_barrier((normed_cols, d_heads_two))
    d_all = attention(backward_kernel, projected, segment, qk_gain, (d_heads_one, d_heads_two), 4)
    d_part, sums = expand(d_all, w_t, parts, 2, gain_column, normed)
    d_normed = lax.psum_scatter(d_part, "mp", scatter_dimension=0, tiled=False)
    sums = sum(exchange_small(sums, "mp")) / full_width
    scale_grad = 1.0 / math.sqrt(group_rows * groups)
    columns = (normed_cols, cot_cols_one, columns_to_owner(cot_two, "dp"))
    sums_near = None
    near, far = gather_xor(d_all, "dp")
    for held, scale in ((near, None), (far, scale_grad)):
        keys = sorted(held)
        sums_near = weight_grads(*columns, [held[key] for key in keys], keys, sums_near, scale)
    d_normed, sums_near = lax.optimization_barrier((d_normed, sums_near))
    qkv_grad, out_grad = sums_near

    d_unit = d_normed.astype(jnp.float32) * my_gain
    d_input = rstd * (d_unit - sums[0:1] - unit_rows * sums[1:2])
    input_grad = (cotangent.astype(jnp.float32) + d_input.T).astype(jnp.bfloat16)
    return (output, input_grad, qkv_grad.transpose(1, 0, 2), out_grad)


def solution(mesh):
    placed = (
        P("dp", "mp"),
        P("dp"),
        P("dp"),
        P("dp"),
        P(),
        P(None, None, "mp"),
        P(),
        P(None, "mp"),
        P("dp", "mp"),
    )
    return jax.shard_map(
        shards,
        mesh=mesh,
        in_specs=placed,
        out_specs=(P("dp", "mp"), P("dp", "mp"), P("dp", None, "mp"), P("dp", "mp")),
        check_vma=False,
    )
```

```python
import functools
import math

import jax
import jax.numpy as jnp
from jax import lax
from jax.experimental import pallas as pl
from jax.experimental.pallas import tpu as pltpu
from jax.sharding import PartitionSpec as P

DH = 128
VMEM_BYTES = 48 * 1024 * 1024
STREAMS = 4


def dot_f32(left, right, left_dims, right_dims):
    return lax.dot_general(
        left, right, ((left_dims, right_dims), ((), ())), preferred_element_type=jnp.float32
    )


def params():
    return pltpu.CompilerParams(vmem_limit_bytes=VMEM_BYTES)


def turn_kernel(x_ref, one_ref, two_ref):
    half = one_ref.shape[1]
    one_ref[...] = x_ref[:half, :].T
    two_ref[...] = x_ref[half:, :].T


def turn_halves(x):
    rows, part = x.shape
    shape = jax.ShapeDtypeStruct((part, rows // 2), x.dtype)
    return pl.pallas_call(
        turn_kernel,
        out_shape=[shape, shape],
        compiler_params=params(),
        cost_estimate=pl.CostEstimate(flops=0, bytes_accessed=4 * rows * part, transcendentals=0),
    )(x)


def project_kernel(steps, width, x_ref, *refs):
    w_refs, (out_ref, total, block) = refs[:STREAMS], refs[STREAMS:]
    at, t = pl.program_id(0), pl.program_id(1)
    columns = pl.ds(pl.multiple_of(t * width, width), width)

    @pl.when(t == 0)
    def _():
        block[...] = x_ref[0].T

    piece = w_refs[0].shape[1]
    term = None
    for order, w_ref in enumerate(w_refs):
        left = block[:, order * piece : (order + 1) * piece]
        more = jnp.dot(left, w_ref[0], preferred_element_type=jnp.float32)
        term = more if term is None else term + more

    @pl.when(at == 0)
    def _():
        total[:, columns] = term

    @pl.when(at > 0)
    def _():
        total[:, columns] += term

    @pl.when(at == steps - 1)
    def _():
        out_ref[:, columns] = total[:, columns].astype(out_ref.dtype)


def project(x, w, dtype):
    steps, part, rows = x.shape
    kinds, depth, width = w.shape
    return pl.pallas_call(
        functools.partial(project_kernel, steps, width),
        grid=(steps, kinds),
        in_specs=[
            pl.BlockSpec((1, part, rows), lambda at, t: (at, 0, 0)),
        ]
        + [
            pl.BlockSpec(
                (1, part // STREAMS, width),
                lambda at, t, order=order: (t, at * STREAMS + order, 0),
            )
            for order in range(STREAMS)
        ],
        out_specs=pl.BlockSpec((rows, kinds * width), lambda at, t: (0, 0)),
        out_shape=jax.ShapeDtypeStruct((rows, kinds * width), dtype),
        scratch_shapes=[
            pltpu.VMEM((rows, kinds * width), jnp.float32),
            pltpu.VMEM((rows, part), jnp.bfloat16),
        ],
        compiler_params=params(),
        cost_estimate=pl.CostEstimate(
            flops=2 * rows * depth * kinds * width,
            bytes_accessed=2 * kinds * depth * width + 2 * rows * depth,
            transcendentals=0,
        ),
    )(x, *[w] * STREAMS)


def expand_kernel(kinds, width, x_ref, *refs):
    w_refs, refs = refs[:STREAMS], refs[STREAMS:]
    pieces = []
    for w_ref in w_refs:
        total = None
        for t in range(kinds):
            term = dot_f32(w_ref[t], x_ref[:, t * width : (t + 1) * width], (1,), (1,))
            total = term if total is None else total + term
        pieces.append(total)
    if len(refs) == 1:
        (out_ref,) = refs
    else:
        gain_ref, normed_ref, out_ref, sums_ref = refs

        @pl.when((pl.program_id(0) == 0) & (pl.program_id(1) == 0))
        def _():
            sums_ref[...] = jnp.zeros_like(sums_ref)

    for order, total in enumerate(pieces):
        here = slice(order * total.shape[0], (order + 1) * total.shape[0])
        out_ref[0, here, :] = total.astype(jnp.bfloat16)
        if len(refs) > 1:
            by_normed = total * normed_ref[0, here, :].astype(jnp.float32)
            sums_ref[0:1, :] += jnp.sum(total * gain_ref[here, :], 0, keepdims=True)
            sums_ref[1:2, :] += jnp.sum(by_normed, 0, keepdims=True)


def expand(x, w, parts, cuts, gain=None, normed=None):
    rows = x.shape[0]
    kinds, depth, width = w.shape
    part = depth // parts
    piece = part // cuts
    turned = pl.BlockSpec((1, piece, rows), lambda at, cut: (at, cut, 0))
    turned_shape = jax.ShapeDtypeStruct((parts, part, rows), jnp.bfloat16)
    more = [] if gain is None else [gain, normed]
    return pl.pallas_call(
        functools.partial(expand_kernel, kinds, width),
        grid=(parts, cuts),
        in_specs=[
            pl.BlockSpec((rows, kinds * width), lambda at, cut: (0, 0)),
        ]
        + [
            pl.BlockSpec(
                (kinds, piece // STREAMS, width),
                lambda at, cut, order=order: (0, (at * cuts + cut) * STREAMS + order, 0),
            )
            for order in range(STREAMS)
        ]
        + ([pl.BlockSpec((piece, 1), lambda at, cut: (at * cuts + cut, 0)), turned] if more else []),
        out_specs=[turned, pl.BlockSpec((2, rows), lambda at, cut: (0, 0))] if more else turned,
        out_shape=[turned_shape, jax.ShapeDtypeStruct((2, rows), jnp.float32)]
        if more
        else turned_shape,
        compiler_params=params(),
        cost_estimate=pl.CostEstimate(
            flops=2 * rows * depth * kinds * width,
            bytes_accessed=2 * kinds * depth * width + 2 * rows * depth,
            transcendentals=0,
        ),
    )(x, *[w] * STREAMS, *more)


def unit_heads(raw):
    center = raw - jnp.mean(raw, -1, keepdims=True)
    rstd = lax.rsqrt(jnp.mean(center * center, -1, keepdims=True) + 1e-06)
    return center * rstd, rstd


def head_forward(proj_ref, same, gain_ref, heads, head):
    width = heads * DH

    def load(kind):
        start = kind * width + head * DH
        return proj_ref[:, start : start + DH]

    q_unit, q_rstd = unit_heads(load(0))
    k_unit, k_rstd = unit_heads(load(1))
    values = load(2).astype(jnp.bfloat16)
    queries = (q_unit * gain_ref[0:1, :]).astype(jnp.bfloat16)
    keys = (k_unit * gain_ref[1:2, :]).astype(jnp.bfloat16)
    scores = dot_f32(queries, keys, (1,), (1,)) * DH ** (-0.5)
    raised = jnp.where(same, jnp.exp(scores), 0.0)
    weights = raised / jnp.sum(raised, -1, keepdims=True)
    return q_unit, q_rstd, k_unit, k_rstd, values, queries, keys, weights


def forward_kernel(heads, proj_ref, row_ref, col_ref, gain_ref, out_ref):
    same = row_ref[...] == col_ref[...]
    for head in range(heads):
        values, _, _, weights = head_forward(proj_ref, same, gain_ref, heads, head)[4:]
        mixed = dot_f32(weights.astype(jnp.bfloat16), values, (1,), (0,))
        out_ref[:, head * DH : (head + 1) * DH] = mixed.astype(jnp.bfloat16)


def unit_backward(grad, unit, rstd, gain):
    scaled = grad.astype(jnp.bfloat16).astype(jnp.float32) * gain
    return rstd * (
        scaled
        - jnp.mean(scaled, -1, keepdims=True)
        - unit * jnp.mean(scaled * unit, -1, keepdims=True)
    )


def backward_kernel(heads, proj_ref, row_ref, col_ref, gain_ref, d_one_ref, d_two_ref, out_ref):
    same = row_ref[...] == col_ref[...]
    width = heads * DH
    for head in range(heads):
        q_unit, q_rstd, k_unit, k_rstd, values, queries, keys, weights = head_forward(
            proj_ref, same, gain_ref, heads, head
        )
        at = head * DH
        weights_bf = weights.astype(jnp.bfloat16)
        d_out = jnp.concatenate([d_one_ref[:, at : at + DH], d_two_ref[:, at : at + DH]], 0)
        d_values = dot_f32(weights_bf, d_out, (0,), (0,))
        out_ref[:, 2 * width + at : 2 * width + at + DH] = d_values.astype(jnp.bfloat16)
        d_weights = dot_f32(d_out, values, (1,), (1,)).astype(jnp.bfloat16).astype(jnp.float32)
        inner = jnp.sum(d_weights * weights, -1, keepdims=True)
        d_scores = (weights * (d_weights - inner) * DH ** (-0.5)).astype(jnp.bfloat16)
        d_queries = unit_backward(
            dot_f32(d_scores, keys, (1,), (0,)), q_unit, q_rstd, gain_ref[0:1, :]
        )
        d_keys = unit_backward(
            dot_f32(d_scores, queries, (0,), (0,)), k_unit, k_rstd, gain_ref[1:2, :]
        )
        out_ref[:, at : at + DH] = d_queries.astype(jnp.bfloat16)
        out_ref[:, width + at : width + at + DH] = d_keys.astype(jnp.bfloat16)


def attention(kernel, projected, segment, qk_gain, extra, kinds):
    rows, wide = projected.shape
    heads = wide // (3 * DH)
    return pl.pallas_call(
        functools.partial(kernel, heads),
        out_shape=jax.ShapeDtypeStruct((rows, kinds * heads * DH), jnp.bfloat16),
        compiler_params=params(),
        cost_estimate=pl.CostEstimate(
            flops=heads * rows * rows * DH * 16,
            bytes_accessed=rows * wide * 8,
            transcendentals=heads * rows * rows,
        ),
    )(projected, segment.reshape(rows, 1), segment.reshape(1, rows), qk_gain, *extra)


def weight_kernel(keys, cuts, scale, more, *refs):
    a_refs, b_refs, refs = refs[:cuts], refs[cuts : cuts + len(keys)], refs[cuts + len(keys) :]
    me = lax.axis_index("dp")
    before_ref = refs[0] if more else None
    out_ref = refs[1] if more else refs[0]
    total = out_ref.at[0] if scale is None else refs[-1]
    for order, key in enumerate(keys):
        left = [ref[me ^ key] for ref in a_refs]
        left = left[0] if cuts == 1 else jnp.concatenate(left, 1)
        term = jnp.dot(left, b_refs[order][...], preferred_element_type=jnp.float32)
        if order == 0:
            total[...] = before_ref[0] + term if more else term
        else:
            total[...] += term
    if scale is not None:
        out_ref[0] = (total[...] * scale).astype(jnp.bfloat16)


def weight_grad(columns, gathered, kinds, before, scale):
    count, depth, _ = columns[0].shape
    keys = sorted(gathered)
    rows, wide = gathered[keys[0]].shape
    width = wide // kinds
    block = pl.BlockSpec((1, depth, width), lambda t: (t, 0, 0))
    more = [] if before is None else [before]
    return pl.pallas_call(
        functools.partial(weight_kernel, keys, len(columns), scale, bool(more)),
        grid=(kinds,),
        in_specs=[pl.BlockSpec(part.shape, lambda t: (0, 0, 0)) for part in columns]
        + [pl.BlockSpec((rows, width), lambda t: (0, t))] * len(keys)
        + [block] * len(more),
        out_specs=block,
        out_shape=jax.ShapeDtypeStruct(
            (kinds, depth, width), jnp.float32 if scale is None else jnp.bfloat16
        ),
        scratch_shapes=[] if scale is None else [pltpu.VMEM((depth, width), jnp.float32)],
        compiler_params=params(),
        cost_estimate=pl.CostEstimate(
            flops=2 * len(keys) * depth * rows * wide,
            bytes_accessed=2 * count * depth * rows + 2 * len(keys) * rows * wide,
            transcendentals=0,
        ),
    )(*columns, *[gathered[key] for key in keys], *more)


def flip(values, axis, bit):
    count = lax.axis_size(axis)
    return lax.ppermute(values, axis, [(at, at ^ bit) for at in range(count)])


def exchange_small(values, axis):
    return [values] + [flip(values, axis, bit) for bit in range(1, lax.axis_size(axis))]


def gather_xor(values, axis):
    count = lax.axis_size(axis)
    high, low = count // 2, count // 4

    def spread(held):
        bit = low // 2
        while bit >= 1:
            for key in sorted(held):
                held[key | bit] = flip(held[key], axis, bit)
            bit //= 2
        return held

    over_high, over_low = flip(values, axis, high), flip(values, axis, low)
    own = spread({0: values})
    keys = sorted(own)
    spread_own, over_high, over_low = lax.optimization_barrier(
        ([own[key] for key in keys], over_high, over_low)
    )
    even = lax.axis_index(axis) % 2 == 0
    onward = jnp.where(even, over_low, over_high)
    pairs = [(at, at ^ (high if at % 2 == 0 else low)) for at in range(count)]
    far = lax.ppermute(onward, axis, pairs)
    near = dict(zip(keys, spread_own))
    near.update(spread({high: over_high}))
    near.update(spread({low: over_low}))
    return near, spread({high | low: far})


def columns_to_owner(turned, axis):
    count = lax.axis_size(axis)
    parts, part, rows = turned.shape
    cut = turned.reshape(count, parts * part // count, rows)
    return lax.all_to_all(cut, axis, 0, 0, tiled=True)


def shards(patches, dest_group, dest_row, segment, ln_gain, w_qkv, qk_gain, w_out, cotangent):
    group_rows, part_width = patches.shape
    groups = lax.axis_size("dp")
    parts = lax.axis_size("mp")
    slot_size = 2 * group_rows // groups
    slots = groups * slot_size
    full_width, local_width = w_out.shape
    my_group, my_index = lax.axis_index("dp"), lax.axis_index("mp")
    w_t = jnp.transpose(w_qkv, (1, 0, 2))
    w_out_t = w_out[None]

    first_cot, second_cot = turn_halves(cotangent)
    cot_one = lax.all_gather(first_cot, "mp", axis=0, tiled=False)

    position = jnp.arange(group_rows, dtype=jnp.int32)
    earlier = (dest_group[:, None] == dest_group[None, :]) & (position[None, :] < position[:, None])
    rank_within = jnp.sum(earlier.astype(jnp.int32), 1)
    place = dest_group * slot_size + rank_within
    to_slot = jnp.arange(slots, dtype=jnp.int32)[:, None] == place[None, :]
    outbox = dot_f32(to_slot.astype(jnp.bfloat16), patches, (1,), (0,)).astype(jnp.bfloat16)
    inbox = lax.all_to_all(
        outbox.reshape(groups, slot_size, part_width), "dp", split_axis=0, concat_axis=0, tiled=True
    ).reshape(slots, part_width)

    outbox, late_patches = lax.optimization_barrier((outbox, patches))
    wide = late_patches.astype(jnp.float32)
    part_mean = jnp.mean(wide, -1)
    part_dev = jnp.sum(jnp.square(wide - part_mean[:, None]), -1)
    seen = exchange_small(jnp.stack([part_mean, part_dev]), "mp")
    row_mean = sum(entry[0] for entry in seen) / parts
    row_dev = sum(entry[1] + part_width * jnp.square(entry[0] - row_mean) for entry in seen)
    row_rstd = lax.rsqrt(row_dev / full_width + 1e-06)
    notes = jnp.stack([dest_row.astype(jnp.float32) + 1.0, row_mean, row_rstd])
    outnotes = jnp.sum(jnp.where(to_slot[None], notes[:, None, :], 0.0), -1)
    outnotes = outnotes.reshape(3, groups, slot_size)
    came = []
    for bit in range(groups):
        mine = lax.dynamic_index_in_dim(outnotes, my_group ^ bit, 1, keepdims=False)
        came.append(mine if bit == 0 else flip(mine, "dp", bit))
    sender = jnp.arange(groups, dtype=jnp.int32)[None, :, None]
    innotes = sum(
        jnp.where(sender == (my_group ^ bit), entry[:, None, :], 0.0)
        for bit, entry in enumerate(came)
    ).reshape(3, slots)
    arrived_at = innotes[0].astype(jnp.int32) - 1
    at_row = arrived_at[:, None] == position[None, :]
    mean = jnp.sum(jnp.where(at_row, innotes[1][:, None], 0.0), 0, keepdims=True)
    rstd = jnp.sum(jnp.where(at_row, innotes[2][:, None], 0.0), 0, keepdims=True)
    packed = dot_f32(inbox, at_row.astype(jnp.bfloat16), (0,), (0,)).astype(jnp.bfloat16)
    gain_column = ln_gain[:, None]
    my_gain = lax.dynamic_slice_in_dim(gain_column, my_index * part_width, part_width, 0)
    unit_rows = (packed.astype(jnp.float32) - mean) * rstd
    normed_part = (unit_rows * my_gain).astype(jnp.bfloat16)

    normed_part, cot_one = lax.optimization_barrier((normed_part, cot_one))
    normed = lax.all_gather(normed_part, "mp", axis=0, tiled=False)
    d_heads_one = project(cot_one, w_out_t, jnp.bfloat16)
    cot_cols_one = columns_to_owner(cot_one, "dp")
    normed, d_heads_one, cot_cols_one, late_cot = lax.optimization_barrier(
        (normed, d_heads_one, cot_cols_one, second_cot)
    )
    cot_two = lax.all_gather(late_cot, "mp", axis=0, tiled=False)
    projected = project(normed, w_t, jnp.float32)
    normed_cols = columns_to_owner(normed, "dp")

    heads_out = attention(forward_kernel, projected, segment, qk_gain, (), 1)
    heads_near, heads_far = gather_xor(heads_out, "dp")
    heads_here, normed_cols = lax.optimization_barrier((heads_out, normed_cols))
    attn_part = expand(heads_here, w_out_t, parts, 1)
    attn_part, cot_two = lax.optimization_barrier((attn_part, cot_two))
    attn = lax.psum_scatter(attn_part, "mp", scatter_dimension=0, tiled=False)
    output = (packed.astype(jnp.float32) + attn.astype(jnp.float32)).astype(jnp.bfloat16).T

    d_heads_two = project(cot_two, w_out_t, jnp.bfloat16)
    d_heads_two, heads_near = lax.optimization_barrier((d_heads_two, heads_near))
    d_all = attention(backward_kernel, projected, segment, qk_gain, (d_heads_one, d_heads_two), 3)
    d_part, sums = expand(d_all, w_t, parts, 2, gain_column, normed)
    d_normed = lax.psum_scatter(d_part, "mp", scatter_dimension=0, tiled=False)
    sums = sum(exchange_small(sums, "mp")) / full_width
    scale_grad = 1.0 / math.sqrt(group_rows * groups)
    cot_cols_two = columns_to_owner(cot_two, "dp")
    out_grad = weight_grad((cot_cols_one, cot_cols_two), heads_near | heads_far, 1, None, scale_grad)
    near, far = gather_xor(d_all, "dp")
    qkv_near = weight_grad((normed_cols,), near, 3, None, None)
    qkv_grad = weight_grad((normed_cols,), far, 3, qkv_near, scale_grad)
    d_normed, qkv_grad, out_grad = lax.optimization_barrier((d_normed, qkv_grad, out_grad))

    d_unit = d_normed.astype(jnp.float32) * my_gain
    d_input = rstd * (d_unit - sums[0:1] - unit_rows * sums[1:2])
    input_grad = (cotangent.astype(jnp.float32) + d_input.T).astype(jnp.bfloat16)
    return (output, input_grad, qkv_grad.transpose(1, 0, 2), out_grad[0])


def solution(mesh):
    placed = (
        P("dp", "mp"),
        P("dp"),
        P("dp"),
        P("dp"),
        P(),
        P(None, None, "mp"),
        P(),
        P(None, "mp"),
        P("dp", "mp"),
    )
    return jax.shard_map(
        shards,
        mesh=mesh,
        in_specs=placed,
        out_specs=(P("dp", "mp"), P("dp", "mp"), P("dp", None, "mp"), P("dp", "mp")),
        check_vma=False,
    )
```

```python
import functools
import math

import jax
import jax.numpy as jnp
from jax import lax
from jax.experimental import pallas as pl
from jax.experimental.pallas import tpu as pltpu
from jax.sharding import PartitionSpec as P

DH = 128
VMEM_BYTES = 48 * 1024 * 1024
STREAMS = 1


def dot_f32(left, right, left_dims, right_dims):
    return lax.dot_general(
        left, right, ((left_dims, right_dims), ((), ())), preferred_element_type=jnp.float32
    )


def params():
    return pltpu.CompilerParams(vmem_limit_bytes=VMEM_BYTES)


def turn_kernel(x_ref, one_ref, two_ref):
    half = one_ref.shape[1]
    one_ref[...] = x_ref[:half, :].T
    two_ref[...] = x_ref[half:, :].T


def turn_halves(x):
    rows, part = x.shape
    shape = jax.ShapeDtypeStruct((part, rows // 2), x.dtype)
    return pl.pallas_call(
        turn_kernel,
        out_shape=[shape, shape],
        compiler_params=params(),
        cost_estimate=pl.CostEstimate(flops=0, bytes_accessed=4 * rows * part, transcendentals=0),
    )(x)


def project_kernel(steps, width, x_ref, *refs):
    w_refs, (out_ref, total, block) = refs[:STREAMS], refs[STREAMS:]
    at, t = pl.program_id(0), pl.program_id(1)
    columns = pl.ds(pl.multiple_of(t * width, width), width)

    @pl.when(t == 0)
    def _():
        block[...] = x_ref[0].T

    piece = w_refs[0].shape[1]
    term = None
    for order, w_ref in enumerate(w_refs):
        left = block[:, order * piece : (order + 1) * piece]
        more = jnp.dot(left, w_ref[0], preferred_element_type=jnp.float32)
        term = more if term is None else term + more

    @pl.when(at == 0)
    def _():
        total[:, columns] = term

    @pl.when(at > 0)
    def _():
        total[:, columns] += term

    @pl.when(at == steps - 1)
    def _():
        out_ref[:, columns] = total[:, columns].astype(out_ref.dtype)


def project(x, w, dtype):
    steps, part, rows = x.shape
    kinds, depth, width = w.shape
    return pl.pallas_call(
        functools.partial(project_kernel, steps, width),
        grid=(steps, kinds),
        in_specs=[
            pl.BlockSpec((1, part, rows), lambda at, t: (at, 0, 0)),
        ]
        + [
            pl.BlockSpec(
                (1, part // STREAMS, width),
                lambda at, t, order=order: (t, at * STREAMS + order, 0),
            )
            for order in range(STREAMS)
        ],
        out_specs=pl.BlockSpec((rows, kinds * width), lambda at, t: (0, 0)),
        out_shape=jax.ShapeDtypeStruct((rows, kinds * width), dtype),
        scratch_shapes=[
            pltpu.VMEM((rows, kinds * width), jnp.float32),
            pltpu.VMEM((rows, part), jnp.bfloat16),
        ],
        compiler_params=params(),
        cost_estimate=pl.CostEstimate(
            flops=2 * rows * depth * kinds * width,
            bytes_accessed=2 * kinds * depth * width + 2 * rows * depth,
            transcendentals=0,
        ),
    )(x, *[w] * STREAMS)


def expand_kernel(kinds, width, x_ref, *refs):
    w_refs, refs = refs[:STREAMS], refs[STREAMS:]
    pieces = []
    for w_ref in w_refs:
        total = None
        for t in range(kinds):
            term = dot_f32(w_ref[t], x_ref[:, t * width : (t + 1) * width], (1,), (1,))
            total = term if total is None else total + term
        pieces.append(total)
    if len(refs) == 1:
        (out_ref,) = refs
    else:
        gain_ref, normed_ref, out_ref, sums_ref = refs

        @pl.when((pl.program_id(0) == 0) & (pl.program_id(1) == 0))
        def _():
            sums_ref[...] = jnp.zeros_like(sums_ref)

    for order, total in enumerate(pieces):
        here = slice(order * total.shape[0], (order + 1) * total.shape[0])
        out_ref[0, here, :] = total.astype(jnp.bfloat16)
        if len(refs) > 1:
            by_normed = total * normed_ref[0, here, :].astype(jnp.float32)
            sums_ref[0:1, :] += jnp.sum(total * gain_ref[here, :], 0, keepdims=True)
            sums_ref[1:2, :] += jnp.sum(by_normed, 0, keepdims=True)


def expand(x, w, parts, cuts, gain=None, normed=None):
    rows = x.shape[0]
    kinds, depth, width = w.shape
    part = depth // parts
    piece = part // cuts
    turned = pl.BlockSpec((1, piece, rows), lambda at, cut: (at, cut, 0))
    turned_shape = jax.ShapeDtypeStruct((parts, part, rows), jnp.bfloat16)
    more = [] if gain is None else [gain, normed]
    return pl.pallas_call(
        functools.partial(expand_kernel, kinds, width),
        grid=(parts, cuts),
        in_specs=[
            pl.BlockSpec((rows, kinds * width), lambda at, cut: (0, 0)),
        ]
        + [
            pl.BlockSpec(
                (kinds, piece // STREAMS, width),
                lambda at, cut, order=order: (0, (at * cuts + cut) * STREAMS + order, 0),
            )
            for order in range(STREAMS)
        ]
        + ([pl.BlockSpec((piece, 1), lambda at, cut: (at * cuts + cut, 0)), turned] if more else []),
        out_specs=[turned, pl.BlockSpec((2, rows), lambda at, cut: (0, 0))] if more else turned,
        out_shape=[turned_shape, jax.ShapeDtypeStruct((2, rows), jnp.float32)]
        if more
        else turned_shape,
        compiler_params=params(),
        cost_estimate=pl.CostEstimate(
            flops=2 * rows * depth * kinds * width,
            bytes_accessed=2 * kinds * depth * width + 2 * rows * depth,
            transcendentals=0,
        ),
    )(x, *[w] * STREAMS, *more)


def unit_heads(raw):
    center = raw - jnp.mean(raw, -1, keepdims=True)
    rstd = lax.rsqrt(jnp.mean(center * center, -1, keepdims=True) + 1e-06)
    return center * rstd, rstd


def head_forward(proj_ref, same, gain_ref, heads, head):
    width = heads * DH

    def load(kind):
        start = kind * width + head * DH
        return proj_ref[:, start : start + DH]

    q_unit, q_rstd = unit_heads(load(0))
    k_unit, k_rstd = unit_heads(load(1))
    values = load(2).astype(jnp.bfloat16)
    queries = (q_unit * gain_ref[0:1, :]).astype(jnp.bfloat16)
    keys = (k_unit * gain_ref[1:2, :]).astype(jnp.bfloat16)
    scores = dot_f32(queries, keys, (1,), (1,)) * DH ** (-0.5)
    raised = jnp.where(same, jnp.exp(scores), 0.0)
    weights = raised / jnp.sum(raised, -1, keepdims=True)
    return q_unit, q_rstd, k_unit, k_rstd, values, queries, keys, weights


def forward_kernel(heads, proj_ref, row_ref, col_ref, gain_ref, out_ref):
    same = row_ref[...] == col_ref[...]
    for head in range(heads):
        values, _, _, weights = head_forward(proj_ref, same, gain_ref, heads, head)[4:]
        mixed = dot_f32(weights.astype(jnp.bfloat16), values, (1,), (0,))
        out_ref[:, head * DH : (head + 1) * DH] = mixed.astype(jnp.bfloat16)


def unit_backward(grad, unit, rstd, gain):
    scaled = grad.astype(jnp.bfloat16).astype(jnp.float32) * gain
    return rstd * (
        scaled
        - jnp.mean(scaled, -1, keepdims=True)
        - unit * jnp.mean(scaled * unit, -1, keepdims=True)
    )


def backward_kernel(heads, proj_ref, row_ref, col_ref, gain_ref, d_one_ref, d_two_ref, out_ref):
    same = row_ref[...] == col_ref[...]
    width = heads * DH
    for head in range(heads):
        q_unit, q_rstd, k_unit, k_rstd, values, queries, keys, weights = head_forward(
            proj_ref, same, gain_ref, heads, head
        )
        at = head * DH
        weights_bf = weights.astype(jnp.bfloat16)
        d_out = jnp.concatenate([d_one_ref[:, at : at + DH], d_two_ref[:, at : at + DH]], 0)
        d_values = dot_f32(weights_bf, d_out, (0,), (0,))
        out_ref[:, 2 * width + at : 2 * width + at + DH] = d_values.astype(jnp.bfloat16)
        d_weights = dot_f32(d_out, values, (1,), (1,)).astype(jnp.bfloat16).astype(jnp.float32)
        inner = jnp.sum(d_weights * weights, -1, keepdims=True)
        d_scores = (weights * (d_weights - inner) * DH ** (-0.5)).astype(jnp.bfloat16)
        d_queries = unit_backward(
            dot_f32(d_scores, keys, (1,), (0,)), q_unit, q_rstd, gain_ref[0:1, :]
        )
        d_keys = unit_backward(
            dot_f32(d_scores, queries, (0,), (0,)), k_unit, k_rstd, gain_ref[1:2, :]
        )
        out_ref[:, at : at + DH] = d_queries.astype(jnp.bfloat16)
        out_ref[:, width + at : width + at + DH] = d_keys.astype(jnp.bfloat16)


def attention(kernel, projected, segment, qk_gain, extra, kinds):
    rows, wide = projected.shape
    heads = wide // (3 * DH)
    return pl.pallas_call(
        functools.partial(kernel, heads),
        out_shape=jax.ShapeDtypeStruct((rows, kinds * heads * DH), jnp.bfloat16),
        compiler_params=params(),
        cost_estimate=pl.CostEstimate(
            flops=heads * rows * rows * DH * 16,
            bytes_accessed=rows * wide * 8,
            transcendentals=heads * rows * rows,
        ),
    )(projected, segment.reshape(rows, 1), segment.reshape(1, rows), qk_gain, *extra)


def weight_kernel(keys, cuts, scale, more, *refs):
    a_refs, b_refs, refs = refs[:cuts], refs[cuts : cuts + len(keys)], refs[cuts + len(keys) :]
    me = lax.axis_index("dp")
    before_ref = refs[0] if more else None
    out_ref = refs[1] if more else refs[0]
    total = out_ref.at[0] if scale is None else refs[-1]
    for order, key in enumerate(keys):
        left = [ref[me ^ key] for ref in a_refs]
        left = left[0] if cuts == 1 else jnp.concatenate(left, 1)
        term = jnp.dot(left, b_refs[order][...], preferred_element_type=jnp.float32)
        if order == 0:
            total[...] = before_ref[0] + term if more else term
        else:
            total[...] += term
    if scale is not None:
        out_ref[0] = (total[...] * scale).astype(jnp.bfloat16)


def weight_grad(columns, gathered, kinds, before, scale):
    count, depth, _ = columns[0].shape
    keys = sorted(gathered)
    rows, wide = gathered[keys[0]].shape
    width = wide // kinds
    block = pl.BlockSpec((1, depth, width), lambda t: (t, 0, 0))
    more = [] if before is None else [before]
    return pl.pallas_call(
        functools.partial(weight_kernel, keys, len(columns), scale, bool(more)),
        grid=(kinds,),
        in_specs=[pl.BlockSpec(part.shape, lambda t: (0, 0, 0)) for part in columns]
        + [pl.BlockSpec((rows, width), lambda t: (0, t))] * len(keys)
        + [block] * len(more),
        out_specs=block,
        out_shape=jax.ShapeDtypeStruct(
            (kinds, depth, width), jnp.float32 if scale is None else jnp.bfloat16
        ),
        scratch_shapes=[] if scale is None else [pltpu.VMEM((depth, width), jnp.float32)],
        compiler_params=params(),
        cost_estimate=pl.CostEstimate(
            flops=2 * len(keys) * depth * rows * wide,
            bytes_accessed=2 * count * depth * rows + 2 * len(keys) * rows * wide,
            transcendentals=0,
        ),
    )(*columns, *[gathered[key] for key in keys], *more)


def flip(values, axis, bit):
    count = lax.axis_size(axis)
    return lax.ppermute(values, axis, [(at, at ^ bit) for at in range(count)])


def exchange_small(values, axis):
    return [values] + [flip(values, axis, bit) for bit in range(1, lax.axis_size(axis))]


def gather_xor(values, axis):
    count = lax.axis_size(axis)
    high, low = count // 2, count // 4

    def spread(held):
        bit = low // 2
        while bit >= 1:
            for key in sorted(held):
                held[key | bit] = flip(held[key], axis, bit)
            bit //= 2
        return held

    over_high, over_low = flip(values, axis, high), flip(values, axis, low)
    own = spread({0: values})
    keys = sorted(own)
    spread_own, over_high, over_low = lax.optimization_barrier(
        ([own[key] for key in keys], over_high, over_low)
    )
    even = lax.axis_index(axis) % 2 == 0
    onward = jnp.where(even, over_low, over_high)
    pairs = [(at, at ^ (high if at % 2 == 0 else low)) for at in range(count)]
    far = lax.ppermute(onward, axis, pairs)
    near = dict(zip(keys, spread_own))
    near.update(spread({high: over_high}))
    near.update(spread({low: over_low}))
    return near, spread({high | low: far})


def columns_to_owner(turned, axis):
    count = lax.axis_size(axis)
    parts, part, rows = turned.shape
    cut = turned.reshape(count, parts * part // count, rows)
    return lax.all_to_all(cut, axis, 0, 0, tiled=True)


def shards(patches, dest_group, dest_row, segment, ln_gain, w_qkv, qk_gain, w_out, cotangent):
    group_rows, part_width = patches.shape
    groups = lax.axis_size("dp")
    parts = lax.axis_size("mp")
    slot_size = 2 * group_rows // groups
    slots = groups * slot_size
    full_width, local_width = w_out.shape
    my_group, my_index = lax.axis_index("dp"), lax.axis_index("mp")
    w_t = jnp.transpose(w_qkv, (1, 0, 2))
    w_out_t = w_out[None]

    first_cot, second_cot = turn_halves(cotangent)
    cot_one = lax.all_gather(first_cot, "mp", axis=0, tiled=False)

    position = jnp.arange(group_rows, dtype=jnp.int32)
    earlier = (dest_group[:, None] == dest_group[None, :]) & (position[None, :] < position[:, None])
    rank_within = jnp.sum(earlier.astype(jnp.int32), 1)
    place = dest_group * slot_size + rank_within
    to_slot = jnp.arange(slots, dtype=jnp.int32)[:, None] == place[None, :]
    outbox = dot_f32(to_slot.astype(jnp.bfloat16), patches, (1,), (0,)).astype(jnp.bfloat16)
    inbox = lax.all_to_all(
        outbox.reshape(groups, slot_size, part_width), "dp", split_axis=0, concat_axis=0, tiled=True
    ).reshape(slots, part_width)

    outbox, late_patches = lax.optimization_barrier((outbox, patches))
    wide = late_patches.astype(jnp.float32)
    part_mean = jnp.mean(wide, -1)
    part_dev = jnp.sum(jnp.square(wide - part_mean[:, None]), -1)
    seen = exchange_small(jnp.stack([part_mean, part_dev]), "mp")
    row_mean = sum(entry[0] for entry in seen) / parts
    row_dev = sum(entry[1] + part_width * jnp.square(entry[0] - row_mean) for entry in seen)
    row_rstd = lax.rsqrt(row_dev / full_width + 1e-06)
    notes = jnp.stack([dest_row.astype(jnp.float32) + 1.0, row_mean, row_rstd])
    outnotes = jnp.sum(jnp.where(to_slot[None], notes[:, None, :], 0.0), -1)
    outnotes = outnotes.reshape(3, groups, slot_size)
    came = []
    for bit in range(groups):
        mine = lax.dynamic_index_in_dim(outnotes, my_group ^ bit, 1, keepdims=False)
        came.append(mine if bit == 0 else flip(mine, "dp", bit))
    sender = jnp.arange(groups, dtype=jnp.int32)[None, :, None]
    innotes = sum(
        jnp.where(sender == (my_group ^ bit), entry[:, None, :], 0.0)
        for bit, entry in enumerate(came)
    ).reshape(3, slots)
    arrived_at = innotes[0].astype(jnp.int32) - 1
    at_row = arrived_at[:, None] == position[None, :]
    mean = jnp.sum(jnp.where(at_row, innotes[1][:, None], 0.0), 0, keepdims=True)
    rstd = jnp.sum(jnp.where(at_row, innotes[2][:, None], 0.0), 0, keepdims=True)
    packed = dot_f32(inbox, at_row.astype(jnp.bfloat16), (0,), (0,)).astype(jnp.bfloat16)
    gain_column = ln_gain[:, None]
    my_gain = lax.dynamic_slice_in_dim(gain_column, my_index * part_width, part_width, 0)
    unit_rows = (packed.astype(jnp.float32) - mean) * rstd
    normed_part = (unit_rows * my_gain).astype(jnp.bfloat16)

    normed_part, cot_one = lax.optimization_barrier((normed_part, cot_one))
    normed = lax.all_gather(normed_part, "mp", axis=0, tiled=False)
    d_heads_one = project(cot_one, w_out_t, jnp.bfloat16)
    cot_cols_one = columns_to_owner(cot_one, "dp")
    normed, d_heads_one, cot_cols_one, late_cot = lax.optimization_barrier(
        (normed, d_heads_one, cot_cols_one, second_cot)
    )
    cot_two = lax.all_gather(late_cot, "mp", axis=0, tiled=False)
    projected = project(normed, w_t, jnp.float32)
    normed_cols = columns_to_owner(normed, "dp")

    heads_out = attention(forward_kernel, projected, segment, qk_gain, (), 1)
    late_heads, normed_cols = lax.optimization_barrier((heads_out, normed_cols))
    heads_near, heads_far = gather_xor(late_heads, "dp")
    attn_part = expand(heads_out, w_out_t, parts, 1)
    attn_part, cot_two = lax.optimization_barrier((attn_part, cot_two))
    attn = lax.psum_scatter(attn_part, "mp", scatter_dimension=0, tiled=False)
    output = (packed.astype(jnp.float32) + attn.astype(jnp.float32)).astype(jnp.bfloat16).T

    d_heads_two = project(cot_two, w_out_t, jnp.bfloat16)
    d_heads_two, heads_near = lax.optimization_barrier((d_heads_two, heads_near))
    d_all = attention(backward_kernel, projected, segment, qk_gain, (d_heads_one, d_heads_two), 3)
    d_part, sums = expand(d_all, w_t, parts, 2, gain_column, normed)
    d_normed = lax.psum_scatter(d_part, "mp", scatter_dimension=0, tiled=False)
    sums = sum(exchange_small(sums, "mp")) / full_width
    scale_grad = 1.0 / math.sqrt(group_rows * groups)
    cot_cols_two = columns_to_owner(cot_two, "dp")
    out_grad = weight_grad((cot_cols_one, cot_cols_two), heads_near | heads_far, 1, None, scale_grad)
    near, far = gather_xor(d_all, "dp")
    qkv_near = weight_grad((normed_cols,), near, 3, None, None)
    qkv_grad = weight_grad((normed_cols,), far, 3, qkv_near, scale_grad)
    d_normed, qkv_grad, out_grad = lax.optimization_barrier((d_normed, qkv_grad, out_grad))

    d_unit = d_normed.astype(jnp.float32) * my_gain
    d_input = rstd * (d_unit - sums[0:1] - unit_rows * sums[1:2])
    input_grad = (cotangent.astype(jnp.float32) + d_input.T).astype(jnp.bfloat16)
    return (output, input_grad, qkv_grad.transpose(1, 0, 2), out_grad[0])


def solution(mesh):
    placed = (
        P("dp", "mp"),
        P("dp"),
        P("dp"),
        P("dp"),
        P(),
        P(None, None, "mp"),
        P(),
        P(None, "mp"),
        P("dp", "mp"),
    )
    return jax.shard_map(
        shards,
        mesh=mesh,
        in_specs=placed,
        out_specs=(P("dp", "mp"), P("dp", "mp"), P("dp", None, "mp"), P("dp", "mp")),
        check_vma=False,
    )
```

```python
import functools
import math

import jax
import jax.numpy as jnp
from jax import lax
from jax.experimental import pallas as pl
from jax.experimental.pallas import tpu as pltpu
from jax.sharding import PartitionSpec as P

DH = 128
VMEM_BYTES = 48 * 1024 * 1024


def dot_f32(left, right, left_dims, right_dims):
    return lax.dot_general(
        left, right, ((left_dims, right_dims), ((), ())), preferred_element_type=jnp.float32
    )


def params():
    return pltpu.CompilerParams(vmem_limit_bytes=VMEM_BYTES)


def turn_kernel(x_ref, one_ref, two_ref):
    half = one_ref.shape[1]
    one_ref[...] = x_ref[:half, :].T
    two_ref[...] = x_ref[half:, :].T


def turn_halves(x):
    rows, part = x.shape
    shape = jax.ShapeDtypeStruct((part, rows // 2), x.dtype)
    return pl.pallas_call(
        turn_kernel,
        out_shape=[shape, shape],
        compiler_params=params(),
        cost_estimate=pl.CostEstimate(flops=0, bytes_accessed=4 * rows * part, transcendentals=0),
    )(x)


def project_kernel(steps, width, x_ref, w_ref, out_ref, total, block):
    at, t = pl.program_id(0), pl.program_id(1)
    columns = pl.ds(pl.multiple_of(t * width, width), width)

    @pl.when(t == 0)
    def _():
        block[...] = x_ref[0].T

    term = jnp.dot(block[...], w_ref[0], preferred_element_type=jnp.float32)

    @pl.when(at == 0)
    def _():
        total[:, columns] = term

    @pl.when(at > 0)
    def _():
        total[:, columns] += term

    @pl.when(at == steps - 1)
    def _():
        out_ref[:, columns] = total[:, columns].astype(out_ref.dtype)


def project(x, w, dtype):
    steps, part, rows = x.shape
    kinds, depth, width = w.shape
    return pl.pallas_call(
        functools.partial(project_kernel, steps, width),
        grid=(steps, kinds),
        in_specs=[
            pl.BlockSpec((1, part, rows), lambda at, t: (at, 0, 0)),
            pl.BlockSpec((1, part, width), lambda at, t: (t, at, 0)),
        ],
        out_specs=pl.BlockSpec((rows, kinds * width), lambda at, t: (0, 0)),
        out_shape=jax.ShapeDtypeStruct((rows, kinds * width), dtype),
        scratch_shapes=[
            pltpu.VMEM((rows, kinds * width), jnp.float32),
            pltpu.VMEM((rows, part), jnp.bfloat16),
        ],
        compiler_params=params(),
        cost_estimate=pl.CostEstimate(
            flops=2 * rows * depth * kinds * width,
            bytes_accessed=2 * kinds * depth * width + 2 * rows * depth,
            transcendentals=0,
        ),
    )(x, w)


def expand_kernel(kinds, width, x_ref, w_ref, *refs):
    total = None
    for t in range(kinds):
        term = dot_f32(w_ref[t], x_ref[:, t * width : (t + 1) * width], (1,), (1,))
        total = term if total is None else total + term
    if len(refs) == 1:
        (out_ref,) = refs
    else:
        gain_ref, normed_ref, out_ref, sums_ref = refs

        @pl.when((pl.program_id(0) == 0) & (pl.program_id(1) == 0))
        def _():
            sums_ref[...] = jnp.zeros_like(sums_ref)

        sums_ref[0:1, :] += jnp.sum(total * gain_ref[...], 0, keepdims=True)
        sums_ref[1:2, :] += jnp.sum(total * normed_ref[0].astype(jnp.float32), 0, keepdims=True)
    out_ref[0] = total.astype(jnp.bfloat16)


def expand(x, w, parts, cuts, gain=None, normed=None):
    rows = x.shape[0]
    kinds, depth, width = w.shape
    part = depth // parts
    piece = part // cuts
    turned = pl.BlockSpec((1, piece, rows), lambda at, cut: (at, cut, 0))
    turned_shape = jax.ShapeDtypeStruct((parts, part, rows), jnp.bfloat16)
    more = [] if gain is None else [gain, normed]
    return pl.pallas_call(
        functools.partial(expand_kernel, kinds, width),
        grid=(parts, cuts),
        in_specs=[
            pl.BlockSpec((rows, kinds * width), lambda at, cut: (0, 0)),
            pl.BlockSpec((kinds, piece, width), lambda at, cut: (0, at * cuts + cut, 0)),
        ]
        + ([pl.BlockSpec((piece, 1), lambda at, cut: (at * cuts + cut, 0)), turned] if more else []),
        out_specs=[turned, pl.BlockSpec((2, rows), lambda at, cut: (0, 0))] if more else turned,
        out_shape=[turned_shape, jax.ShapeDtypeStruct((2, rows), jnp.float32)]
        if more
        else turned_shape,
        compiler_params=params(),
        cost_estimate=pl.CostEstimate(
            flops=2 * rows * depth * kinds * width,
            bytes_accessed=2 * kinds * depth * width + 2 * rows * depth,
            transcendentals=0,
        ),
    )(x, w, *more)


def unit_heads(raw):
    center = raw - jnp.mean(raw, -1, keepdims=True)
    rstd = lax.rsqrt(jnp.mean(center * center, -1, keepdims=True) + 1e-06)
    return center * rstd, rstd


def head_forward(proj_ref, same, gain_ref, heads, head):
    width = heads * DH

    def load(kind):
        start = kind * width + head * DH
        return proj_ref[:, start : start + DH]

    q_unit, q_rstd = unit_heads(load(0))
    k_unit, k_rstd = unit_heads(load(1))
    values = load(2).astype(jnp.bfloat16)
    queries = (q_unit * gain_ref[0:1, :]).astype(jnp.bfloat16)
    keys = (k_unit * gain_ref[1:2, :]).astype(jnp.bfloat16)
    scores = dot_f32(queries, keys, (1,), (1,)) * DH ** (-0.5)
    raised = jnp.where(same, jnp.exp(scores), 0.0)
    weights = raised / jnp.sum(raised, -1, keepdims=True)
    return q_unit, q_rstd, k_unit, k_rstd, values, queries, keys, weights


def forward_kernel(heads, proj_ref, row_ref, col_ref, gain_ref, out_ref):
    same = row_ref[...] == col_ref[...]
    for head in range(heads):
        values, _, _, weights = head_forward(proj_ref, same, gain_ref, heads, head)[4:]
        mixed = dot_f32(weights.astype(jnp.bfloat16), values, (1,), (0,))
        out_ref[:, head * DH : (head + 1) * DH] = mixed.astype(jnp.bfloat16)


def unit_backward(grad, unit, rstd, gain):
    scaled = grad.astype(jnp.bfloat16).astype(jnp.float32) * gain
    return rstd * (
        scaled
        - jnp.mean(scaled, -1, keepdims=True)
        - unit * jnp.mean(scaled * unit, -1, keepdims=True)
    )


def backward_kernel(heads, proj_ref, row_ref, col_ref, gain_ref, d_one_ref, d_two_ref, out_ref):
    same = row_ref[...] == col_ref[...]
    width = heads * DH
    for head in range(heads):
        q_unit, q_rstd, k_unit, k_rstd, values, queries, keys, weights = head_forward(
            proj_ref, same, gain_ref, heads, head
        )
        at = head * DH
        weights_bf = weights.astype(jnp.bfloat16)
        d_out = jnp.concatenate([d_one_ref[:, at : at + DH], d_two_ref[:, at : at + DH]], 0)
        mixed = dot_f32(weights_bf, values, (1,), (0,))
        out_ref[:, 3 * width + at : 3 * width + at + DH] = mixed.astype(jnp.bfloat16)
        d_values = dot_f32(weights_bf, d_out, (0,), (0,))
        out_ref[:, 2 * width + at : 2 * width + at + DH] = d_values.astype(jnp.bfloat16)
        d_weights = dot_f32(d_out, values, (1,), (1,)).astype(jnp.bfloat16).astype(jnp.float32)
        inner = jnp.sum(d_weights * weights, -1, keepdims=True)
        d_scores = (weights * (d_weights - inner) * DH ** (-0.5)).astype(jnp.bfloat16)
        d_queries = unit_backward(
            dot_f32(d_scores, keys, (1,), (0,)), q_unit, q_rstd, gain_ref[0:1, :]
        )
        d_keys = unit_backward(
            dot_f32(d_scores, queries, (0,), (0,)), k_unit, k_rstd, gain_ref[1:2, :]
        )
        out_ref[:, at : at + DH] = d_queries.astype(jnp.bfloat16)
        out_ref[:, width + at : width + at + DH] = d_keys.astype(jnp.bfloat16)


def attention(kernel, projected, segment, qk_gain, extra, kinds):
    rows, wide = projected.shape
    heads = wide // (3 * DH)
    return pl.pallas_call(
        functools.partial(kernel, heads),
        out_shape=jax.ShapeDtypeStruct((rows, kinds * heads * DH), jnp.bfloat16),
        compiler_params=params(),
        cost_estimate=pl.CostEstimate(
            flops=heads * rows * rows * DH * 16,
            bytes_accessed=rows * wide * 8,
            transcendentals=heads * rows * rows,
        ),
    )(projected, segment.reshape(rows, 1), segment.reshape(1, rows), qk_gain, *extra)


def weight_kernel(keys, scale, normed_ref, one_ref, two_ref, *refs):
    b_refs, refs = refs[: len(keys)], refs[len(keys) :]
    me, t = lax.axis_index("dp"), pl.program_id(0)

    def product(load, total):
        for order, key in enumerate(keys):
            term = jnp.dot(load(me ^ key), b_refs[order][...], preferred_element_type=jnp.float32)
            if scale is None and order == 0:
                total[...] = term
            else:
                total[...] += term

    def normed(at):
        return normed_ref[at]

    def cot(at):
        return jnp.concatenate([one_ref[at], two_ref[at]], 1)

    if scale is None:
        total = refs[0].at[0]
    else:
        before_ref, qkv_ref, out_ref, total = refs
        total[...] = before_ref[0]

    @pl.when(t < 3)
    def _():
        product(normed, total)
        if scale is not None:
            qkv_ref[0] = (total[...] * scale).astype(jnp.bfloat16)

    @pl.when(t == 3)
    def _():
        product(cot, total)
        if scale is not None:
            out_ref[...] = (total[...] * scale).astype(jnp.bfloat16)


def weight_grads(normed_cols, cot_one, cot_two, gathered, keys, before, scale):
    count, depth, rows = normed_cols.shape
    width = gathered[0].shape[1] // 4
    whole = pl.BlockSpec((count, depth, rows), lambda t: (0, 0, 0))
    half = pl.BlockSpec((count, depth, rows // 2), lambda t: (0, 0, 0))
    sums = pl.BlockSpec((1, depth, width), lambda t: (t, 0, 0))
    sums_shape = jax.ShapeDtypeStruct((4, depth, width), jnp.float32)
    return pl.pallas_call(
        functools.partial(weight_kernel, keys, scale),
        grid=(4,),
        in_specs=[whole, half, half]
        + [pl.BlockSpec((rows, width), lambda t: (0, t))] * len(keys)
        + ([] if before is None else [sums]),
        out_specs=sums
        if before is None
        else [
            pl.BlockSpec((1, depth, width), lambda t: (jnp.minimum(t, 2), 0, 0)),
            pl.BlockSpec((depth, width), lambda t: (0, 0)),
        ],
        out_shape=sums_shape
        if before is None
        else [
            jax.ShapeDtypeStruct((3, depth, width), jnp.bfloat16),
            jax.ShapeDtypeStruct((depth, width), jnp.bfloat16),
        ],
        scratch_shapes=[] if before is None else [pltpu.VMEM((depth, width), jnp.float32)],
        compiler_params=params(),
        cost_estimate=pl.CostEstimate(
            flops=8 * len(keys) * depth * rows * width,
            bytes_accessed=4 * count * depth * rows + 8 * len(keys) * rows * width,
            transcendentals=0,
        ),
    )(normed_cols, cot_one, cot_two, *gathered, *([] if before is None else [before]))


def flip(values, axis, bit):
    count = lax.axis_size(axis)
    return lax.ppermute(values, axis, [(at, at ^ bit) for at in range(count)])


def exchange_small(values, axis):
    return [values] + [flip(values, axis, bit) for bit in range(1, lax.axis_size(axis))]


def gather_xor(values, axis):
    count = lax.axis_size(axis)
    high, low = count // 2, count // 4

    def spread(held):
        bit = low // 2
        while bit >= 1:
            for key in sorted(held):
                held[key | bit] = flip(held[key], axis, bit)
            bit //= 2
        return held

    over_high, over_low = flip(values, axis, high), flip(values, axis, low)
    own = spread({0: values})
    keys = sorted(own)
    spread_own, over_high, over_low = lax.optimization_barrier(
        ([own[key] for key in keys], over_high, over_low)
    )
    even = lax.axis_index(axis) % 2 == 0
    onward = jnp.where(even, over_low, over_high)
    pairs = [(at, at ^ (high if at % 2 == 0 else low)) for at in range(count)]
    far = lax.ppermute(onward, axis, pairs)
    near = dict(zip(keys, spread_own))
    near.update(spread({high: over_high}))
    near.update(spread({low: over_low}))
    return near, high | low, far, spread


def columns_to_owner(turned, axis):
    count = lax.axis_size(axis)
    parts, part, rows = turned.shape
    cut = turned.reshape(count, parts * part // count, rows)
    return lax.all_to_all(cut, axis, 0, 0, tiled=True)


def shards(patches, dest_group, dest_row, segment, ln_gain, w_qkv, qk_gain, w_out, cotangent):
    group_rows, part_width = patches.shape
    groups = lax.axis_size("dp")
    parts = lax.axis_size("mp")
    slot_size = 2 * group_rows // groups
    slots = groups * slot_size
    full_width, local_width = w_out.shape
    my_group, my_index = lax.axis_index("dp"), lax.axis_index("mp")
    w_t = jnp.transpose(w_qkv, (1, 0, 2))
    w_out_t = w_out[None]

    first_cot, second_cot = turn_halves(cotangent)
    cot_one = lax.all_gather(first_cot, "mp", axis=0, tiled=False)

    position = jnp.arange(group_rows, dtype=jnp.int32)
    earlier = (dest_group[:, None] == dest_group[None, :]) & (position[None, :] < position[:, None])
    rank_within = jnp.sum(earlier.astype(jnp.int32), 1)
    place = dest_group * slot_size + rank_within
    to_slot = jnp.arange(slots, dtype=jnp.int32)[:, None] == place[None, :]
    outbox = dot_f32(to_slot.astype(jnp.bfloat16), patches, (1,), (0,)).astype(jnp.bfloat16)
    inbox = lax.all_to_all(
        outbox.reshape(groups, slot_size, part_width), "dp", split_axis=0, concat_axis=0, tiled=True
    ).reshape(slots, part_width)

    outbox, late_patches = lax.optimization_barrier((outbox, patches))
    wide = late_patches.astype(jnp.float32)
    part_mean = jnp.mean(wide, -1)
    part_dev = jnp.sum(jnp.square(wide - part_mean[:, None]), -1)
    seen = exchange_small(jnp.stack([part_mean, part_dev]), "mp")
    row_mean = sum(entry[0] for entry in seen) / parts
    row_dev = sum(entry[1] + part_width * jnp.square(entry[0] - row_mean) for entry in seen)
    row_rstd = lax.rsqrt(row_dev / full_width + 1e-06)
    notes = jnp.stack([dest_row.astype(jnp.float32) + 1.0, row_mean, row_rstd])
    outnotes = jnp.sum(jnp.where(to_slot[None], notes[:, None, :], 0.0), -1)
    outnotes = outnotes.reshape(3, groups, slot_size)
    came = []
    for bit in range(groups):
        mine = lax.dynamic_index_in_dim(outnotes, my_group ^ bit, 1, keepdims=False)
        came.append(mine if bit == 0 else flip(mine, "dp", bit))
    sender = jnp.arange(groups, dtype=jnp.int32)[None, :, None]
    innotes = sum(
        jnp.where(sender == (my_group ^ bit), entry[:, None, :], 0.0)
        for bit, entry in enumerate(came)
    ).reshape(3, slots)
    arrived_at = innotes[0].astype(jnp.int32) - 1
    at_row = arrived_at[:, None] == position[None, :]
    mean = jnp.sum(jnp.where(at_row, innotes[1][:, None], 0.0), 0, keepdims=True)
    rstd = jnp.sum(jnp.where(at_row, innotes[2][:, None], 0.0), 0, keepdims=True)
    packed = dot_f32(inbox, at_row.astype(jnp.bfloat16), (0,), (0,)).astype(jnp.bfloat16)
    gain_column = ln_gain[:, None]
    my_gain = lax.dynamic_slice_in_dim(gain_column, my_index * part_width, part_width, 0)
    unit_rows = (packed.astype(jnp.float32) - mean) * rstd
    normed_part = (unit_rows * my_gain).astype(jnp.bfloat16)

    normed_part, cot_one = lax.optimization_barrier((normed_part, cot_one))
    normed = lax.all_gather(normed_part, "mp", axis=0, tiled=False)
    d_heads_one = project(cot_one, w_out_t, jnp.bfloat16)
    cot_cols_one = columns_to_owner(cot_one, "dp")
    normed, d_heads_one, cot_cols_one, late_cot = lax.optimization_barrier(
        (normed, d_heads_one, cot_cols_one, second_cot)
    )
    cot_two = lax.all_gather(late_cot, "mp", axis=0, tiled=False)
    projected = project(normed, w_t, jnp.float32)
    normed_cols = columns_to_owner(normed, "dp")

    heads_out = attention(forward_kernel, projected, segment, qk_gain, (), 1)
    heads_out, normed_cols = lax.optimization_barrier((heads_out, normed_cols))
    attn_part = expand(heads_out, w_out_t, parts, 1)
    attn_part, cot_two = lax.optimization_barrier((attn_part, cot_two))
    attn = lax.psum_scatter(attn_part, "mp", scatter_dimension=0, tiled=False)
    output = (packed.astype(jnp.float32) + attn.astype(jnp.float32)).astype(jnp.bfloat16).T

    d_heads_two = project(cot_two, w_out_t, jnp.bfloat16)
    d_all = attention(backward_kernel, projected, segment, qk_gain, (d_heads_one, d_heads_two), 4)
    d_part, sums = expand(d_all, w_t, parts, 2, gain_column, normed)
    d_normed = lax.psum_scatter(d_part, "mp", scatter_dimension=0, tiled=False)
    sums = sum(exchange_small(sums, "mp")) / full_width
    scale_grad = 1.0 / math.sqrt(group_rows * groups)
    columns = (normed_cols, cot_cols_one, columns_to_owner(cot_two, "dp"))
    near, far_key, far, spread = gather_xor(d_all, "dp")
    keys = sorted(near)
    sums_near = weight_grads(*columns, [near[key] for key in keys], keys, None, None)
    far, sums_near = lax.optimization_barrier((far, sums_near))
    far = spread({far_key: far})
    keys = sorted(far)
    sums_near = weight_grads(*columns, [far[key] for key in keys], keys, sums_near, scale_grad)
    d_normed, sums_near = lax.optimization_barrier((d_normed, sums_near))
    qkv_grad, out_grad = sums_near

    d_unit = d_normed.astype(jnp.float32) * my_gain
    d_input = rstd * (d_unit - sums[0:1] - unit_rows * sums[1:2])
    input_grad = (cotangent.astype(jnp.float32) + d_input.T).astype(jnp.bfloat16)
    return (output, input_grad, qkv_grad.transpose(1, 0, 2), out_grad)


def solution(mesh):
    placed = (
        P("dp", "mp"),
        P("dp"),
        P("dp"),
        P("dp"),
        P(),
        P(None, None, "mp"),
        P(),
        P(None, "mp"),
        P("dp", "mp"),
    )
    return jax.shard_map(
        shards,
        mesh=mesh,
        in_specs=placed,
        out_specs=(P("dp", "mp"), P("dp", "mp"), P("dp", None, "mp"), P("dp", "mp")),
        check_vma=False,
    )
```

```python
import functools
import math

import jax
import jax.numpy as jnp
from jax import lax
from jax.experimental import pallas as pl
from jax.experimental.pallas import tpu as pltpu
from jax.sharding import PartitionSpec as P

DH = 128
VMEM_BYTES = 48 * 1024 * 1024


def dot_f32(left, right, left_dims, right_dims):
    return lax.dot_general(
        left, right, ((left_dims, right_dims), ((), ())), preferred_element_type=jnp.float32
    )


def params():
    return pltpu.CompilerParams(vmem_limit_bytes=VMEM_BYTES)


def turn_kernel(x_ref, out_ref):
    out_ref[...] = x_ref[...].T


def turn(x):
    rows, part = x.shape
    return pl.pallas_call(
        turn_kernel,
        out_shape=jax.ShapeDtypeStruct((part, rows), x.dtype),
        compiler_params=params(),
        cost_estimate=pl.CostEstimate(flops=0, bytes_accessed=4 * rows * part, transcendentals=0),
    )(x)


def add_block_kernel(first, at_ref, x_ref, w_ref, *refs):
    out_ref, block = refs[-2:]

    @pl.when(pl.program_id(0) == 0)
    def _():
        block[...] = x_ref[...].T

    term = jnp.dot(block[...], w_ref[0], preferred_element_type=jnp.float32)
    out_ref[...] = term if first else refs[0][...] + term


def add_block(total, x, w, at):
    part, rows = x.shape
    kinds, _, width = w.shape
    sums = pl.BlockSpec((rows, width), lambda t, at_ref: (0, t))
    before = [] if total is None else [total]
    return pl.pallas_call(
        functools.partial(add_block_kernel, total is None),
        grid_spec=pltpu.PrefetchScalarGridSpec(
            num_scalar_prefetch=1,
            grid=(kinds,),
            in_specs=[
                pl.BlockSpec((part, rows), lambda t, at_ref: (0, 0)),
                pl.BlockSpec((1, part, width), lambda t, at_ref: (t, at_ref[0], 0)),
            ]
            + [sums] * len(before),
            out_specs=sums,
            scratch_shapes=[pltpu.VMEM((rows, part), jnp.bfloat16)],
        ),
        out_shape=jax.ShapeDtypeStruct((rows, kinds * width), jnp.float32),
        input_output_aliases={} if total is None else {3: 0},
        compiler_params=params(),
        cost_estimate=pl.CostEstimate(
            flops=2 * rows * part * kinds * width,
            bytes_accessed=2 * kinds * part * width + 8 * rows * kinds * width,
            transcendentals=0,
        ),
    )(at.reshape(1).astype(jnp.int32), x, w, *before)


def project_kernel(steps, width, x_ref, w_ref, out_ref, total, block):
    at, t = pl.program_id(0), pl.program_id(1)
    columns = pl.ds(pl.multiple_of(t * width, width), width)

    @pl.when(t == 0)
    def _():
        block[...] = x_ref[0].T

    term = jnp.dot(block[...], w_ref[0], preferred_element_type=jnp.float32)

    @pl.when(at == 0)
    def _():
        total[:, columns] = term

    @pl.when(at > 0)
    def _():
        total[:, columns] += term

    @pl.when(at == steps - 1)
    def _():
        out_ref[:, columns] = total[:, columns].astype(out_ref.dtype)


def project(x, w, dtype):
    steps, part, rows = x.shape
    kinds, depth, width = w.shape
    return pl.pallas_call(
        functools.partial(project_kernel, steps, width),
        grid=(steps, kinds),
        in_specs=[
            pl.BlockSpec((1, part, rows), lambda at, t: (at, 0, 0)),
            pl.BlockSpec((1, part, width), lambda at, t: (t, at, 0)),
        ],
        out_specs=pl.BlockSpec((rows, kinds * width), lambda at, t: (0, 0)),
        out_shape=jax.ShapeDtypeStruct((rows, kinds * width), dtype),
        scratch_shapes=[
            pltpu.VMEM((rows, kinds * width), jnp.float32),
            pltpu.VMEM((rows, part), jnp.bfloat16),
        ],
        compiler_params=params(),
        cost_estimate=pl.CostEstimate(
            flops=2 * rows * depth * kinds * width,
            bytes_accessed=2 * kinds * depth * width + 2 * rows * depth,
            transcendentals=0,
        ),
    )(x, w)


def expand_kernel(kinds, width, x_ref, w_ref, *refs):
    total = None
    for t in range(kinds):
        term = dot_f32(w_ref[t], x_ref[:, t * width : (t + 1) * width], (1,), (1,))
        total = term if total is None else total + term
    if len(refs) == 1:
        (out_ref,) = refs
    else:
        gain_ref, normed_ref, out_ref, sums_ref = refs

        @pl.when((pl.program_id(0) == 0) & (pl.program_id(1) == 0))
        def _():
            sums_ref[...] = jnp.zeros_like(sums_ref)

        sums_ref[0:1, :] += jnp.sum(total * gain_ref[...], 0, keepdims=True)
        sums_ref[1:2, :] += jnp.sum(total * normed_ref[0].astype(jnp.float32), 0, keepdims=True)
    out_ref[0] = total.astype(jnp.bfloat16)


def expand(x, w, parts, cuts, gain=None, normed=None):
    rows = x.shape[0]
    kinds, depth, width = w.shape
    part = depth // parts
    piece = part // cuts
    turned = pl.BlockSpec((1, piece, rows), lambda at, cut: (at, cut, 0))
    turned_shape = jax.ShapeDtypeStruct((parts, part, rows), jnp.bfloat16)
    more = [] if gain is None else [gain, normed]
    return pl.pallas_call(
        functools.partial(expand_kernel, kinds, width),
        grid=(parts, cuts),
        in_specs=[
            pl.BlockSpec((rows, kinds * width), lambda at, cut: (0, 0)),
            pl.BlockSpec((kinds, piece, width), lambda at, cut: (0, at * cuts + cut, 0)),
        ]
        + ([pl.BlockSpec((piece, 1), lambda at, cut: (at * cuts + cut, 0)), turned] if more else []),
        out_specs=[turned, pl.BlockSpec((2, rows), lambda at, cut: (0, 0))] if more else turned,
        out_shape=[turned_shape, jax.ShapeDtypeStruct((2, rows), jnp.float32)]
        if more
        else turned_shape,
        compiler_params=params(),
        cost_estimate=pl.CostEstimate(
            flops=2 * rows * depth * kinds * width,
            bytes_accessed=2 * kinds * depth * width + 2 * rows * depth,
            transcendentals=0,
        ),
    )(x, w, *more)


def unit_heads(raw):
    center = raw - jnp.mean(raw, -1, keepdims=True)
    rstd = lax.rsqrt(jnp.mean(center * center, -1, keepdims=True) + 1e-06)
    return center * rstd, rstd


def head_forward(proj_ref, same, gain_ref, heads, head):
    width = heads * DH

    def load(kind):
        start = kind * width + head * DH
        return proj_ref[:, start : start + DH]

    q_unit, q_rstd = unit_heads(load(0))
    k_unit, k_rstd = unit_heads(load(1))
    values = load(2).astype(jnp.bfloat16)
    queries = (q_unit * gain_ref[0:1, :]).astype(jnp.bfloat16)
    keys = (k_unit * gain_ref[1:2, :]).astype(jnp.bfloat16)
    scores = dot_f32(queries, keys, (1,), (1,)) * DH ** (-0.5)
    raised = jnp.where(same, jnp.exp(scores), 0.0)
    weights = raised / jnp.sum(raised, -1, keepdims=True)
    return q_unit, q_rstd, k_unit, k_rstd, values, queries, keys, weights


def forward_kernel(heads, proj_ref, row_ref, col_ref, gain_ref, out_ref):
    same = row_ref[...] == col_ref[...]
    for head in range(heads):
        values, _, _, weights = head_forward(proj_ref, same, gain_ref, heads, head)[4:]
        mixed = dot_f32(weights.astype(jnp.bfloat16), values, (1,), (0,))
        out_ref[:, head * DH : (head + 1) * DH] = mixed.astype(jnp.bfloat16)


def unit_backward(grad, unit, rstd, gain):
    scaled = grad.astype(jnp.bfloat16).astype(jnp.float32) * gain
    return rstd * (
        scaled
        - jnp.mean(scaled, -1, keepdims=True)
        - unit * jnp.mean(scaled * unit, -1, keepdims=True)
    )


def backward_kernel(heads, proj_ref, row_ref, col_ref, gain_ref, d_ref, out_ref):
    same = row_ref[...] == col_ref[...]
    width = heads * DH
    for head in range(heads):
        q_unit, q_rstd, k_unit, k_rstd, values, queries, keys, weights = head_forward(
            proj_ref, same, gain_ref, heads, head
        )
        at = head * DH
        weights_bf = weights.astype(jnp.bfloat16)
        d_out = d_ref[:, at : at + DH]
        mixed = dot_f32(weights_bf, values, (1,), (0,))
        out_ref[:, 3 * width + at : 3 * width + at + DH] = mixed.astype(jnp.bfloat16)
        d_values = dot_f32(weights_bf, d_out, (0,), (0,))
        out_ref[:, 2 * width + at : 2 * width + at + DH] = d_values.astype(jnp.bfloat16)
        d_weights = dot_f32(d_out, values, (1,), (1,)).astype(jnp.bfloat16).astype(jnp.float32)
        inner = jnp.sum(d_weights * weights, -1, keepdims=True)
        d_scores = (weights * (d_weights - inner) * DH ** (-0.5)).astype(jnp.bfloat16)
        d_queries = unit_backward(
            dot_f32(d_scores, keys, (1,), (0,)), q_unit, q_rstd, gain_ref[0:1, :]
        )
        d_keys = unit_backward(
            dot_f32(d_scores, queries, (0,), (0,)), k_unit, k_rstd, gain_ref[1:2, :]
        )
        out_ref[:, at : at + DH] = d_queries.astype(jnp.bfloat16)
        out_ref[:, width + at : width + at + DH] = d_keys.astype(jnp.bfloat16)


def attention(kernel, projected, segment, qk_gain, extra, kinds):
    rows, wide = projected.shape
    heads = wide // (3 * DH)
    return pl.pallas_call(
        functools.partial(kernel, heads),
        out_shape=jax.ShapeDtypeStruct((rows, kinds * heads * DH), jnp.bfloat16),
        compiler_params=params(),
        cost_estimate=pl.CostEstimate(
            flops=heads * rows * rows * DH * 16,
            bytes_accessed=rows * wide * 8,
            transcendentals=heads * rows * rows,
        ),
    )(projected, segment.reshape(rows, 1), segment.reshape(1, rows), qk_gain, *extra)


def weight_kernel(keys, scale, normed_ref, cot_ref, *refs):
    b_refs, refs = refs[: len(keys)], refs[len(keys) :]
    me, t = lax.axis_index("dp"), pl.program_id(0)

    def product(load, total):
        for order, key in enumerate(keys):
            term = jnp.dot(load(me ^ key), b_refs[order][...], preferred_element_type=jnp.float32)
            if scale is None and order == 0:
                total[...] = term
            else:
                total[...] += term

    def normed(at):
        return normed_ref[at]

    def cot(at):
        return cot_ref[at]

    if scale is None:
        total = refs[0].at[0]
    else:
        before_ref, qkv_ref, out_ref, total = refs
        total[...] = before_ref[0]

    @pl.when(t < 3)
    def _():
        product(normed, total)
        if scale is not None:
            qkv_ref[0] = (total[...] * scale).astype(jnp.bfloat16)

    @pl.when(t == 3)
    def _():
        product(cot, total)
        if scale is not None:
            out_ref[...] = (total[...] * scale).astype(jnp.bfloat16)


def weight_grads(normed_cols, cot_cols, gathered, keys, before, scale):
    count, depth, rows = normed_cols.shape
    width = gathered[0].shape[1] // 4
    whole = pl.BlockSpec((count, depth, rows), lambda t: (0, 0, 0))
    sums = pl.BlockSpec((1, depth, width), lambda t: (t, 0, 0))
    sums_shape = jax.ShapeDtypeStruct((4, depth, width), jnp.float32)
    return pl.pallas_call(
        functools.partial(weight_kernel, keys, scale),
        grid=(4,),
        in_specs=[whole, whole]
        + [pl.BlockSpec((rows, width), lambda t: (0, t))] * len(keys)
        + ([] if before is None else [sums]),
        out_specs=sums
        if before is None
        else [
            pl.BlockSpec((1, depth, width), lambda t: (jnp.minimum(t, 2), 0, 0)),
            pl.BlockSpec((depth, width), lambda t: (0, 0)),
        ],
        out_shape=sums_shape
        if before is None
        else [
            jax.ShapeDtypeStruct((3, depth, width), jnp.bfloat16),
            jax.ShapeDtypeStruct((depth, width), jnp.bfloat16),
        ],
        scratch_shapes=[] if before is None else [pltpu.VMEM((depth, width), jnp.float32)],
        compiler_params=params(),
        cost_estimate=pl.CostEstimate(
            flops=8 * len(keys) * depth * rows * width,
            bytes_accessed=4 * count * depth * rows + 8 * len(keys) * rows * width,
            transcendentals=0,
        ),
    )(normed_cols, cot_cols, *gathered, *([] if before is None else [before]))


def flip(values, axis, bit):
    count = lax.axis_size(axis)
    return lax.ppermute(values, axis, [(at, at ^ bit) for at in range(count)])


def exchange_small(values, axis):
    return [values] + [flip(values, axis, bit) for bit in range(1, lax.axis_size(axis))]


def gather_xor(values, axis):
    count = lax.axis_size(axis)
    high, low = count // 2, count // 4

    def spread(held):
        bit = low // 2
        while bit >= 1:
            for key in sorted(held):
                held[key | bit] = flip(held[key], axis, bit)
            bit //= 2
        return held

    over_high, over_low = flip(values, axis, high), flip(values, axis, low)
    own = spread({0: values})
    keys = sorted(own)
    spread_own, over_high, over_low = lax.optimization_barrier(
        ([own[key] for key in keys], over_high, over_low)
    )
    even = lax.axis_index(axis) % 2 == 0
    onward = jnp.where(even, over_low, over_high)
    pairs = [(at, at ^ (high if at % 2 == 0 else low)) for at in range(count)]
    far = lax.ppermute(onward, axis, pairs)
    near = dict(zip(keys, spread_own))
    near.update(spread({high: over_high}))
    near.update(spread({low: over_low}))
    return near, high | low, far, spread


def line_blocks(values, axis, beside):
    count, me = lax.axis_size(axis), lax.axis_index(axis)
    blocks = [(me, None, values)]
    right = left = values
    for step in range(1, count):
        right = lax.ppermute(right, axis, [(at, at + 1) for at in range(step - 1, count - 1)])
        left = lax.ppermute(left, axis, [(at, at - 1) for at in range(1, count - step + 1)])
        if step == 1:
            right, left, beside = lax.optimization_barrier((right, left, beside))
        over, under = me >= step, me + step < count
        if 2 * step >= count:
            at = jnp.where(over, me - step, jnp.minimum(me + step, count - 1))
            blocks.append((at, over | under, right + left))
        else:
            blocks.append((jnp.maximum(me - step, 0), over, right))
            blocks.append((jnp.minimum(me + step, count - 1), under, left))
    return blocks, beside


def columns_to_owner(turned, axis):
    count = lax.axis_size(axis)
    parts, part, rows = turned.shape
    cut = turned.reshape(count, parts * part // count, rows)
    return lax.all_to_all(cut, axis, 0, 0, tiled=True)


def shards(patches, dest_group, dest_row, segment, ln_gain, w_qkv, qk_gain, w_out, cotangent):
    group_rows, part_width = patches.shape
    groups = lax.axis_size("dp")
    parts = lax.axis_size("mp")
    slot_size = 2 * group_rows // groups
    slots = groups * slot_size
    full_width, local_width = w_out.shape
    my_group, my_index = lax.axis_index("dp"), lax.axis_index("mp")
    w_t = jnp.transpose(w_qkv, (1, 0, 2))
    w_out_t = w_out[None]

    whole_cot = lax.all_gather(turn(cotangent), "mp", axis=0, tiled=False)

    position = jnp.arange(group_rows, dtype=jnp.int32)
    earlier = (dest_group[:, None] == dest_group[None, :]) & (position[None, :] < position[:, None])
    rank_within = jnp.sum(earlier.astype(jnp.int32), 1)
    place = dest_group * slot_size + rank_within
    to_slot = jnp.arange(slots, dtype=jnp.int32)[:, None] == place[None, :]
    outbox = dot_f32(to_slot.astype(jnp.bfloat16), patches, (1,), (0,)).astype(jnp.bfloat16)
    inbox = lax.all_to_all(
        outbox.reshape(groups, slot_size, part_width), "dp", split_axis=0, concat_axis=0, tiled=True
    ).reshape(slots, part_width)

    outbox, late_patches = lax.optimization_barrier((outbox, patches))
    wide = late_patches.astype(jnp.float32)
    part_mean = jnp.mean(wide, -1)
    part_dev = jnp.sum(jnp.square(wide - part_mean[:, None]), -1)
    seen = exchange_small(jnp.stack([part_mean, part_dev]), "mp")
    row_mean = sum(entry[0] for entry in seen) / parts
    row_dev = sum(entry[1] + part_width * jnp.square(entry[0] - row_mean) for entry in seen)
    row_rstd = lax.rsqrt(row_dev / full_width + 1e-06)
    notes = jnp.stack([dest_row.astype(jnp.float32) + 1.0, row_mean, row_rstd])
    outnotes = jnp.sum(jnp.where(to_slot[None], notes[:, None, :], 0.0), -1)
    outnotes = outnotes.reshape(3, groups, slot_size)
    came = []
    for bit in range(groups):
        mine = lax.dynamic_index_in_dim(outnotes, my_group ^ bit, 1, keepdims=False)
        came.append(mine if bit == 0 else flip(mine, "dp", bit))
    sender = jnp.arange(groups, dtype=jnp.int32)[None, :, None]
    innotes = sum(
        jnp.where(sender == (my_group ^ bit), entry[:, None, :], 0.0)
        for bit, entry in enumerate(came)
    ).reshape(3, slots)
    arrived_at = innotes[0].astype(jnp.int32) - 1
    at_row = arrived_at[:, None] == position[None, :]
    mean = jnp.sum(jnp.where(at_row, innotes[1][:, None], 0.0), 0, keepdims=True)
    rstd = jnp.sum(jnp.where(at_row, innotes[2][:, None], 0.0), 0, keepdims=True)
    packed = dot_f32(inbox, at_row.astype(jnp.bfloat16), (0,), (0,)).astype(jnp.bfloat16)
    gain_column = ln_gain[:, None]
    my_gain = lax.dynamic_slice_in_dim(gain_column, my_index * part_width, part_width, 0)
    unit_rows = (packed.astype(jnp.float32) - mean) * rstd
    normed_part = (unit_rows * my_gain).astype(jnp.bfloat16)

    blocks, whole_cot = line_blocks(normed_part, "mp", whole_cot)
    d_heads = project(whole_cot, w_out_t, jnp.bfloat16)
    cot_cols = columns_to_owner(whole_cot, "dp")
    projected = None
    normed = jnp.zeros((parts, part_width, group_rows), jnp.bfloat16)
    for order, (at, there, block) in enumerate(blocks):
        if order == len(blocks) - 1:
            block, cot_cols, d_heads, projected = lax.optimization_barrier(
                (block, cot_cols, d_heads, projected)
            )
        projected = add_block(projected, block, w_t, at)
        if there is not None:
            at, block = jnp.where(there, at, my_index), jnp.where(there, block, normed_part)
        normed = lax.dynamic_update_slice(normed, block[None], (at, 0, 0))
    normed_cols = columns_to_owner(normed, "dp")

    heads_out = attention(forward_kernel, projected, segment, qk_gain, (), 1)
    attn_part = expand(heads_out, w_out_t, parts, 1)
    attn_part, d_heads = lax.optimization_barrier((attn_part, d_heads))
    attn = lax.psum_scatter(attn_part, "mp", scatter_dimension=0, tiled=False)
    output = (packed.astype(jnp.float32) + attn.astype(jnp.float32)).astype(jnp.bfloat16).T

    d_all = attention(backward_kernel, projected, segment, qk_gain, (d_heads,), 4)
    late_all, normed_cols = lax.optimization_barrier((d_all, normed_cols))
    d_part, sums = expand(late_all, w_t, parts, 2, gain_column, normed)
    d_normed = lax.psum_scatter(d_part, "mp", scatter_dimension=0, tiled=False)
    sums = sum(exchange_small(sums, "mp")) / full_width
    scale_grad = 1.0 / math.sqrt(group_rows * groups)
    columns = (normed_cols, cot_cols)
    near, far_key, far, spread = gather_xor(d_all, "dp")
    keys = sorted(near)
    sums_near = weight_grads(*columns, [near[key] for key in keys], keys, None, None)
    far, sums_near = lax.optimization_barrier((far, sums_near))
    far = spread({far_key: far})
    keys = sorted(far)
    sums_near = weight_grads(*columns, [far[key] for key in keys], keys, sums_near, scale_grad)
    d_normed, sums_near = lax.optimization_barrier((d_normed, sums_near))
    qkv_grad, out_grad = sums_near

    d_unit = d_normed.astype(jnp.float32) * my_gain
    d_input = rstd * (d_unit - sums[0:1] - unit_rows * sums[1:2])
    input_grad = (cotangent.astype(jnp.float32) + d_input.T).astype(jnp.bfloat16)
    return (output, input_grad, qkv_grad.transpose(1, 0, 2), out_grad)


def solution(mesh):
    placed = (
        P("dp", "mp"),
        P("dp"),
        P("dp"),
        P("dp"),
        P(),
        P(None, None, "mp"),
        P(),
        P(None, "mp"),
        P("dp", "mp"),
    )
    return jax.shard_map(
        shards,
        mesh=mesh,
        in_specs=placed,
        out_specs=(P("dp", "mp"), P("dp", "mp"), P("dp", None, "mp"), P("dp", "mp")),
        check_vma=False,
    )
```

```python
import functools
import math

import jax
import jax.numpy as jnp
from jax import lax
from jax.experimental import pallas as pl
from jax.experimental.pallas import tpu as pltpu
from jax.sharding import PartitionSpec as P

DH = 128
VMEM_BYTES = 48 * 1024 * 1024


def dot_f32(left, right, left_dims, right_dims):
    return lax.dot_general(
        left, right, ((left_dims, right_dims), ((), ())), preferred_element_type=jnp.float32
    )


def params():
    return pltpu.CompilerParams(vmem_limit_bytes=VMEM_BYTES)


def turn_kernel(x_ref, out_ref):
    out_ref[...] = x_ref[...].T


def turn(x):
    rows, part = x.shape
    return pl.pallas_call(
        turn_kernel,
        out_shape=jax.ShapeDtypeStruct((part, rows), x.dtype),
        compiler_params=params(),
        cost_estimate=pl.CostEstimate(flops=0, bytes_accessed=4 * rows * part, transcendentals=0),
    )(x)


def add_block_kernel(first, at_ref, x_ref, w_ref, *refs):
    out_ref, block = refs[-2:]

    @pl.when(pl.program_id(0) == 0)
    def _():
        block[...] = x_ref[...].T

    term = jnp.dot(block[...], w_ref[0], preferred_element_type=jnp.float32)
    out_ref[...] = term if first else refs[0][...] + term


def add_block(total, x, w, at):
    part, rows = x.shape
    kinds, _, width = w.shape
    sums = pl.BlockSpec((rows, width), lambda t, at_ref: (0, t))
    before = [] if total is None else [total]
    return pl.pallas_call(
        functools.partial(add_block_kernel, total is None),
        grid_spec=pltpu.PrefetchScalarGridSpec(
            num_scalar_prefetch=1,
            grid=(kinds,),
            in_specs=[
                pl.BlockSpec((part, rows), lambda t, at_ref: (0, 0)),
                pl.BlockSpec((1, part, width), lambda t, at_ref: (t, at_ref[0], 0)),
            ]
            + [sums] * len(before),
            out_specs=sums,
            scratch_shapes=[pltpu.VMEM((rows, part), jnp.bfloat16)],
        ),
        out_shape=jax.ShapeDtypeStruct((rows, kinds * width), jnp.float32),
        input_output_aliases={} if total is None else {3: 0},
        compiler_params=params(),
        cost_estimate=pl.CostEstimate(
            flops=2 * rows * part * kinds * width,
            bytes_accessed=2 * kinds * part * width + 8 * rows * kinds * width,
            transcendentals=0,
        ),
    )(at.reshape(1).astype(jnp.int32), x, w, *before)


def project_kernel(steps, width, x_ref, w_ref, out_ref, total, block):
    at, t = pl.program_id(0), pl.program_id(1)
    columns = pl.ds(pl.multiple_of(t * width, width), width)

    @pl.when(t == 0)
    def _():
        block[...] = x_ref[0].T

    term = jnp.dot(block[...], w_ref[0], preferred_element_type=jnp.float32)

    @pl.when(at == 0)
    def _():
        total[:, columns] = term

    @pl.when(at > 0)
    def _():
        total[:, columns] += term

    @pl.when(at == steps - 1)
    def _():
        out_ref[:, columns] = total[:, columns].astype(out_ref.dtype)


def project(x, w, dtype):
    steps, part, rows = x.shape
    kinds, depth, width = w.shape
    return pl.pallas_call(
        functools.partial(project_kernel, steps, width),
        grid=(steps, kinds),
        in_specs=[
            pl.BlockSpec((1, part, rows), lambda at, t: (at, 0, 0)),
            pl.BlockSpec((1, part, width), lambda at, t: (t, at, 0)),
        ],
        out_specs=pl.BlockSpec((rows, kinds * width), lambda at, t: (0, 0)),
        out_shape=jax.ShapeDtypeStruct((rows, kinds * width), dtype),
        scratch_shapes=[
            pltpu.VMEM((rows, kinds * width), jnp.float32),
            pltpu.VMEM((rows, part), jnp.bfloat16),
        ],
        compiler_params=params(),
        cost_estimate=pl.CostEstimate(
            flops=2 * rows * depth * kinds * width,
            bytes_accessed=2 * kinds * depth * width + 2 * rows * depth,
            transcendentals=0,
        ),
    )(x, w)


def expand_kernel(kinds, width, x_ref, w_ref, *refs):
    total = None
    for t in range(kinds):
        term = dot_f32(w_ref[t], x_ref[:, t * width : (t + 1) * width], (1,), (1,))
        total = term if total is None else total + term
    if len(refs) == 1:
        (out_ref,) = refs
    else:
        gain_ref, normed_ref, out_ref, sums_ref = refs

        @pl.when((pl.program_id(0) == 0) & (pl.program_id(1) == 0))
        def _():
            sums_ref[...] = jnp.zeros_like(sums_ref)

        sums_ref[0:1, :] += jnp.sum(total * gain_ref[...], 0, keepdims=True)
        sums_ref[1:2, :] += jnp.sum(total * normed_ref[0].astype(jnp.float32), 0, keepdims=True)
    out_ref[0] = total.astype(jnp.bfloat16)


def expand(x, w, parts, cuts, gain=None, normed=None):
    rows = x.shape[0]
    kinds, depth, width = w.shape
    part = depth // parts
    piece = part // cuts
    turned = pl.BlockSpec((1, piece, rows), lambda at, cut: (at, cut, 0))
    turned_shape = jax.ShapeDtypeStruct((parts, part, rows), jnp.bfloat16)
    more = [] if gain is None else [gain, normed]
    return pl.pallas_call(
        functools.partial(expand_kernel, kinds, width),
        grid=(parts, cuts),
        in_specs=[
            pl.BlockSpec((rows, kinds * width), lambda at, cut: (0, 0)),
            pl.BlockSpec((kinds, piece, width), lambda at, cut: (0, at * cuts + cut, 0)),
        ]
        + ([pl.BlockSpec((piece, 1), lambda at, cut: (at * cuts + cut, 0)), turned] if more else []),
        out_specs=[turned, pl.BlockSpec((2, rows), lambda at, cut: (0, 0))] if more else turned,
        out_shape=[turned_shape, jax.ShapeDtypeStruct((2, rows), jnp.float32)]
        if more
        else turned_shape,
        compiler_params=params(),
        cost_estimate=pl.CostEstimate(
            flops=2 * rows * depth * kinds * width,
            bytes_accessed=2 * kinds * depth * width + 2 * rows * depth,
            transcendentals=0,
        ),
    )(x, w, *more)


def unit_heads(raw):
    center = raw - jnp.mean(raw, -1, keepdims=True)
    rstd = lax.rsqrt(jnp.mean(center * center, -1, keepdims=True) + 1e-06)
    return center * rstd, rstd


def head_forward(proj_ref, same, gain_ref, heads, head):
    width = heads * DH

    def load(kind):
        start = kind * width + head * DH
        return proj_ref[:, start : start + DH]

    q_unit, q_rstd = unit_heads(load(0))
    k_unit, k_rstd = unit_heads(load(1))
    values = load(2).astype(jnp.bfloat16)
    queries = (q_unit * gain_ref[0:1, :]).astype(jnp.bfloat16)
    keys = (k_unit * gain_ref[1:2, :]).astype(jnp.bfloat16)
    scores = dot_f32(queries, keys, (1,), (1,)) * DH ** (-0.5)
    raised = jnp.where(same, jnp.exp(scores), 0.0)
    weights = raised / jnp.sum(raised, -1, keepdims=True)
    return q_unit, q_rstd, k_unit, k_rstd, values, queries, keys, weights


def forward_kernel(heads, proj_ref, row_ref, col_ref, gain_ref, out_ref):
    same = row_ref[...] == col_ref[...]
    for head in range(heads):
        values, _, _, weights = head_forward(proj_ref, same, gain_ref, heads, head)[4:]
        mixed = dot_f32(weights.astype(jnp.bfloat16), values, (1,), (0,))
        out_ref[:, head * DH : (head + 1) * DH] = mixed.astype(jnp.bfloat16)


def unit_backward(grad, unit, rstd, gain):
    scaled = grad.astype(jnp.bfloat16).astype(jnp.float32) * gain
    return rstd * (
        scaled
        - jnp.mean(scaled, -1, keepdims=True)
        - unit * jnp.mean(scaled * unit, -1, keepdims=True)
    )


def backward_kernel(heads, proj_ref, row_ref, col_ref, gain_ref, d_ref, out_ref):
    same = row_ref[...] == col_ref[...]
    width = heads * DH
    for head in range(heads):
        q_unit, q_rstd, k_unit, k_rstd, values, queries, keys, weights = head_forward(
            proj_ref, same, gain_ref, heads, head
        )
        at = head * DH
        weights_bf = weights.astype(jnp.bfloat16)
        d_out = d_ref[:, at : at + DH]
        mixed = dot_f32(weights_bf, values, (1,), (0,))
        out_ref[:, 3 * width + at : 3 * width + at + DH] = mixed.astype(jnp.bfloat16)
        d_values = dot_f32(weights_bf, d_out, (0,), (0,))
        out_ref[:, 2 * width + at : 2 * width + at + DH] = d_values.astype(jnp.bfloat16)
        d_weights = dot_f32(d_out, values, (1,), (1,)).astype(jnp.bfloat16).astype(jnp.float32)
        inner = jnp.sum(d_weights * weights, -1, keepdims=True)
        d_scores = (weights * (d_weights - inner) * DH ** (-0.5)).astype(jnp.bfloat16)
        d_queries = unit_backward(
            dot_f32(d_scores, keys, (1,), (0,)), q_unit, q_rstd, gain_ref[0:1, :]
        )
        d_keys = unit_backward(
            dot_f32(d_scores, queries, (0,), (0,)), k_unit, k_rstd, gain_ref[1:2, :]
        )
        out_ref[:, at : at + DH] = d_queries.astype(jnp.bfloat16)
        out_ref[:, width + at : width + at + DH] = d_keys.astype(jnp.bfloat16)


def attention(kernel, projected, segment, qk_gain, extra, kinds):
    rows, wide = projected.shape
    heads = wide // (3 * DH)
    return pl.pallas_call(
        functools.partial(kernel, heads),
        out_shape=jax.ShapeDtypeStruct((rows, kinds * heads * DH), jnp.bfloat16),
        compiler_params=params(),
        cost_estimate=pl.CostEstimate(
            flops=heads * rows * rows * DH * 16,
            bytes_accessed=rows * wide * 8,
            transcendentals=heads * rows * rows,
        ),
    )(projected, segment.reshape(rows, 1), segment.reshape(1, rows), qk_gain, *extra)


def weight_kernel(keys, scale, normed_ref, cot_ref, *refs):
    b_refs, refs = refs[: len(keys)], refs[len(keys) :]
    me, t = lax.axis_index("dp"), pl.program_id(0)

    def product(load, total):
        for order, key in enumerate(keys):
            term = jnp.dot(load(me ^ key), b_refs[order][...], preferred_element_type=jnp.float32)
            if scale is None and order == 0:
                total[...] = term
            else:
                total[...] += term

    def normed(at):
        return normed_ref[at]

    def cot(at):
        return cot_ref[at]

    if scale is None:
        total = refs[0].at[0]
    else:
        before_ref, qkv_ref, out_ref, total = refs
        total[...] = before_ref[0]

    @pl.when(t < 3)
    def _():
        product(normed, total)
        if scale is not None:
            qkv_ref[0] = (total[...] * scale).astype(jnp.bfloat16)

    @pl.when(t == 3)
    def _():
        product(cot, total)
        if scale is not None:
            out_ref[...] = (total[...] * scale).astype(jnp.bfloat16)


def weight_grads(normed_cols, cot_cols, gathered, keys, before, scale):
    count, depth, rows = normed_cols.shape
    width = gathered[0].shape[1] // 4
    whole = pl.BlockSpec((count, depth, rows), lambda t: (0, 0, 0))
    sums = pl.BlockSpec((1, depth, width), lambda t: (t, 0, 0))
    sums_shape = jax.ShapeDtypeStruct((4, depth, width), jnp.float32)
    return pl.pallas_call(
        functools.partial(weight_kernel, keys, scale),
        grid=(4,),
        in_specs=[whole, whole]
        + [pl.BlockSpec((rows, width), lambda t: (0, t))] * len(keys)
        + ([] if before is None else [sums]),
        out_specs=sums
        if before is None
        else [
            pl.BlockSpec((1, depth, width), lambda t: (jnp.minimum(t, 2), 0, 0)),
            pl.BlockSpec((depth, width), lambda t: (0, 0)),
        ],
        out_shape=sums_shape
        if before is None
        else [
            jax.ShapeDtypeStruct((3, depth, width), jnp.bfloat16),
            jax.ShapeDtypeStruct((depth, width), jnp.bfloat16),
        ],
        scratch_shapes=[] if before is None else [pltpu.VMEM((depth, width), jnp.float32)],
        compiler_params=params(),
        cost_estimate=pl.CostEstimate(
            flops=8 * len(keys) * depth * rows * width,
            bytes_accessed=4 * count * depth * rows + 8 * len(keys) * rows * width,
            transcendentals=0,
        ),
    )(normed_cols, cot_cols, *gathered, *([] if before is None else [before]))


def flip(values, axis, bit):
    count = lax.axis_size(axis)
    return lax.ppermute(values, axis, [(at, at ^ bit) for at in range(count)])


def exchange_small(values, axis):
    return [values] + [flip(values, axis, bit) for bit in range(1, lax.axis_size(axis))]


def gather_xor(values, axis):
    count = lax.axis_size(axis)
    high, low = count // 2, count // 4

    def spread(held):
        bit = low // 2
        while bit >= 1:
            for key in sorted(held):
                held[key | bit] = flip(held[key], axis, bit)
            bit //= 2
        return held

    over_high, over_low = flip(values, axis, high), flip(values, axis, low)
    own = spread({0: values})
    keys = sorted(own)
    spread_own, over_high, over_low = lax.optimization_barrier(
        ([own[key] for key in keys], over_high, over_low)
    )
    even = lax.axis_index(axis) % 2 == 0
    onward = jnp.where(even, over_low, over_high)
    pairs = [(at, at ^ (high if at % 2 == 0 else low)) for at in range(count)]
    far = lax.ppermute(onward, axis, pairs)
    near = dict(zip(keys, spread_own))
    near.update(spread({high: over_high}))
    near.update(spread({low: over_low}))
    return near, high | low, far, spread


def line_blocks(values, axis, beside):
    count, me = lax.axis_size(axis), lax.axis_index(axis)
    blocks = [(me, None, values)]
    right = left = values
    for step in range(1, count):
        right = lax.ppermute(right, axis, [(at, at + 1) for at in range(step - 1, count - 1)])
        left = lax.ppermute(left, axis, [(at, at - 1) for at in range(1, count - step + 1)])
        if step == 1:
            right, left, beside = lax.optimization_barrier((right, left, beside))
        over, under = me >= step, me + step < count
        if 2 * step >= count:
            at = jnp.where(over, me - step, jnp.minimum(me + step, count - 1))
            blocks.append((at, over | under, right + left))
        else:
            blocks.append((jnp.maximum(me - step, 0), over, right))
            blocks.append((jnp.minimum(me + step, count - 1), under, left))
    return blocks, beside


def columns_to_owner(turned, axis):
    count = lax.axis_size(axis)
    parts, part, rows = turned.shape
    cut = turned.reshape(count, parts * part // count, rows)
    return lax.all_to_all(cut, axis, 0, 0, tiled=True)


def shards(patches, dest_group, dest_row, segment, ln_gain, w_qkv, qk_gain, w_out, cotangent):
    group_rows, part_width = patches.shape
    groups = lax.axis_size("dp")
    parts = lax.axis_size("mp")
    slot_size = 2 * group_rows // groups
    slots = groups * slot_size
    full_width, local_width = w_out.shape
    my_group, my_index = lax.axis_index("dp"), lax.axis_index("mp")
    w_t = jnp.transpose(w_qkv, (1, 0, 2))
    w_out_t = w_out[None]

    whole_cot = lax.all_gather(turn(cotangent), "mp", axis=0, tiled=False)

    position = jnp.arange(group_rows, dtype=jnp.int32)
    earlier = (dest_group[:, None] == dest_group[None, :]) & (position[None, :] < position[:, None])
    rank_within = jnp.sum(earlier.astype(jnp.int32), 1)
    place = dest_group * slot_size + rank_within
    to_slot = jnp.arange(slots, dtype=jnp.int32)[:, None] == place[None, :]
    outbox = dot_f32(to_slot.astype(jnp.bfloat16), patches, (1,), (0,)).astype(jnp.bfloat16)
    inbox = lax.all_to_all(
        outbox.reshape(groups, slot_size, part_width), "dp", split_axis=0, concat_axis=0, tiled=True
    ).reshape(slots, part_width)

    outbox, late_patches = lax.optimization_barrier((outbox, patches))
    wide = late_patches.astype(jnp.float32)
    part_mean = jnp.mean(wide, -1)
    part_dev = jnp.sum(jnp.square(wide - part_mean[:, None]), -1)
    seen = exchange_small(jnp.stack([part_mean, part_dev]), "mp")
    row_mean = sum(entry[0] for entry in seen) / parts
    row_dev = sum(entry[1] + part_width * jnp.square(entry[0] - row_mean) for entry in seen)
    row_rstd = lax.rsqrt(row_dev / full_width + 1e-06)
    notes = jnp.stack([dest_row.astype(jnp.float32) + 1.0, row_mean, row_rstd])
    outnotes = jnp.sum(jnp.where(to_slot[None], notes[:, None, :], 0.0), -1)
    outnotes = outnotes.reshape(3, groups, slot_size)
    came = []
    for bit in range(groups):
        mine = lax.dynamic_index_in_dim(outnotes, my_group ^ bit, 1, keepdims=False)
        came.append(mine if bit == 0 else flip(mine, "dp", bit))
    sender = jnp.arange(groups, dtype=jnp.int32)[None, :, None]
    innotes = sum(
        jnp.where(sender == (my_group ^ bit), entry[:, None, :], 0.0)
        for bit, entry in enumerate(came)
    ).reshape(3, slots)
    arrived_at = innotes[0].astype(jnp.int32) - 1
    at_row = arrived_at[:, None] == position[None, :]
    mean = jnp.sum(jnp.where(at_row, innotes[1][:, None], 0.0), 0, keepdims=True)
    rstd = jnp.sum(jnp.where(at_row, innotes[2][:, None], 0.0), 0, keepdims=True)
    packed = dot_f32(inbox, at_row.astype(jnp.bfloat16), (0,), (0,)).astype(jnp.bfloat16)
    gain_column = ln_gain[:, None]
    my_gain = lax.dynamic_slice_in_dim(gain_column, my_index * part_width, part_width, 0)
    unit_rows = (packed.astype(jnp.float32) - mean) * rstd
    normed_part = (unit_rows * my_gain).astype(jnp.bfloat16)

    projected = add_block(None, normed_part, w_t, my_index)
    blocks, (whole_cot, projected) = line_blocks(normed_part, "mp", (whole_cot, projected))
    d_heads = project(whole_cot, w_out_t, jnp.bfloat16)
    normed = jnp.zeros((parts, part_width, group_rows), jnp.bfloat16)
    for order, (at, there, block) in enumerate(blocks):
        if order == len(blocks) - 1:
            block, cot_cols, d_heads, projected = lax.optimization_barrier(
                (block, cot_cols, d_heads, projected)
            )
        if order > 0:
            projected = add_block(projected, block, w_t, at)
        if order == 1:
            projected, late_cot = lax.optimization_barrier((projected, whole_cot))
            cot_cols = columns_to_owner(late_cot, "dp")
        if there is not None:
            at, block = jnp.where(there, at, my_index), jnp.where(there, block, normed_part)
        normed = lax.dynamic_update_slice(normed, block[None], (at, 0, 0))
    normed_cols = columns_to_owner(normed, "dp")

    heads_out = attention(forward_kernel, projected, segment, qk_gain, (), 1)
    attn_part = expand(heads_out, w_out_t, parts, 1)
    attn_part, d_heads = lax.optimization_barrier((attn_part, d_heads))
    attn = lax.psum_scatter(attn_part, "mp", scatter_dimension=0, tiled=False)
    output = (packed.astype(jnp.float32) + attn.astype(jnp.float32)).astype(jnp.bfloat16).T

    d_all = attention(backward_kernel, projected, segment, qk_gain, (d_heads,), 4)
    late_all, normed_cols = lax.optimization_barrier((d_all, normed_cols))
    d_part, sums = expand(late_all, w_t, parts, 2, gain_column, normed)
    d_normed = lax.psum_scatter(d_part, "mp", scatter_dimension=0, tiled=False)
    sums = sum(exchange_small(sums, "mp")) / full_width
    scale_grad = 1.0 / math.sqrt(group_rows * groups)
    columns = (normed_cols, cot_cols)
    near, far_key, far, spread = gather_xor(d_all, "dp")
    keys = sorted(near)
    sums_near = weight_grads(*columns, [near[key] for key in keys], keys, None, None)
    far, sums_near = lax.optimization_barrier((far, sums_near))
    far = spread({far_key: far})
    keys = sorted(far)
    sums_near = weight_grads(*columns, [far[key] for key in keys], keys, sums_near, scale_grad)
    d_normed, sums_near = lax.optimization_barrier((d_normed, sums_near))
    qkv_grad, out_grad = sums_near

    d_unit = d_normed.astype(jnp.float32) * my_gain
    d_input = rstd * (d_unit - sums[0:1] - unit_rows * sums[1:2])
    input_grad = (cotangent.astype(jnp.float32) + d_input.T).astype(jnp.bfloat16)
    return (output, input_grad, qkv_grad.transpose(1, 0, 2), out_grad)


def solution(mesh):
    placed = (
        P("dp", "mp"),
        P("dp"),
        P("dp"),
        P("dp"),
        P(),
        P(None, None, "mp"),
        P(),
        P(None, "mp"),
        P("dp", "mp"),
    )
    return jax.shard_map(
        shards,
        mesh=mesh,
        in_specs=placed,
        out_specs=(P("dp", "mp"), P("dp", "mp"), P("dp", None, "mp"), P("dp", "mp")),
        check_vma=False,
    )
```

```python
import functools
import math

import jax
import jax.numpy as jnp
from jax import lax
from jax.experimental import pallas as pl
from jax.experimental.pallas import tpu as pltpu
from jax.sharding import PartitionSpec as P

DH = 128
VMEM_BYTES = 48 * 1024 * 1024


def dot_f32(left, right, left_dims, right_dims):
    return lax.dot_general(
        left, right, ((left_dims, right_dims), ((), ())), preferred_element_type=jnp.float32
    )


def params():
    return pltpu.CompilerParams(vmem_limit_bytes=VMEM_BYTES)


def turn_kernel(x_ref, out_ref):
    out_ref[...] = x_ref[...].T


def turn(x):
    rows, part = x.shape
    return pl.pallas_call(
        turn_kernel,
        out_shape=jax.ShapeDtypeStruct((part, rows), x.dtype),
        compiler_params=params(),
        cost_estimate=pl.CostEstimate(flops=0, bytes_accessed=4 * rows * part, transcendentals=0),
    )(x)


def add_block_kernel(first, at_ref, x_ref, w_ref, *refs):
    out_ref, block = refs[-2:]

    @pl.when(pl.program_id(0) == 0)
    def _():
        block[...] = x_ref[...].T

    term = jnp.dot(block[...], w_ref[0], preferred_element_type=jnp.float32)
    out_ref[...] = term if first else refs[0][...] + term


def add_block(total, x, w, at):
    part, rows = x.shape
    kinds, _, width = w.shape
    sums = pl.BlockSpec((rows, width), lambda t, at_ref: (0, t))
    before = [] if total is None else [total]
    return pl.pallas_call(
        functools.partial(add_block_kernel, total is None),
        grid_spec=pltpu.PrefetchScalarGridSpec(
            num_scalar_prefetch=1,
            grid=(kinds,),
            in_specs=[
                pl.BlockSpec((part, rows), lambda t, at_ref: (0, 0)),
                pl.BlockSpec((1, part, width), lambda t, at_ref: (t, at_ref[0], 0)),
            ]
            + [sums] * len(before),
            out_specs=sums,
            scratch_shapes=[pltpu.VMEM((rows, part), jnp.bfloat16)],
        ),
        out_shape=jax.ShapeDtypeStruct((rows, kinds * width), jnp.float32),
        input_output_aliases={} if total is None else {3: 0},
        compiler_params=params(),
        cost_estimate=pl.CostEstimate(
            flops=2 * rows * part * kinds * width,
            bytes_accessed=2 * kinds * part * width + 8 * rows * kinds * width,
            transcendentals=0,
        ),
    )(at.reshape(1).astype(jnp.int32), x, w, *before)


def project_kernel(steps, width, x_ref, w_ref, out_ref, total, block):
    at, t = pl.program_id(0), pl.program_id(1)
    columns = pl.ds(pl.multiple_of(t * width, width), width)

    @pl.when(t == 0)
    def _():
        block[...] = x_ref[0].T

    term = jnp.dot(block[...], w_ref[0], preferred_element_type=jnp.float32)

    @pl.when(at == 0)
    def _():
        total[:, columns] = term

    @pl.when(at > 0)
    def _():
        total[:, columns] += term

    @pl.when(at == steps - 1)
    def _():
        out_ref[:, columns] = total[:, columns].astype(out_ref.dtype)


def project(x, w, dtype):
    steps, part, rows = x.shape
    kinds, depth, width = w.shape
    return pl.pallas_call(
        functools.partial(project_kernel, steps, width),
        grid=(steps, kinds),
        in_specs=[
            pl.BlockSpec((1, part, rows), lambda at, t: (at, 0, 0)),
            pl.BlockSpec((1, part, width), lambda at, t: (t, at, 0)),
        ],
        out_specs=pl.BlockSpec((rows, kinds * width), lambda at, t: (0, 0)),
        out_shape=jax.ShapeDtypeStruct((rows, kinds * width), dtype),
        scratch_shapes=[
            pltpu.VMEM((rows, kinds * width), jnp.float32),
            pltpu.VMEM((rows, part), jnp.bfloat16),
        ],
        compiler_params=params(),
        cost_estimate=pl.CostEstimate(
            flops=2 * rows * depth * kinds * width,
            bytes_accessed=2 * kinds * depth * width + 2 * rows * depth,
            transcendentals=0,
        ),
    )(x, w)


def expand_kernel(kinds, width, x_ref, w_ref, *refs):
    total = None
    for t in range(kinds):
        term = dot_f32(w_ref[t], x_ref[:, t * width : (t + 1) * width], (1,), (1,))
        total = term if total is None else total + term
    if len(refs) == 1:
        (out_ref,) = refs
    else:
        gain_ref, normed_ref, out_ref, sums_ref = refs

        @pl.when((pl.program_id(0) == 0) & (pl.program_id(1) == 0))
        def _():
            sums_ref[...] = jnp.zeros_like(sums_ref)

        sums_ref[0:1, :] += jnp.sum(total * gain_ref[...], 0, keepdims=True)
        sums_ref[1:2, :] += jnp.sum(total * normed_ref[0].astype(jnp.float32), 0, keepdims=True)
    out_ref[0] = total.astype(jnp.bfloat16)


def expand(x, w, parts, cuts, gain=None, normed=None):
    rows = x.shape[0]
    kinds, depth, width = w.shape
    part = depth // parts
    piece = part // cuts
    turned = pl.BlockSpec((1, piece, rows), lambda at, cut: (at, cut, 0))
    turned_shape = jax.ShapeDtypeStruct((parts, part, rows), jnp.bfloat16)
    more = [] if gain is None else [gain, normed]
    return pl.pallas_call(
        functools.partial(expand_kernel, kinds, width),
        grid=(parts, cuts),
        in_specs=[
            pl.BlockSpec((rows, kinds * width), lambda at, cut: (0, 0)),
            pl.BlockSpec((kinds, piece, width), lambda at, cut: (0, at * cuts + cut, 0)),
        ]
        + ([pl.BlockSpec((piece, 1), lambda at, cut: (at * cuts + cut, 0)), turned] if more else []),
        out_specs=[turned, pl.BlockSpec((2, rows), lambda at, cut: (0, 0))] if more else turned,
        out_shape=[turned_shape, jax.ShapeDtypeStruct((2, rows), jnp.float32)]
        if more
        else turned_shape,
        compiler_params=params(),
        cost_estimate=pl.CostEstimate(
            flops=2 * rows * depth * kinds * width,
            bytes_accessed=2 * kinds * depth * width + 2 * rows * depth,
            transcendentals=0,
        ),
    )(x, w, *more)


def unit_heads(raw):
    center = raw - jnp.mean(raw, -1, keepdims=True)
    rstd = lax.rsqrt(jnp.mean(center * center, -1, keepdims=True) + 1e-06)
    return center * rstd, rstd


def head_forward(proj_ref, same, gain_ref, heads, head):
    width = heads * DH

    def load(kind):
        start = kind * width + head * DH
        return proj_ref[:, start : start + DH]

    q_unit, q_rstd = unit_heads(load(0))
    k_unit, k_rstd = unit_heads(load(1))
    values = load(2).astype(jnp.bfloat16)
    queries = (q_unit * gain_ref[0:1, :]).astype(jnp.bfloat16)
    keys = (k_unit * gain_ref[1:2, :]).astype(jnp.bfloat16)
    scores = dot_f32(queries, keys, (1,), (1,)) * DH ** (-0.5)
    raised = jnp.where(same, jnp.exp(scores), 0.0)
    weights = raised / jnp.sum(raised, -1, keepdims=True)
    return q_unit, q_rstd, k_unit, k_rstd, values, queries, keys, weights


def forward_kernel(heads, proj_ref, row_ref, col_ref, gain_ref, out_ref):
    same = row_ref[...] == col_ref[...]
    for head in range(heads):
        values, _, _, weights = head_forward(proj_ref, same, gain_ref, heads, head)[4:]
        mixed = dot_f32(weights.astype(jnp.bfloat16), values, (1,), (0,))
        out_ref[:, head * DH : (head + 1) * DH] = mixed.astype(jnp.bfloat16)


def unit_backward(grad, unit, rstd, gain):
    scaled = grad.astype(jnp.bfloat16).astype(jnp.float32) * gain
    return rstd * (
        scaled
        - jnp.mean(scaled, -1, keepdims=True)
        - unit * jnp.mean(scaled * unit, -1, keepdims=True)
    )


def backward_kernel(heads, proj_ref, row_ref, col_ref, gain_ref, d_ref, out_ref):
    same = row_ref[...] == col_ref[...]
    width = heads * DH
    for head in range(heads):
        q_unit, q_rstd, k_unit, k_rstd, values, queries, keys, weights = head_forward(
            proj_ref, same, gain_ref, heads, head
        )
        at = head * DH
        weights_bf = weights.astype(jnp.bfloat16)
        d_out = d_ref[:, at : at + DH]
        mixed = dot_f32(weights_bf, values, (1,), (0,))
        out_ref[:, 3 * width + at : 3 * width + at + DH] = mixed.astype(jnp.bfloat16)
        d_values = dot_f32(weights_bf, d_out, (0,), (0,))
        out_ref[:, 2 * width + at : 2 * width + at + DH] = d_values.astype(jnp.bfloat16)
        d_weights = dot_f32(d_out, values, (1,), (1,)).astype(jnp.bfloat16).astype(jnp.float32)
        inner = jnp.sum(d_weights * weights, -1, keepdims=True)
        d_scores = (weights * (d_weights - inner) * DH ** (-0.5)).astype(jnp.bfloat16)
        d_queries = unit_backward(
            dot_f32(d_scores, keys, (1,), (0,)), q_unit, q_rstd, gain_ref[0:1, :]
        )
        d_keys = unit_backward(
            dot_f32(d_scores, queries, (0,), (0,)), k_unit, k_rstd, gain_ref[1:2, :]
        )
        out_ref[:, at : at + DH] = d_queries.astype(jnp.bfloat16)
        out_ref[:, width + at : width + at + DH] = d_keys.astype(jnp.bfloat16)


def attention(kernel, projected, segment, qk_gain, extra, kinds):
    rows, wide = projected.shape
    heads = wide // (3 * DH)
    return pl.pallas_call(
        functools.partial(kernel, heads),
        out_shape=jax.ShapeDtypeStruct((rows, kinds * heads * DH), jnp.bfloat16),
        compiler_params=params(),
        cost_estimate=pl.CostEstimate(
            flops=heads * rows * rows * DH * 16,
            bytes_accessed=rows * wide * 8,
            transcendentals=heads * rows * rows,
        ),
    )(projected, segment.reshape(rows, 1), segment.reshape(1, rows), qk_gain, *extra)


def weight_kernel(keys, scale, normed_ref, cot_ref, *refs):
    b_refs, refs = refs[: len(keys)], refs[len(keys) :]
    me, t = lax.axis_index("dp"), pl.program_id(0)

    def product(load, total):
        for order, key in enumerate(keys):
            term = jnp.dot(load(me ^ key), b_refs[order][...], preferred_element_type=jnp.float32)
            if scale is None and order == 0:
                total[...] = term
            else:
                total[...] += term

    def normed(at):
        return normed_ref[at]

    def cot(at):
        return cot_ref[at]

    if scale is None:
        total = refs[0].at[0]
    else:
        before_ref, qkv_ref, out_ref, total = refs
        total[...] = before_ref[0]

    @pl.when(t < 3)
    def _():
        product(normed, total)
        if scale is not None:
            qkv_ref[0] = (total[...] * scale).astype(jnp.bfloat16)

    @pl.when(t == 3)
    def _():
        product(cot, total)
        if scale is not None:
            out_ref[...] = (total[...] * scale).astype(jnp.bfloat16)


def weight_grads(normed_cols, cot_cols, gathered, keys, before, scale):
    count, depth, rows = normed_cols.shape
    width = gathered[0].shape[1] // 4
    whole = pl.BlockSpec((count, depth, rows), lambda t: (0, 0, 0))
    sums = pl.BlockSpec((1, depth, width), lambda t: (t, 0, 0))
    sums_shape = jax.ShapeDtypeStruct((4, depth, width), jnp.float32)
    return pl.pallas_call(
        functools.partial(weight_kernel, keys, scale),
        grid=(4,),
        in_specs=[whole, whole]
        + [pl.BlockSpec((rows, width), lambda t: (0, t))] * len(keys)
        + ([] if before is None else [sums]),
        out_specs=sums
        if before is None
        else [
            pl.BlockSpec((1, depth, width), lambda t: (jnp.minimum(t, 2), 0, 0)),
            pl.BlockSpec((depth, width), lambda t: (0, 0)),
        ],
        out_shape=sums_shape
        if before is None
        else [
            jax.ShapeDtypeStruct((3, depth, width), jnp.bfloat16),
            jax.ShapeDtypeStruct((depth, width), jnp.bfloat16),
        ],
        scratch_shapes=[] if before is None else [pltpu.VMEM((depth, width), jnp.float32)],
        compiler_params=params(),
        cost_estimate=pl.CostEstimate(
            flops=8 * len(keys) * depth * rows * width,
            bytes_accessed=4 * count * depth * rows + 8 * len(keys) * rows * width,
            transcendentals=0,
        ),
    )(normed_cols, cot_cols, *gathered, *([] if before is None else [before]))


def flip(values, axis, bit):
    count = lax.axis_size(axis)
    return lax.ppermute(values, axis, [(at, at ^ bit) for at in range(count)])


def exchange_small(values, axis):
    return [values] + [flip(values, axis, bit) for bit in range(1, lax.axis_size(axis))]


def gather_xor(values, axis):
    count = lax.axis_size(axis)
    high, low = count // 2, count // 4

    def spread(held):
        bit = low // 2
        while bit >= 1:
            for key in sorted(held):
                held[key | bit] = flip(held[key], axis, bit)
            bit //= 2
        return held

    over_high, over_low = flip(values, axis, high), flip(values, axis, low)
    own = spread({0: values})
    keys = sorted(own)
    spread_own, over_high, over_low = lax.optimization_barrier(
        ([own[key] for key in keys], over_high, over_low)
    )
    even = lax.axis_index(axis) % 2 == 0
    onward = jnp.where(even, over_low, over_high)
    pairs = [(at, at ^ (high if at % 2 == 0 else low)) for at in range(count)]
    far = lax.ppermute(onward, axis, pairs)
    near = dict(zip(keys, spread_own))
    near.update(spread({high: over_high}))
    near.update(spread({low: over_low}))
    return near, high | low, far, spread


def line_blocks(values, axis, beside):
    count, me = lax.axis_size(axis), lax.axis_index(axis)
    blocks = [(me, None, values)]
    right = left = values
    for step in range(1, count):
        right = lax.ppermute(right, axis, [(at, at + 1) for at in range(step - 1, count - 1)])
        left = lax.ppermute(left, axis, [(at, at - 1) for at in range(1, count - step + 1)])
        if step == 1:
            right, left, beside = lax.optimization_barrier((right, left, beside))
        if step == 2:
            early = [block for _, _, block in blocks[1:]]
            right, left, early = lax.optimization_barrier((right, left, early))
            blocks[1:] = [entry[:2] + (block,) for entry, block in zip(blocks[1:], early)]
        over, under = me >= step, me + step < count
        if 2 * step >= count:
            at = jnp.where(over, me - step, jnp.minimum(me + step, count - 1))
            blocks.append((at, over | under, right + left))
        else:
            blocks.append((jnp.maximum(me - step, 0), over, right))
            blocks.append((jnp.minimum(me + step, count - 1), under, left))
    return blocks, beside


def columns_to_owner(turned, axis):
    count = lax.axis_size(axis)
    parts, part, rows = turned.shape
    cut = turned.reshape(count, parts * part // count, rows)
    return lax.all_to_all(cut, axis, 0, 0, tiled=True)


def shards(patches, dest_group, dest_row, segment, ln_gain, w_qkv, qk_gain, w_out, cotangent):
    group_rows, part_width = patches.shape
    groups = lax.axis_size("dp")
    parts = lax.axis_size("mp")
    slot_size = 2 * group_rows // groups
    slots = groups * slot_size
    full_width, local_width = w_out.shape
    my_group, my_index = lax.axis_index("dp"), lax.axis_index("mp")
    w_t = jnp.transpose(w_qkv, (1, 0, 2))
    w_out_t = w_out[None]

    whole_cot = lax.all_gather(turn(cotangent), "mp", axis=0, tiled=False)

    position = jnp.arange(group_rows, dtype=jnp.int32)
    earlier = (dest_group[:, None] == dest_group[None, :]) & (position[None, :] < position[:, None])
    rank_within = jnp.sum(earlier.astype(jnp.int32), 1)
    place = dest_group * slot_size + rank_within
    to_slot = jnp.arange(slots, dtype=jnp.int32)[:, None] == place[None, :]
    outbox = dot_f32(to_slot.astype(jnp.bfloat16), patches, (1,), (0,)).astype(jnp.bfloat16)
    inbox = lax.all_to_all(
        outbox.reshape(groups, slot_size, part_width), "dp", split_axis=0, concat_axis=0, tiled=True
    ).reshape(slots, part_width)

    outbox, late_patches = lax.optimization_barrier((outbox, patches))
    wide = late_patches.astype(jnp.float32)
    part_mean = jnp.mean(wide, -1)
    part_dev = jnp.sum(jnp.square(wide - part_mean[:, None]), -1)
    seen = exchange_small(jnp.stack([part_mean, part_dev]), "mp")
    row_mean = sum(entry[0] for entry in seen) / parts
    row_dev = sum(entry[1] + part_width * jnp.square(entry[0] - row_mean) for entry in seen)
    row_rstd = lax.rsqrt(row_dev / full_width + 1e-06)
    notes = jnp.stack([dest_row.astype(jnp.float32) + 1.0, row_mean, row_rstd])
    outnotes = jnp.sum(jnp.where(to_slot[None], notes[:, None, :], 0.0), -1)
    outnotes = outnotes.reshape(3, groups, slot_size)
    came = []
    for bit in range(groups):
        mine = lax.dynamic_index_in_dim(outnotes, my_group ^ bit, 1, keepdims=False)
        came.append(mine if bit == 0 else flip(mine, "dp", bit))
    sender = jnp.arange(groups, dtype=jnp.int32)[None, :, None]
    innotes = sum(
        jnp.where(sender == (my_group ^ bit), entry[:, None, :], 0.0)
        for bit, entry in enumerate(came)
    ).reshape(3, slots)
    arrived_at = innotes[0].astype(jnp.int32) - 1
    at_row = arrived_at[:, None] == position[None, :]
    mean = jnp.sum(jnp.where(at_row, innotes[1][:, None], 0.0), 0, keepdims=True)
    rstd = jnp.sum(jnp.where(at_row, innotes[2][:, None], 0.0), 0, keepdims=True)
    packed = dot_f32(inbox, at_row.astype(jnp.bfloat16), (0,), (0,)).astype(jnp.bfloat16)
    gain_column = ln_gain[:, None]
    my_gain = lax.dynamic_slice_in_dim(gain_column, my_index * part_width, part_width, 0)
    unit_rows = (packed.astype(jnp.float32) - mean) * rstd
    normed_part = (unit_rows * my_gain).astype(jnp.bfloat16)

    projected = add_block(None, normed_part, w_t, my_index)
    blocks, (whole_cot, projected) = line_blocks(normed_part, "mp", (whole_cot, projected))
    d_heads = project(whole_cot, w_out_t, jnp.bfloat16)
    cot_cols = columns_to_owner(whole_cot, "dp")
    normed = jnp.zeros((parts, part_width, group_rows), jnp.bfloat16)
    for order, (at, there, block) in enumerate(blocks):
        if order == len(blocks) - 1:
            block, cot_cols, d_heads, projected = lax.optimization_barrier(
                (block, cot_cols, d_heads, projected)
            )
        if order > 0:
            projected = add_block(projected, block, w_t, at)
        if there is not None:
            at, block = jnp.where(there, at, my_index), jnp.where(there, block, normed_part)
        normed = lax.dynamic_update_slice(normed, block[None], (at, 0, 0))
    normed_cols = columns_to_owner(normed, "dp")

    heads_out = attention(forward_kernel, projected, segment, qk_gain, (), 1)
    attn_part = expand(heads_out, w_out_t, parts, 1)
    attn_part, d_heads = lax.optimization_barrier((attn_part, d_heads))
    attn = lax.psum_scatter(attn_part, "mp", scatter_dimension=0, tiled=False)
    output = (packed.astype(jnp.float32) + attn.astype(jnp.float32)).astype(jnp.bfloat16).T

    d_all = attention(backward_kernel, projected, segment, qk_gain, (d_heads,), 4)
    late_all, normed_cols = lax.optimization_barrier((d_all, normed_cols))
    d_part, sums = expand(late_all, w_t, parts, 2, gain_column, normed)
    d_normed = lax.psum_scatter(d_part, "mp", scatter_dimension=0, tiled=False)
    sums = sum(exchange_small(sums, "mp")) / full_width
    scale_grad = 1.0 / math.sqrt(group_rows * groups)
    columns = (normed_cols, cot_cols)
    near, far_key, far, spread = gather_xor(d_all, "dp")
    keys = sorted(near)
    sums_near = weight_grads(*columns, [near[key] for key in keys], keys, None, None)
    far, sums_near = lax.optimization_barrier((far, sums_near))
    far = spread({far_key: far})
    keys = sorted(far)
    sums_near = weight_grads(*columns, [far[key] for key in keys], keys, sums_near, scale_grad)
    d_normed, sums_near = lax.optimization_barrier((d_normed, sums_near))
    qkv_grad, out_grad = sums_near

    d_unit = d_normed.astype(jnp.float32) * my_gain
    d_input = rstd * (d_unit - sums[0:1] - unit_rows * sums[1:2])
    input_grad = (cotangent.astype(jnp.float32) + d_input.T).astype(jnp.bfloat16)
    return (output, input_grad, qkv_grad.transpose(1, 0, 2), out_grad)


def solution(mesh):
    placed = (
        P("dp", "mp"),
        P("dp"),
        P("dp"),
        P("dp"),
        P(),
        P(None, None, "mp"),
        P(),
        P(None, "mp"),
        P("dp", "mp"),
    )
    return jax.shard_map(
        shards,
        mesh=mesh,
        in_specs=placed,
        out_specs=(P("dp", "mp"), P("dp", "mp"), P("dp", None, "mp"), P("dp", "mp")),
        check_vma=False,
    )
```
